512 devices in a mesh: lon: 32 (over y, x_hi, core), lat: 16 (over x_lo, z).
Axes of the slice: x: 4 (x_hi: 2, x_lo: 2; x = x_hi * 2 + x_lo), y: 8, z: 8, core: 2. Of those that a mesh axis runs over, the one named last changes fastest.
Arguments:
- state: float32 [5, 256, 4096], P(None, 'lat', 'lon'), may hold values from -6 to 6
- prior_in: bfloat16 [9, 64, 5], replicated, may hold values from -0.875 to 0.875
- prior_bias: float32 [64], replicated, may hold values from -3 to 3
- prior_out: bfloat16 [9, 5, 64], replicated, may hold values from -0.25 to 0.25
- lstm_weight: bfloat16 [9, 256, 69], replicated, may hold values from -0.25 to 0.25
- lstm_bias: float32 [256], replicated, may hold values from -3 to 3
- lstm_out: bfloat16 [5, 64], replicated, may hold values from -0.75 to 0.75
- obs_value: float32 [262144], P(('lon', 'lat')), may hold values from -6 to 6
- obs_weight: float32 [4, 262144], P(None, ('lon', 'lat')), may hold values from 0.05 to 0.5
- obs_tile: int32 [262144, 1], P(('lon', 'lat')), may hold values from 0 to 15; in each aligned block of 512 rows (0 to 511, 512 to 1023, ...) at most 128 rows name the same one
- obs_time: int32 [262144], P(('lon', 'lat')), may hold values from 0 to 4
- obs_row: int32 [262144], P(('lon', 'lat')), may hold values from 0 to 14
- obs_col: int32 [262144], P(('lon', 'lat')), may hold values from 0 to 126
Outputs:
- estimate: float32 [5, 256, 4096], P(None, 'lat', 'lon')
- cell_state: float32 [64, 256, 4096], P(None, 'lat', 'lon')
The draws below stay inside these ranges and needn't reach their ends.
Inputs may be any that keep to these rules, and one draw needn't show every extreme that they name: `obs_tile`: each row falls in a tile of its own owner's longitude column; at most 128 rows of one track owner fall in the same tile.
All inputs are finite; a program needn't handle non-finite values.
Results may differ from the reference program's by a relative error of at most 0.0035.
Values may be sent and summed in bfloat16 or wider, within the bound.
No kernel may reach another device: no remote copies, remote signals or barrier semaphores. Data moves between devices by JAX's collectives and lax.ppermute only.
A program may use at most 64 MiB of HBM per device.

```python
import math
import jax
import jax.numpy as jnp
import numpy as np

TIMES = 5
PRIOR = 64
HIDDEN_SIZE = 64
ITERS = 2
TX = 128
TY = 16
ROWS_DEV = 512
CAP = 128
NX = 4096
NY = 256
OBS_ROWS = 262144
N_LAT = 16


def set_ends(entries, rng, smallest, largest):
    extent = entries.shape
    index_at = [jax.random.randint(jax.random.fold_in(rng, axis), (), 0, extent[axis]) for axis in range(len(extent))]
    entries = entries.at[tuple(index_at)].set(smallest)
    longest = extent.index(max(extent))
    index_at[longest] = (index_at[longest] + 1) % extent[longest]
    return entries.at[tuple(index_at)].set(largest)


def level_of(own_key, shape, cuts, least, top_value):
    factor_of, own = 1.0, jax.random.fold_in(own_key, 6)
    for position, shards_of in cuts:
        draws = jnp.exp(jax.random.uniform(jax.random.fold_in(own, position), (shards_of,), jnp.float32, least / len(cuts), top_value / len(cuts)))
        factor_of = factor_of * jnp.repeat(draws, shape[position] // shards_of).reshape([-1 if axis == position else 1 for axis in range(len(shape))])
    return factor_of


def routed_block(stream_key, own, number, rows, number_of, top, bound, skew):
    order = jax.random.permutation(stream_key, number_of)
    crowded, ordinary = shares(number_of, rows * top, bound, skew, True), shares(number_of, rows * top, bound, skew, False)
    places = jnp.arange(number_of)

    def named(tallies, turn):
        used = int((tallies > 0).sum())
        fixed = max(1, used // 4)
        moved = fixed + (places - fixed + turn * (used - fixed)) % max(1, number_of - fixed)
        return jnp.zeros((number_of,), jnp.int32).at[order[jnp.where(places < fixed, places, moved)]].set(jnp.asarray(tallies, jnp.int32))

    tallies = jnp.where(number % 4 == 0, named(crowded, number // 4), named(ordinary, number - number // 4 - 1))
    mixed = jax.random.permutation(jax.random.fold_in(own, 3), number_of)
    giver, sink = mixed[0:number_of // 2 * 2:2], mixed[1:number_of // 2 * 2:2]
    margin = jnp.minimum(tallies[giver] - 1, bound - tallies[sink]) // 2
    margin = jnp.where((giver == order[0]) | (sink == order[0]) | (tallies[sink] == 0), 0, jnp.maximum(margin, 0))
    moved = jax.random.randint(jax.random.fold_in(own, 4), (number_of // 2,), 0, 1 << 20) % (margin + 1)
    tallies = tallies.at[giver].add(-moved).at[sink].add(moved)
    members = jnp.searchsorted(jnp.cumsum(tallies), jnp.arange(rows * top), side="right").astype(jnp.int32)
    table = members.reshape(top, rows).T
    table = table[jax.random.permutation(jax.random.fold_in(own, 1), rows)]
    turn = jax.random.randint(jax.random.fold_in(own, 2), (rows, 1), 0, top)
    return jnp.take_along_axis(table, (jnp.arange(top)[None, :] + turn) % top, axis=1)


def shares(count, total, reach, skew, full):
    loads = [(1 << 20) // math.isqrt(standing ** skew) + 1 for standing in range(1, count + 1)]
    largest = reach if full else min(reach, max(-(-total // count), total * loads[0] // sum(loads)))
    least = 1 if total - largest >= count - 1 else 0
    given, surplus = [largest] + [least] * (count - 1), total - largest - least * (count - 1)
    while surplus > 0:
        candidates = [i for i in range(1, count) if given[i] < largest] or [i for i in range(1, count) if given[i] < reach]
        mass, remaining = sum([loads[i] for i in candidates]), surplus
        for i in candidates:
            extra = min(reach - given[i], max(1, remaining * loads[i] // mass), surplus)
            given[i] = given[i] + extra
            surplus = surplus - extra
    return np.array(given)


def bell_draw(own_key, shape, deviation, bound, cuts=(), kind=jnp.bfloat16):
    factor_of = level_of(own_key, shape, cuts, -0.22, 0.18) if cuts else 1.0
    array = jax.random.normal(own_key, shape, jnp.float32) * deviation * factor_of
    return jnp.minimum(jnp.maximum(array, -bound), bound).astype(kind)


def setup_inputs(seed: int = 0) -> dict:
    seeds = jax.random.split(jax.random.key(seed), 14)
    state = bell_draw(seeds[0], (TIMES, NY, NX), 1.0, 6.0, ((1, 16), (2, 32)), jnp.float32)
    prior_in = bell_draw(seeds[1], (9, PRIOR, TIMES), (9 * TIMES) ** -0.5, 0.875)
    prior_bias = bell_draw(seeds[2], (PRIOR,), 0.5, 3.0, (), jnp.float32)
    prior_out = bell_draw(seeds[3], (9, TIMES, PRIOR), (9 * PRIOR) ** -0.5, 0.25)
    lstm_weight = bell_draw(seeds[4], (9, 4 * HIDDEN_SIZE, TIMES + HIDDEN_SIZE), (9 * (TIMES + HIDDEN_SIZE)) ** -0.5, 0.25)
    lstm_bias = bell_draw(seeds[5], (4 * HIDDEN_SIZE,), 0.5, 3.0, (), jnp.float32)
    lstm_out = bell_draw(seeds[6], (TIMES, HIDDEN_SIZE), HIDDEN_SIZE ** -0.5, 0.75)
    obs_value = bell_draw(seeds[7], (OBS_ROWS,), 1.0, 6.0, ((0, 512),), jnp.float32)
    obs_weight = jnp.clip(0.05 + 0.45 * jax.random.uniform(seeds[8], (4, OBS_ROWS), jnp.float32) ** level_of(seeds[8], (4, OBS_ROWS), ((1, 512),), -0.2, 0.2), 0.05, 0.5)
    obs_tile_keys = jax.random.split(jax.random.fold_in(seeds[9], 1), OBS_ROWS // ROWS_DEV)
    obs_tile_turns = jax.random.permutation(jax.random.fold_in(seeds[9], 3), OBS_ROWS // ROWS_DEV)
    obs_tile = jax.vmap(lambda own, number: routed_block(jax.random.fold_in(seeds[9], 2), own, number, ROWS_DEV, N_LAT, 1, CAP, 2))(obs_tile_keys, obs_tile_turns).reshape((OBS_ROWS, 1))
    obs_time = set_ends(jax.random.randint(seeds[10], (OBS_ROWS,), 0, TIMES), jax.random.fold_in(seeds[10], 1), 0, TIMES - 1).astype(jnp.int32)
    obs_row = set_ends(jax.random.randint(seeds[11], (OBS_ROWS,), 0, TY - 1), jax.random.fold_in(seeds[11], 1), 0, (TY - 1) - 1).astype(jnp.int32)
    obs_col = set_ends(jax.random.randint(seeds[12], (OBS_ROWS,), 0, TX - 1), jax.random.fold_in(seeds[12], 1), 0, (TX - 1) - 1).astype(jnp.int32)
    return dict(state=state, prior_in=prior_in, prior_bias=prior_bias, prior_out=prior_out, lstm_weight=lstm_weight, lstm_bias=lstm_bias, lstm_out=lstm_out, obs_value=obs_value, obs_weight=obs_weight, obs_tile=obs_tile, obs_time=obs_time, obs_row=obs_row, obs_col=obs_col)


block_rows = 32


def extend_grid(values, rim_width):
    wrapped = jnp.concatenate([values[..., -rim_width:], values, values[..., :rim_width]], axis=-1)
    return jnp.pad(wrapped, ((0, 0), (rim_width, rim_width), (0, 0)))


def stencil(weight, padded, rows_out, cols_out, finish):
    pieces = []
    for first_row in range(0, rows_out, block_rows):
        row_count = min(block_rows, rows_out - first_row)
        accumulated = None
        for offset in range(9):
            window = padded[:, first_row + offset // 3:first_row + offset // 3 + row_count, offset % 3:offset % 3 + cols_out]
            term = jnp.einsum('oc,cyx->oyx', weight[offset].astype(jnp.float32), window.astype(jnp.float32))
            accumulated = term if accumulated is None else accumulated + term
        pieces.append(finish(accumulated, first_row, row_count))
    return jax.tree.map(lambda *parts: jnp.concatenate(parts, axis=1), *pieces)


def reference(state, prior_in, prior_bias, prior_out, lstm_weight, lstm_bias, lstm_out, obs_value, obs_weight, obs_tile, obs_time, obs_row, obs_col):
    owner = jnp.arange(OBS_ROWS, dtype=jnp.int32) // ROWS_DEV
    grid_col = (owner // N_LAT) * TX + obs_col
    grid_row = obs_tile[:, 0] * TY + obs_row
    rows_at = jnp.stack([grid_row, grid_row, grid_row + 1, grid_row + 1])
    cols_at = jnp.stack([grid_col, grid_col + 1, grid_col, grid_col + 1])
    times_at = jnp.broadcast_to(obs_time, (4, OBS_ROWS))
    estimate = state
    cell_state = jnp.zeros((HIDDEN_SIZE, NY, NX), jnp.float32)
    hidden = jnp.zeros((HIDDEN_SIZE, NY, NX), jnp.bfloat16)

    def relu_block(accumulated, first_row, row_count):
        return jax.nn.relu(accumulated + prior_bias[:, None, None]).astype(jnp.bfloat16)

    def plain_block(accumulated, first_row, row_count):
        return accumulated

    for iteration in range(ITERS):
        coarse = estimate.astype(jnp.bfloat16)
        latent = stencil(prior_in, extend_grid(coarse, 1), NY, NX, relu_block)
        prior_term = stencil(prior_out, extend_grid(latent, 1), NY, NX, plain_block)
        innovation = jnp.sum(obs_weight * estimate[times_at, rows_at, cols_at], axis=0) - obs_value
        adjoint = jnp.zeros_like(estimate).at[times_at, rows_at, cols_at].add(obs_weight * innovation[None, :])
        gradient = estimate - prior_term + adjoint
        joined = jnp.concatenate([gradient.astype(jnp.bfloat16), hidden], axis=0)
        old_cell = cell_state

        def gate_block(accumulated, first_row, row_count):
            gate_sums = accumulated + lstm_bias[:, None, None]
            input_gate = jax.nn.sigmoid(gate_sums[:HIDDEN_SIZE])
            forget_gate = jax.nn.sigmoid(gate_sums[HIDDEN_SIZE:2 * HIDDEN_SIZE])
            output_gate = jax.nn.sigmoid(gate_sums[2 * HIDDEN_SIZE:3 * HIDDEN_SIZE])
            candidate = jnp.tanh(gate_sums[3 * HIDDEN_SIZE:])
            new_cell = forget_gate * old_cell[:, first_row:first_row + row_count] + input_gate * candidate
            new_hidden = (output_gate * jnp.tanh(new_cell)).astype(jnp.bfloat16)
            update = jnp.einsum('ch,hyx->cyx', lstm_out.astype(jnp.float32), new_hidden.astype(jnp.float32))
            return new_cell, new_hidden, update

        cell_state, hidden, update = stencil(lstm_weight, extend_grid(joined, 1), NY, NX, gate_block)
        estimate = estimate - update
    return estimate, cell_state
```

```python
import jax
import jax.numpy as jnp
from jax import lax
from jax.experimental import pallas as pl
from jax.experimental.pallas import tpu as pltpu
from jax.sharding import PartitionSpec as P

DAYS = 5
ROWS = 16
COLS = 128
LANES = 128
HID = 64
TRACK = 512
HALO = 8
BASES = 25
CHUNK = 2048
FIRST = 7
TILES = 60
F32 = jnp.float32
BF16 = jnp.bfloat16


def nt_dot(left, right):
    return lax.dot_general(left, right, (((1,), (1,)), ((), ())), preferred_element_type=F32)


def lane_roll(value, shift):
    return pltpu.roll(value, shift % value.shape[1], 1)


def day_rows(low_ref, mid_ref, high_ref, row):
    if row < 0:
        picked = low_ref[pl.ds(row + HALO, DAYS, stride=HALO), :]
    elif row < ROWS:
        picked = mid_ref[pl.ds(row, DAYS, stride=ROWS), :]
    else:
        picked = high_ref[pl.ds(row - ROWS, DAYS, stride=HALO), :]
    return jnp.concatenate([picked, jnp.zeros((8 - DAYS, LANES), F32)], axis=0)


def adjoint_terms(sums_ref, base, here, above):
    low = pl.ds(5 * base, 8)
    high = pl.ds(LANES + 5 * base, 8)
    here_right = lane_roll(here, -1)
    above_right = lane_roll(above, -1)
    s01 = sums_ref[1, low, :]
    s02 = sums_ref[2, low, :]
    s03 = sums_ref[3, low, :]
    s12 = sums_ref[2, high, :]
    s13 = sums_ref[3, high, :]
    s23 = sums_ref[6, low, :]
    g0 = sums_ref[0, low, :] * here + s01 * here_right + s02 * above + s03 * above_right - sums_ref[4, low, :]
    g1 = s01 * here + sums_ref[1, high, :] * here_right + s12 * above + s13 * above_right - sums_ref[4, high, :]
    g2 = s02 * here + s12 * here_right + sums_ref[5, low, :] * above + s23 * above_right - sums_ref[7, low, :]
    g3 = s03 * here + s13 * here_right + s23 * above + sums_ref[6, high, :] * above_right - sums_ref[7, high, :]
    return g0 + lane_roll(g1, 1), g2 + lane_roll(g3, 1)


def build_kernel(
    lat_ref, track_ref, mid_ref, low_ref, high_ref, sums_ref, adjoint_ref, east_ref, west_ref, rw_ref, cw_ref, ce_ref, edge_ref
):
    base_row = (lat_ref[0] * ROWS - 5).astype(F32)
    entry = lax.broadcasted_iota(jnp.int32, (LANES, TRACK), 0).astype(F32)
    sums_ref[...] = jnp.zeros_like(sums_ref)
    edge_ref[...] = jnp.zeros_like(edge_ref)

    def chunk_step(chunk, carry):
        for half in range(2):
            both = track_ref[pl.ds(pl.multiple_of(chunk * 32 + half * 16, 16), 16), :].astype(F32)
            for part in range(2):
                block = both[8 * part : 8 * part + 8]
                at = (2 * half + part) * TRACK
                time = block[5:6]
                offset = block[6:7] - base_row
                column = block[7:8]
                inside = (offset >= 0.0) & (offset < float(BASES))
                key = jnp.where(inside, offset * 5.0 + time, -1.0)
                row_hit = entry == key
                col_hit = entry == column
                for k in range(4):
                    rw_ref[128 * k : 128 * k + 128, at : at + TRACK] = jnp.where(
                        row_hit, block[1 + k : 2 + k], 0.0
                    ).astype(BF16)
                for k in range(5):
                    source = (1 + k) % 5
                    cw_ref[128 * k : 128 * k + 128, at : at + TRACK] = jnp.where(
                        col_hit, block[source : source + 1], 0.0
                    ).astype(BF16)
                ce_ref[:, at : at + TRACK] = jnp.concatenate(
                    [
                        jnp.where(column == float(COLS - 2), block, 0.0),
                        jnp.where(column == 0.0, block, 0.0),
                    ],
                    axis=0,
                ).astype(BF16)
        first = nt_dot(rw_ref[0:256, :], cw_ref[...])
        for k in range(5):
            sums_ref[k] += first[:, 128 * k : 128 * k + 128]
        second = nt_dot(rw_ref[256:512, :], cw_ref[256:640, :])
        for k in range(3):
            sums_ref[5 + k] += second[:, 128 * k : 128 * k + 128]
        edge_ref[...] += nt_dot(ce_ref[...], rw_ref[...])
        return carry

    lax.fori_loop(0, track_ref.shape[0] * TRACK // (8 * CHUNK), chunk_step, 0)

    lane_group = lax.broadcasted_iota(jnp.int32, (8, LANES), 1) // 8

    def pack(slot, row, east, west):
        return (
            jnp.where(lane_group == slot, lane_roll(row, 8 * slot + 8), east),
            jnp.where(lane_group == slot, lane_roll(row, 8 * slot), west),
        )

    zero = jnp.zeros((8, LANES), F32)
    for part in range(2):
        east, west = zero, zero
        for slot in range(16):
            row = part * 16 + slot - 6
            if row < ROWS + 6:
                east, west = pack(slot, day_rows(low_ref, mid_ref, high_ref, row), east, west)
        east_ref[8 * part : 8 * part + 8, :] = east
        west_ref[8 * part : 8 * part + 8, :] = west
    packed = [[zero, zero], [zero, zero]]
    here = day_rows(low_ref, mid_ref, high_ref, -5)
    carried = zero
    for base in range(BASES):
        above = day_rows(low_ref, mid_ref, high_ref, base - 4)
        now, later = adjoint_terms(sums_ref, base, here, above)
        if base > 0:
            total = carried + now
            adjoint_ref[base - 1] = total
            part, slot = divmod(base - 1, 16)
            packed[part] = list(pack(slot, total, *packed[part]))
        carried = later
        here = above
    for part in range(2):
        east_ref[16 + 8 * part : 24 + 8 * part, :] = packed[part][0]
        west_ref[16 + 8 * part : 24 + 8 * part, :] = packed[part][1]
    east_ref[32:40, :] = edge_ref[0:8, 128:256]
    east_ref[40:48, :] = edge_ref[0:8, 384:512]
    west_ref[32:40, :] = edge_ref[8:16, 0:128]
    west_ref[40:48, :] = edge_ref[8:16, 256:384]


def solve_kernel(
    lat_ref,
    mid_ref,
    low_ref,
    high_ref,
    sums_ref,
    adjoint_ref,
    fromw_ref,
    frome_ref,
    w_in_ref,
    w_out_ref,
    w_gate_ref,
    w_inc_ref,
    est_out_ref,
    cell_out_ref,
    est_ref,
    grad_ref,
    minus_ref,
    plus_ref,
    latent_ref,
    spread_ref,
    cell_ref,
    hidden_ref,
    hid16_ref,
    edge_ref,
    *,
    lat_count,
):
    lat = lat_ref[0]
    lane = lax.broadcasted_iota(jnp.int32, (8, LANES), 1)
    zero = jnp.zeros((8, LANES), F32)

    def tile(index, count=1):
        return slice(index * LANES, (index + count) * LANES)

    def inside(first_tile, count):
        place = lax.broadcasted_iota(jnp.int32, (1, count * LANES), 1) + (first_tile * LANES + 64)
        row = lax.shift_right_logical(place, 8) - FIRST + lat * ROWS
        return (row >= 0) & (row < lat_count * ROWS)

    def unpack(ref, first, row_slot, east):
        part, slot = divmod(row_slot, 16)
        value = ref[first + 8 * part : first + 8 * part + 8, :]
        return lane_roll(value, -8 * slot if east else -8 * slot - 8)

    def side(first, here_slot, next_slot, count):
        right = unpack(frome_ref, first, here_slot, True) if 0 <= here_slot < count else zero
        left = unpack(fromw_ref, first, next_slot, False) if 0 <= next_slot < count else zero
        return jnp.where(lane < 8, right, jnp.where(lane >= 120, left, 0.0))

    est_ref[:, 0:LANES] = zero
    est_ref[:, tile(58, 2)] = jnp.zeros((8, 2 * LANES), F32)
    for block in range(0, 29):
        row = block - FIRST
        if block >= 1:
            est_ref[:, tile(2 * block)] = day_rows(low_ref, mid_ref, high_ref, row)
        est_ref[:, tile(2 * block + 1)] = side(0, row + 6, row + 7, 28)

    ones = jnp.where(lax.broadcasted_iota(jnp.int32, (8, 256), 0) < 3, 1.0, 0.0).astype(F32)

    def shifted(ref, first_tile, count):
        value = ref[:, tile(first_tile, count)]
        minus_ref[:, tile(first_tile, count)] = lane_roll(value, 1)
        plus_ref[:, tile(first_tile, count)] = lane_roll(value, -1)

    def windows(ref, tiles):
        pieces = []
        for a in (-2, 0, 2):
            for source in (minus_ref, ref, plus_ref):
                pieces.append(jnp.concatenate([source[:, tile(t + a)] for t in tiles], axis=1))
        return jnp.concatenate(pieces + [ones], axis=0).astype(BF16)

    def prior(first_row, last_row):
        low_tile = 2 * (first_row - 1 + FIRST) - 1
        high_tile = 2 * (last_row + 1 + FIRST) + 2
        shifted(est_ref, low_tile - 2, high_tile - low_tile + 5)
        for t in range(low_tile, high_tile, 2):
            value = jnp.dot(w_in_ref[...], windows(est_ref, (t, t + 1)), preferred_element_type=F32)
            value = jnp.maximum(value, 0.0)
            if t + 2 > 2 * (ROWS + FIRST) - 2 or t < 2 * FIRST:
                value = jnp.where(inside(t, 2), value, 0.0)
            latent_ref[:, tile(t, 2)] = value.astype(BF16)
            spread_ref[:, tile(t, 2)] = jnp.dot(w_out_ref[...], latent_ref[:, tile(t, 2)], preferred_element_type=F32)
        out_tile = low_tile + 2
        count = 2 * (last_row + FIRST) + 2 - out_tile
        columns = []
        for b in range(3):
            total = None
            for a in range(3):
                k = 8 * (3 * a + b)
                piece = spread_ref[k : k + 8, tile(out_tile + 2 * a - 2, count)]
                total = piece if total is None else total + piece
            columns.append(total)
        grad_ref[:, tile(out_tile, count)] = -(columns[1] + lane_roll(columns[0], 1) + lane_roll(columns[2], -1))

    prior(-4, 19)
    for t in range(5, 54):
        block = t // 2
        row = block - FIRST
        if t % 2 == 0:
            extra = adjoint_ref[row + 4]
        else:
            extra = side(16, row + 4, row + 5, 24)
        total = est_ref[:, tile(t)] + grad_ref[:, tile(t)] + extra
        if row < 0 or row >= ROWS - 1:
            total = jnp.where(inside(t, 1), total, 0.0)
        grad_ref[:, tile(t)] = total
    grad_ref[:, tile(54)] = zero
    shifted(grad_ref, 5, 50)
    for t in range(7, 53, 2):
        sums = jnp.dot(w_gate_ref[HID:, 0:80], windows(grad_ref, (t, t + 1)), preferred_element_type=F32)
        gate_in = 0.5 * jnp.tanh(sums[0:HID]) + 0.5
        gate_out = 0.5 * jnp.tanh(sums[HID : 2 * HID]) + 0.5
        cell = gate_in * jnp.tanh(sums[2 * HID : 3 * HID])
        hidden = gate_out * jnp.tanh(cell)
        if t + 2 > 2 * (ROWS + FIRST) - 2 or t < 2 * FIRST:
            hidden = jnp.where(inside(t, 2), hidden, 0.0)
        cell_ref[:, tile(t, 2)] = cell
        hidden_ref[:, tile(t, 2)] = hidden
        update = jnp.dot(w_inc_ref[...], hidden.astype(BF16), preferred_element_type=F32)
        est_ref[:, tile(t, 2)] -= update[0:8]

    for group in range(0, HID, 16):
        value = hidden_ref[group : group + 16, tile(11, 37)]
        hid16_ref[0, group : group + 16, tile(11, 37)] = lane_roll(value, 1).astype(BF16)
        hid16_ref[1, group : group + 16, tile(11, 37)] = value.astype(BF16)
        hid16_ref[2, group : group + 16, tile(11, 37)] = lane_roll(value, -1).astype(BF16)

    prior(-1, 16)
    edges = jnp.concatenate(
        [fromw_ref[32:48, :], frome_ref[32:48, :], jnp.zeros((LANES - 32, LANES), F32)], axis=0
    )
    edge_ref[...] = edges.T
    carried = zero
    carried_w = zero
    carried_e = zero
    side_w = {}
    side_e = {}
    for row in range(-2, 17):
        base = row + 5
        block = row + FIRST
        now, later = adjoint_terms(sums_ref, base, est_ref[:, tile(2 * block)], est_ref[:, tile(2 * block + 2)])
        if row > -2:
            grad_ref[:, tile(2 * block)] += est_ref[:, tile(2 * block)] + carried + now
        carried = later
        factors = edge_ref[pl.ds(5 * base, 8), :]

        def edge_term(first, e0, e1, e2, e3):
            def factor(j):
                return factors[:, first + j : first + j + 1]

            return factor(1) * e0 + factor(2) * e1 + factor(3) * e2 + factor(4) * e3 - factor(0)

        here = est_ref[:, tile(2 * block - 1)]
        above = est_ref[:, tile(2 * block + 1)]
        far_here, far_above = lane_roll(here, 1), lane_roll(above, 1)
        side_w[row] = carried_w + edge_term(0, far_here, here, far_above, above)
        carried_w = edge_term(8, far_here, here, far_above, above)
        here = above
        above = est_ref[:, tile(2 * block + 3)]
        far_here, far_above = lane_roll(here, -1), lane_roll(above, -1)
        side_e[row] = carried_e + edge_term(16, here, far_here, above, far_above)
        carried_e = edge_term(24, here, far_here, above, far_above)
    for row in range(-2, 17):
        block = row + FIRST
        t = 2 * block + 1
        right = side_e[row] if row > -2 else zero
        left = side_w[row + 1] if row < 16 else zero
        grad_ref[:, tile(t)] += est_ref[:, tile(t)] + jnp.where(lane < 64, right, left)
    for t in (11, 12, 13, 45, 46, 47):
        grad_ref[:, tile(t)] = jnp.where(inside(t, 1), grad_ref[:, tile(t)], 0.0)
    shifted(grad_ref, 11, 37)
    for row in range(0, ROWS, 2):
        tiles = (2 * (row + FIRST), 2 * (row + FIRST) + 2)
        pieces = [windows(grad_ref, tiles)]
        for a in (-2, 0, 2):
            for b in range(3):
                pieces.append(jnp.concatenate([hid16_ref[b, :, tile(t + a)] for t in tiles], axis=1))
        sums = jnp.dot(w_gate_ref[...], jnp.concatenate(pieces, axis=0), preferred_element_type=F32)
        old = jnp.concatenate([cell_ref[:, tile(t)] for t in tiles], axis=1)
        forget = 0.5 * jnp.tanh(sums[0:HID]) + 0.5
        gate_in = 0.5 * jnp.tanh(sums[HID : 2 * HID]) + 0.5
        gate_out = 0.5 * jnp.tanh(sums[2 * HID : 3 * HID]) + 0.5
        cell = forget * old + gate_in * jnp.tanh(sums[3 * HID :])
        hidden = gate_out * jnp.tanh(cell)
        update = jnp.dot(w_inc_ref[...], hidden.astype(BF16), preferred_element_type=F32)
        for k in range(2):
            cell_out_ref[pl.ds(row + k, HID, stride=ROWS), :] = cell[:, tile(k)]
            final = est_ref[:, tile(tiles[k])] - update[0:8, tile(k)]
            est_out_ref[pl.ds(row + k, DAYS, stride=ROWS), :] = final[0:DAYS]


def bias_pieces(bias):
    high = lax.reduce_precision(bias, 8, 7)
    middle = lax.reduce_precision(bias - high, 8, 7)
    low = bias - high - middle
    pieces = jnp.stack([high, middle, low], axis=1).astype(BF16)
    return jnp.pad(pieces, ((0, 0), (0, 5)))


def by_offset(weight):
    padded = jnp.pad(weight, ((0, 0), (0, 0), (0, 8 - DAYS)))
    return jnp.transpose(padded, (1, 0, 2)).reshape(weight.shape[1], 72)


def on_device(
    state,
    prior_in,
    prior_bias,
    prior_out,
    lstm_weight,
    lstm_bias,
    lstm_out,
    obs_value,
    obs_weight,
    obs_tile,
    obs_time,
    obs_row,
    obs_col,
):
    lat_count = lax.axis_size("lat")
    lon_count = lax.axis_size("lon")
    keys = jnp.stack([obs_time, obs_tile[:, 0] * ROWS + obs_row, obs_col]).astype(F32)
    track = jnp.concatenate([obs_value[None], obs_weight, keys], axis=0).astype(BF16)
    gathered = lax.all_gather(track, "lat", axis=0, tiled=True)

    up = [(i, i + 1) for i in range(lat_count - 1)]
    down = [(i + 1, i) for i in range(lat_count - 1)]
    low = lax.ppermute(state[:, ROWS - HALO :], "lat", up).reshape(DAYS * HALO, LANES)
    high = lax.ppermute(state[:, :HALO], "lat", down).reshape(DAYS * HALO, LANES)
    mid = state.reshape(DAYS * ROWS, LANES)
    lat = lax.axis_index("lat").astype(jnp.int32).reshape(1)

    w_in = jnp.concatenate([by_offset(prior_in), bias_pieces(prior_bias)], axis=1)
    w_out = jnp.pad(
        jnp.pad(prior_out, ((0, 0), (0, 8 - DAYS), (0, 0))).reshape(72, HID), ((0, 8), (0, 0))
    )
    half = jnp.concatenate([jnp.full((3 * HID,), 0.5, F32), jnp.ones((HID,), F32)])
    gates = jnp.concatenate(
        [lstm_weight[:, HID : 2 * HID], lstm_weight[:, :HID], lstm_weight[:, 2 * HID :]], axis=1
    ) * half.astype(BF16)[None, :, None]
    gate_bias = jnp.concatenate([lstm_bias[HID : 2 * HID], lstm_bias[:HID], lstm_bias[2 * HID :]]) * half
    w_gate = jnp.concatenate(
        [
            by_offset(gates[:, :, :DAYS]),
            bias_pieces(gate_bias),
            jnp.transpose(gates[:, :, DAYS:], (1, 0, 2)).reshape(4 * HID, 9 * HID),
        ],
        axis=1,
    )
    w_inc = jnp.pad(lstm_out, ((0, 16 - DAYS), (0, 0)))

    smem = pl.BlockSpec(memory_space=pltpu.SMEM)
    vmem = pl.BlockSpec(memory_space=pltpu.VMEM)
    sums, adjoint, to_east, to_west = pl.pallas_call(
        build_kernel,
        out_shape=(
            jax.ShapeDtypeStruct((8, 256, LANES), F32),
            jax.ShapeDtypeStruct((24, 8, LANES), F32),
            jax.ShapeDtypeStruct((48, LANES), F32),
            jax.ShapeDtypeStruct((48, LANES), F32),
        ),
        in_specs=[smem, vmem, vmem, vmem, vmem],
        out_specs=(vmem, vmem, vmem, vmem),
        scratch_shapes=[
            pltpu.VMEM((512, CHUNK), BF16),
            pltpu.VMEM((640, CHUNK), BF16),
            pltpu.VMEM((16, CHUNK), BF16),
            pltpu.VMEM((16, 512), F32),
        ],
        compiler_params=pltpu.CompilerParams(vmem_limit_bytes=32 * 1024 * 1024),
        name="build",
    )(lat, gathered, mid, low, high)

    east = [(i, (i + 1) % lon_count) for i in range(lon_count)]
    west = [(target, source) for source, target in east]
    from_west = lax.ppermute(to_east, "lon", east)
    from_east = lax.ppermute(to_west, "lon", west)

    def solve(*refs):
        solve_kernel(*refs, lat_count=lat_count)

    width = TILES * LANES
    estimate, cell_state = pl.pallas_call(
        solve,
        out_shape=(
            jax.ShapeDtypeStruct((DAYS * ROWS, LANES), F32),
            jax.ShapeDtypeStruct((HID * ROWS, LANES), F32),
        ),
        in_specs=[smem] + [vmem] * 11,
        out_specs=(vmem, vmem),
        scratch_shapes=[
            pltpu.VMEM((8, width), F32),
            pltpu.VMEM((8, width), F32),
            pltpu.VMEM((8, width), F32),
            pltpu.VMEM((8, width), F32),
            pltpu.VMEM((HID, width), BF16),
            pltpu.VMEM((80, width), F32),
            pltpu.VMEM((HID, width), F32),
            pltpu.VMEM((HID, width), F32),
            pltpu.VMEM((3, HID, width), BF16),
            pltpu.VMEM((LANES, LANES), F32),
        ],
        compiler_params=pltpu.CompilerParams(vmem_limit_bytes=32 * 1024 * 1024),
        name="solve",
    )(lat, mid, low, high, sums, adjoint, from_west, from_east, w_in, w_out, w_gate, w_inc)
    return (
        estimate.reshape(DAYS, ROWS, LANES),
        cell_state.reshape(HID, ROWS, LANES),
    )


def solution(mesh):
    return jax.shard_map(
        on_device,
        mesh=mesh,
        in_specs=(
            P(None, "lat", "lon"),
            P(),
            P(),
            P(),
            P(),
            P(),
            P(),
            P(("lon", "lat")),
            P(None, ("lon", "lat")),
            P(("lon", "lat"), None),
            P(("lon", "lat")),
            P(("lon", "lat")),
            P(("lon", "lat")),
        ),
        out_specs=(P(None, "lat", "lon"), P(None, "lat", "lon")),
        check_vma=False,
    )
```

```python
import jax
import jax.numpy as jnp
from jax import lax
from jax.experimental import pallas as pl
from jax.experimental.pallas import tpu as pltpu
from jax.sharding import PartitionSpec as P

DAYS = 5
ROWS = 16
COLS = 128
LANES = 128
HID = 64
TRACK = 512
HALO = 8
BASES = 25
CHUNK = 2048
FIRST = 7
STRIP = 30
TILES = 37
GROUP = 4
F32 = jnp.float32
BF16 = jnp.bfloat16


def nt_dot(left, right):
    return lax.dot_general(left, right, (((1,), (1,)), ((), ())), preferred_element_type=F32)


def lane_roll(value, shift):
    return pltpu.roll(value, shift % value.shape[1], 1)


def strip_place(row):
    return (row + 6) // 4, (row + 6) % 4 * 32


def day_rows(near_ref, mid_ref, far_ref, even, row):
    if 0 <= row < ROWS:
        picked = mid_ref[pl.ds(row, DAYS, stride=ROWS), :]
    else:
        place = pl.ds(row + HALO if row < 0 else row - ROWS, DAYS, stride=HALO)
        near, far = near_ref[place, :], far_ref[place, :]
        picked = jnp.where(even, far, near) if row < 0 else jnp.where(even, near, far)
    return jnp.concatenate([picked, jnp.zeros((8 - DAYS, LANES), F32)], axis=0)


def adjoint_terms(sums_ref, base, here, above):
    low = pl.ds(5 * base, 8)
    high = pl.ds(LANES + 5 * base, 8)
    here_right = lane_roll(here, -1)
    above_right = lane_roll(above, -1)
    s01 = sums_ref[1, low, :]
    s02 = sums_ref[2, low, :]
    s03 = sums_ref[3, low, :]
    s12 = sums_ref[2, high, :]
    s13 = sums_ref[3, high, :]
    s23 = sums_ref[6, low, :]
    g0 = sums_ref[0, low, :] * here + s01 * here_right + s02 * above + s03 * above_right - sums_ref[4, low, :]
    g1 = s01 * here + sums_ref[1, high, :] * here_right + s12 * above + s13 * above_right - sums_ref[4, high, :]
    g2 = s02 * here + s12 * here_right + sums_ref[5, low, :] * above + s23 * above_right - sums_ref[7, low, :]
    g3 = s03 * here + s13 * here_right + s23 * above + sums_ref[6, high, :] * above_right - sums_ref[7, high, :]
    return g0 + lane_roll(g1, 1), g2 + lane_roll(g3, 1)


def track_kernel(value_ref, weight_ref, tile_ref, time_ref, row_ref, col_ref, out_ref):
    latitude = tile_ref[...] * ROWS + row_ref[...]
    keys = [time_ref[...].astype(F32), latitude.astype(F32), col_ref[...].astype(F32)]
    block = jnp.concatenate([value_ref[...], weight_ref[...]] + keys, axis=0)
    twice = jnp.concatenate([block, block], axis=0).astype(BF16)
    for k in range(out_ref.shape[0] // 16):
        out_ref[16 * k : 16 * k + 16, :] = twice


def prepare_kernel(gate_ref, gate_bias_ref, in_ref, in_bias_ref, out_ref, inc_ref, w_gate_ref, w_in_ref, w_out_ref, w_inc_ref):
    def rows_of(ref, k):
        return jnp.concatenate([ref[k].astype(F32)[0:DAYS], jnp.zeros((8 - DAYS, ref.shape[2]), F32)], axis=0)

    def bias_rows(bias):
        high = bias.astype(BF16).astype(F32)
        middle = (bias - high).astype(BF16).astype(F32)
        low = bias - high - middle
        return jnp.concatenate([high, middle, low, jnp.zeros((5, bias.shape[1]), F32)], axis=0)

    pieces = [rows_of(gate_ref, k) for k in range(9)] + [bias_rows(gate_bias_ref[...])]
    pieces += [gate_ref[k].astype(F32)[DAYS:] for k in range(9)]
    whole = jnp.concatenate(pieces + [jnp.zeros((768 - 656, 4 * HID), F32)], axis=0)
    for k in range(6):
        block = whole[128 * k : 128 * k + 128]
        first = lane_roll(block[:, 0:128], HID) * 0.5
        second = block[:, 128:256]
        lane = lax.broadcasted_iota(jnp.int32, (128, 128), 1)
        second = jnp.where(lane < HID, 0.5 * second, second)
        w_gate_ref[0:128, 128 * k : 128 * k + 128] = first.T.astype(BF16)
        w_gate_ref[128:256, 128 * k : 128 * k + 128] = second.T.astype(BF16)
    narrow = jnp.concatenate([rows_of(in_ref, k) for k in range(9)] + [bias_rows(in_bias_ref[...])], axis=0)
    narrow = jnp.concatenate([narrow, jnp.zeros((48, HID), F32)], axis=0)
    narrow = jnp.concatenate([narrow, jnp.zeros((128, 128 - HID), F32)], axis=1)
    w_in_ref[...] = narrow.T[0:HID].astype(BF16)
    spread = [rows_of(out_ref, k) for k in range(9)]
    w_out_ref[...] = jnp.concatenate(spread + [jnp.zeros((8, HID), F32)], axis=0).astype(BF16)
    w_inc_ref[...] = jnp.concatenate(
        [inc_ref[...].astype(F32), jnp.zeros((16 - DAYS, HID), F32)], axis=0
    ).astype(BF16)


EAST_FIELDS = ((4, 1), (1, 0), (1, 1), (2, 1), (3, 1), (7, 1), (3, 0), (6, 0), (6, 1))
WEST_FIELDS = ((4, 0), (0, 0), (1, 0), (2, 0), (3, 0), (7, 0), (2, 1), (5, 0), (6, 0))
EAST_LANES = ((0, 1, 2, 3, 4), (5, 6, 4, 7, 8))
WEST_LANES = ((0, 1, 2, 3, 4), (5, 3, 6, 7, 8))


def build_kernel(
    place_ref, track_ref, mid_ref, near_ref, far_ref, sums_ref, adjoint_ref, to_near_ref, to_far_ref, rw_ref, cw_ref
):
    base_row = (place_ref[0] * ROWS - 5).astype(F32)
    even_lat = place_ref[0] % 2 == 0
    even_lon = place_ref[1] % 2 == 0
    entry = lax.broadcasted_iota(jnp.int32, (LANES, TRACK), 0).astype(F32).astype(BF16)
    nothing = jnp.zeros((LANES, TRACK), BF16)

    def spread(row):
        part = jnp.broadcast_to(row, (16, TRACK)).astype(BF16)
        return jnp.concatenate([part] * 8, axis=0)

    per_chunk = CHUNK // TRACK
    chunks = track_ref.shape[0] * TRACK // (8 * CHUNK)
    for chunk in range(chunks):
        slot = chunk % 2
        for pair in range(per_chunk // 2):
            first_row = chunk * per_chunk * 8 + pair * 16
            both = track_ref[first_row : first_row + 16, :].astype(F32)
            for part in range(2):
                block = both[8 * part : 8 * part + 8]
                at = (2 * pair + part) * TRACK
                offset = block[6:7] - base_row
                within = (offset >= 0.0) & (offset < float(BASES))
                row_hit = entry == spread(jnp.where(within, offset * 5.0 + block[5:6], -1.0))
                col_hit = entry == spread(block[7:8])
                for k in range(5):
                    source = (1 + k) % 5
                    value = spread(block[source : source + 1])
                    if k < 4:
                        rw_ref[slot, 128 * k : 128 * k + 128, at : at + TRACK] = jnp.where(row_hit, value, nothing)
                    cw_ref[slot, 128 * k : 128 * k + 128, at : at + TRACK] = jnp.where(col_hit, value, nothing)
        first = nt_dot(rw_ref[slot, 0:256, :], cw_ref[slot])
        second = nt_dot(rw_ref[slot, 256:512, :], cw_ref[slot, 256:640, :])
        for k in range(8):
            total = first[:, 128 * k : 128 * k + 128] if k < 5 else second[:, 128 * k - 640 : 128 * k - 512]
            sums_ref[k] = total if chunk == 0 else sums_ref[k] + total

    lane = lax.broadcasted_iota(jnp.int32, (8, LANES), 1)
    zero = jnp.zeros((8, LANES), F32)
    east, west = zero, zero
    carried = zero
    for row in range(-6, ROWS + 6):
        part, place = strip_place(row)
        here = day_rows(near_ref, mid_ref, far_ref, even_lat, row)
        picked = lane // 8 == place // 8
        east = jnp.where(picked, lane_roll(here, place - 120), east)
        west = jnp.where(picked, lane_roll(here, place), west)
        if -5 <= row <= 19:
            above = day_rows(near_ref, mid_ref, far_ref, even_lat, row + 1)
            now, later = adjoint_terms(sums_ref, row + 5, here, above)
            if row > -5:
                total = carried + now
                adjoint_ref[row + 4] = total
                picked = lane // 8 == place // 8 + 1
                east = jnp.where(picked, lane_roll(total, place + 8 - 120), east)
                west = jnp.where(picked, lane_roll(total, place + 8), west)
            carried = later
        if -2 <= row <= ROWS:
            for k in range(9):
                target = place + 16 + k
                array, half = EAST_FIELDS[k]
                piece = sums_ref[array, pl.ds(LANES * half + 5 * (row + 5), 8), :]
                east = jnp.where(lane == target, lane_roll(piece, target - (COLS - 2)), east)
                array, half = WEST_FIELDS[k]
                piece = sums_ref[array, pl.ds(LANES * half + 5 * (row + 5), 8), :]
                west = jnp.where(lane == target, lane_roll(piece, target), west)
        if place == 96:
            to_near_ref[8 * part : 8 * part + 8, :] = jnp.where(even_lon, east, west)
            to_far_ref[8 * part : 8 * part + 8, :] = jnp.where(even_lon, west, east)
            east, west = zero, zero


def solve_kernel(
    place_ref,
    mid_ref,
    near_ref,
    far_ref,
    sums_ref,
    adjoint_ref,
    own_near_ref,
    own_far_ref,
    from_near_ref,
    from_far_ref,
    w_in_ref,
    w_out_ref,
    w_gate_ref,
    w_inc_ref,
    est_out_ref,
    cell_out_ref,
    est_ref,
    grad_ref,
    minus_ref,
    plus_ref,
    mask_ref,
    window_ref,
    spread_ref,
    cell_ref,
    hidden_ref,
    hid_minus_ref,
    hid_plus_ref,
    *,
    lat_count,
):
    lat = place_ref[0]
    even_lat = lat % 2 == 0
    even_lon = place_ref[1] % 2 == 0
    lane = lax.broadcasted_iota(jnp.int32, (8, LANES), 1)
    zero = jnp.zeros((8, LANES), F32)
    strips = slice(STRIP * LANES, TILES * LANES)
    strip_width = (TILES - STRIP) * LANES
    strip_lane = lax.broadcasted_iota(jnp.int32, (8, strip_width), 1)

    def tile(index, count=1):
        return slice(index * LANES, (index + count) * LANES)

    def at(row):
        return tile(row + FIRST)

    def within(row):
        row = row + lat * ROWS
        return (row >= 0) & (row < lat_count * ROWS)

    def left(main, strip, row):
        part, place = strip_place(row)
        edge = lane_roll(strip[:, tile(part)], -(place + 7))
        return jnp.where(lane[: main.shape[0]] == 0, edge, lane_roll(main, 1))

    def right(main, strip, row):
        part, place = strip_place(row)
        edge = lane_roll(strip[:, tile(part)], 127 - (place + 24))
        return jnp.where(lane[: main.shape[0]] == 127, edge, lane_roll(main, -1))

    est_ref[:, at(-7)] = zero
    est_ref[:, at(22)] = zero
    for row in range(-6, 22):
        est_ref[:, at(row)] = day_rows(near_ref, mid_ref, far_ref, even_lat, row)
    quarter = (lane % 32) // 8
    from_west, from_east, adjoint_strip = [], [], []
    for part in range(TILES - STRIP):
        rows = slice(8 * part, 8 * part + 8)
        own_east = jnp.where(even_lon, own_near_ref[rows, :], own_far_ref[rows, :])
        own_west = jnp.where(even_lon, own_far_ref[rows, :], own_near_ref[rows, :])
        west = jnp.where(even_lon, from_far_ref[rows, :], from_near_ref[rows, :])
        east = jnp.where(even_lon, from_near_ref[rows, :], from_far_ref[rows, :])
        from_west.append(west)
        from_east.append(east)

        def join(first, second, third, fourth):
            return jnp.where(
                quarter < 2, jnp.where(quarter == 0, first, second), jnp.where(quarter == 2, third, fourth)
            )

        est_ref[:, tile(STRIP + part)] = join(west, lane_roll(own_west, 8), lane_roll(own_east, 16), lane_roll(east, 24))
        adjoint_strip.append(join(lane_roll(west, -8), own_west, lane_roll(own_east, 8), lane_roll(east, 16)))
    from_west = jnp.concatenate(from_west, axis=1)
    from_east = jnp.concatenate(from_east, axis=1)
    adjoint_strip = jnp.concatenate(adjoint_strip, axis=1)
    for row in range(-7, 23):
        mask_ref[:, at(row)] = jnp.where(within(row), jnp.ones((8, LANES), F32), 0.0)
    mask_ref[:, strips] = jnp.where(within(strip_lane // 32 - 6), 1.0, 0.0)

    ones = jnp.where(lax.broadcasted_iota(jnp.int32, (8, LANES), 0) < 3, 1.0, 0.0).astype(F32)

    def windows(ref, first_row, last_row, with_strips):
        strip = ref[:, strips]
        for row in range(first_row - 1, last_row + 2):
            main = ref[:, at(row)]
            minus_ref[:, at(row)] = left(main, strip, row)
            plus_ref[:, at(row)] = right(main, strip, row)
        for row in range(first_row, last_row + 1):
            pieces = [source[:, at(row + a)] for a in (-1, 0, 1) for source in (minus_ref, ref, plus_ref)]
            window_ref[:, at(row)] = jnp.concatenate(pieces + [ones], axis=0).astype(BF16)
        if with_strips:
            pieces = []
            shifts = (lane_roll(strip, 1), strip, lane_roll(strip, -1))
            for a in (-1, 0, 1):
                pieces += [lane_roll(value, -32 * a) if a else value for value in shifts]
            pieces.append(jnp.concatenate([ones] * (TILES - STRIP), axis=1))
            window_ref[:, strips] = jnp.concatenate(pieces, axis=0).astype(BF16)

    def pieces_of(first_row, last_row):
        runs = [(first_row + FIRST, last_row + 1 + FIRST), (STRIP, TILES)]
        return [tile(t, min(GROUP, end - t)) for start, end in runs for t in range(start, end, GROUP)]

    def gradient(first_row, last_row):
        windows(est_ref, first_row - 1, last_row + 1, True)
        for where in pieces_of(first_row - 1, last_row + 1):
            value = jnp.dot(w_in_ref[:, 0:80], window_ref[:, where], preferred_element_type=F32)
            value = jnp.maximum(value, 0.0) * mask_ref[0:1, where]
            spread_ref[:, where] = jnp.dot(w_out_ref[...], value.astype(BF16), preferred_element_type=F32)
        totals = []
        for b in range(3):
            total = None
            for a in range(3):
                k = 8 * (3 * a + b)
                piece = spread_ref[k : k + 8, strips]
                piece = lane_roll(piece, 32 - 32 * a) if a != 1 else piece
                total = piece if total is None else total + piece
            totals.append(total)
        grad_ref[:, strips] = est_ref[:, strips] - (totals[1] + lane_roll(totals[0], 1) + lane_roll(totals[2], -1))
        for row in range(first_row, last_row + 1):
            columns = []
            for b in range(3):
                terms = [spread_ref[8 * (3 * a + b) : 8 * (3 * a + b) + 8, at(row + a - 1)] for a in range(3)]
                columns.append(terms[0] + terms[1] + terms[2])
            term = columns[1] + left(columns[0], totals[0], row) + right(columns[2], totals[2], row)
            grad_ref[:, at(row)] = est_ref[:, at(row)] - term

    gradient(-4, 19)
    for row in range(-4, 20):
        total = grad_ref[:, at(row)] + adjoint_ref[row + 4]
        grad_ref[:, at(row)] = total if 0 <= row < ROWS else total * mask_ref[:, at(row)]
    grad_ref[:, strips] = (grad_ref[:, strips] + adjoint_strip) * mask_ref[:, strips]
    windows(grad_ref, -3, 18, True)
    for where in pieces_of(-3, 18):
        sums = jnp.dot(w_gate_ref[HID:, 0:80], window_ref[:, where], preferred_element_type=F32)
        gate_in = 0.5 * jnp.tanh(sums[0:HID]) + 0.5
        gate_out = 0.5 * jnp.tanh(sums[HID : 2 * HID]) + 0.5
        cell = gate_in * jnp.tanh(sums[2 * HID : 3 * HID])
        hidden = (gate_out * jnp.tanh(cell) * mask_ref[0:1, where]).astype(BF16)
        cell_ref[:, where] = cell
        hidden_ref[:, where] = hidden
        update = jnp.dot(w_inc_ref[...], hidden, preferred_element_type=F32)
        est_ref[:, where] -= update[0:8]

    lane64 = lax.broadcasted_iota(jnp.int32, (HID, LANES), 1)
    for row in range(-1, ROWS + 1):
        part, place = strip_place(row)
        main = hidden_ref[:, at(row)].astype(F32)
        strip = hidden_ref[:, tile(STRIP + part)].astype(F32)
        hid_minus_ref[:, at(row)] = jnp.where(
            lane64 == 0, lane_roll(strip, -(place + 7)), lane_roll(main, 1)
        ).astype(BF16)
        hid_plus_ref[:, at(row)] = jnp.where(
            lane64 == 127, lane_roll(strip, 127 - (place + 24)), lane_roll(main, -1)
        ).astype(BF16)
    gradient(-1, 16)
    carried = zero
    for row in range(-2, ROWS + 1):
        now, later = adjoint_terms(sums_ref, row + 5, est_ref[:, at(row)], est_ref[:, at(row + 1)])
        if row > -2:
            total = grad_ref[:, at(row)] + carried + now
            grad_ref[:, at(row)] = total if 0 <= row < ROWS else total * mask_ref[:, at(row)]
        carried = later
    here = est_ref[:, strips]
    above = lane_roll(here, -32)

    def edge_term(source, lane_at, lanes, e0, e1, e2, e3):
        d, f0, f1, f2, f3 = [lane_roll(source, lane_at - (16 + k)) for k in lanes]
        return f0 * e0 + f1 * e1 + f2 * e2 + f3 * e3 - d

    west = (lane_roll(here, 1), here, lane_roll(above, 1), above)
    east = (here, lane_roll(here, -1), above, lane_roll(above, -1))
    extra_w = edge_term(from_west, 7, EAST_LANES[0], *west) + lane_roll(
        edge_term(from_west, 7, EAST_LANES[1], *west), 32
    )
    extra_e = edge_term(from_east, 24, WEST_LANES[0], *east) + lane_roll(
        edge_term(from_east, 24, WEST_LANES[1], *east), 32
    )
    grad_ref[:, strips] = (
        grad_ref[:, strips] + jnp.where(strip_lane % 32 < 16, extra_w, extra_e)
    ) * mask_ref[:, strips]
    windows(grad_ref, 0, ROWS - 1, False)
    for row in range(0, ROWS, 2):
        pieces = [window_ref[:, tile(row + FIRST, 2)]]
        for a in (-1, 0, 1):
            for source in (hid_minus_ref, hidden_ref, hid_plus_ref):
                pieces.append(source[:, tile(row + a + FIRST, 2)])
        sums = jnp.dot(w_gate_ref[:, 0:656], jnp.concatenate(pieces, axis=0), preferred_element_type=F32)
        old = cell_ref[:, tile(row + FIRST, 2)]
        forget = 0.5 * jnp.tanh(sums[0:HID]) + 0.5
        gate_in = 0.5 * jnp.tanh(sums[HID : 2 * HID]) + 0.5
        gate_out = 0.5 * jnp.tanh(sums[2 * HID : 3 * HID]) + 0.5
        cell = forget * old + gate_in * jnp.tanh(sums[3 * HID :])
        hidden = gate_out * jnp.tanh(cell)
        update = jnp.dot(w_inc_ref[...], hidden.astype(BF16), preferred_element_type=F32)
        for k in range(2):
            cell_out_ref[pl.ds(row + k, HID, stride=ROWS), :] = cell[:, tile(k)]
            final = est_ref[:, at(row + k)] - update[0:8, tile(k)]
            est_out_ref[pl.ds(row + k, DAYS, stride=ROWS), :] = final[0:DAYS]


def swap(value, axis, first, count, periodic):
    last = count if periodic else count - 1
    pairs = [(i, (i + 1) % count) for i in range(first, last, 2)]
    return lax.ppermute(value, axis, pairs + [(target, source) for source, target in pairs])


def on_device(
    state,
    prior_in,
    prior_bias,
    prior_out,
    lstm_weight,
    lstm_bias,
    lstm_out,
    obs_value,
    obs_weight,
    obs_tile,
    obs_time,
    obs_row,
    obs_col,
):
    lat_count = lax.axis_size("lat")
    lon_count = lax.axis_size("lon")
    lat = lax.axis_index("lat").astype(jnp.int32)
    lon = lax.axis_index("lon").astype(jnp.int32)
    place = jnp.stack([lat, lon])
    upper, lower = state[:, ROWS - HALO :], state[:, :HALO]
    even_lat = lat % 2 == 0
    far = swap(jnp.where(even_lat, lower, upper), "lat", 1, lat_count, False).reshape(DAYS * HALO, LANES)
    near = swap(jnp.where(even_lat, upper, lower), "lat", 0, lat_count, False).reshape(DAYS * HALO, LANES)
    mid = state.reshape(DAYS * ROWS, LANES)

    smem = pl.BlockSpec(memory_space=pltpu.SMEM)
    vmem = pl.BlockSpec(memory_space=pltpu.VMEM)
    track = pl.pallas_call(
        track_kernel,
        out_shape=jax.ShapeDtypeStruct((lat_count * 8, TRACK), BF16),
        in_specs=[vmem] * 6,
        out_specs=vmem,
        cost_estimate=pl.CostEstimate(flops=100_000, bytes_accessed=150_000, transcendentals=0),
        name="track",
    )(
        obs_value.reshape(1, TRACK),
        obs_weight,
        obs_tile.reshape(1, TRACK),
        obs_time.reshape(1, TRACK),
        obs_row.reshape(1, TRACK),
        obs_col.reshape(1, TRACK),
    )
    track, near, far = lax.optimization_barrier((track, near, far))
    gathered = lax.all_to_all(
        track.reshape(lat_count, 8, TRACK), "lat", split_axis=0, concat_axis=0, tiled=True
    ).reshape(lat_count * 8, TRACK)
    w_gate, w_in, w_out, w_inc = pl.pallas_call(
        prepare_kernel,
        out_shape=(
            jax.ShapeDtypeStruct((4 * HID, 768), BF16),
            jax.ShapeDtypeStruct((HID, LANES), BF16),
            jax.ShapeDtypeStruct((80, HID), BF16),
            jax.ShapeDtypeStruct((16, HID), BF16),
        ),
        in_specs=[vmem] * 6,
        out_specs=(vmem,) * 4,
        compiler_params=pltpu.CompilerParams(vmem_limit_bytes=16 * 1024 * 1024),
        cost_estimate=pl.CostEstimate(flops=2_000_000, bytes_accessed=1_500_000, transcendentals=0),
        name="prepare",
    )(
        jnp.transpose(lstm_weight, (0, 2, 1)),
        lstm_bias.reshape(1, 4 * HID),
        jnp.transpose(prior_in, (0, 2, 1)),
        prior_bias.reshape(1, HID),
        prior_out,
        lstm_out,
    )
    sums, adjoint, to_near, to_far = pl.pallas_call(
        build_kernel,
        out_shape=(
            jax.ShapeDtypeStruct((8, 256, LANES), F32),
            jax.ShapeDtypeStruct((24, 8, LANES), F32),
            jax.ShapeDtypeStruct((56, LANES), F32),
            jax.ShapeDtypeStruct((56, LANES), F32),
        ),
        in_specs=[smem, vmem, vmem, vmem, vmem],
        out_specs=(vmem, vmem, vmem, vmem),
        scratch_shapes=[
            pltpu.VMEM((2, 512, CHUNK), BF16),
            pltpu.VMEM((2, 640, CHUNK), BF16),
        ],
        compiler_params=pltpu.CompilerParams(vmem_limit_bytes=32 * 1024 * 1024),
        cost_estimate=pl.CostEstimate(flops=4_000_000_000, bytes_accessed=1_500_000, transcendentals=0),
        name="build",
    )(place, gathered, mid, near, far)

    from_far = swap(to_far, "lon", 1, lon_count, True)
    from_near = swap(to_near, "lon", 0, lon_count, True)

    def solve(*refs):
        solve_kernel(*refs, lat_count=lat_count)

    width = TILES * LANES
    estimate, cell_state = pl.pallas_call(
        solve,
        out_shape=(
            jax.ShapeDtypeStruct((DAYS * ROWS, LANES), F32),
            jax.ShapeDtypeStruct((HID * ROWS, LANES), F32),
        ),
        in_specs=[smem] + [vmem] * 13,
        out_specs=(vmem, vmem),
        scratch_shapes=[
            pltpu.VMEM((8, width), F32),
            pltpu.VMEM((8, width), F32),
            pltpu.VMEM((8, width), F32),
            pltpu.VMEM((8, width), F32),
            pltpu.VMEM((8, width), F32),
            pltpu.VMEM((80, width), BF16),
            pltpu.VMEM((80, width), F32),
            pltpu.VMEM((HID, width), F32),
            pltpu.VMEM((HID, width), BF16),
            pltpu.VMEM((HID, width), BF16),
            pltpu.VMEM((HID, width), BF16),
        ],
        compiler_params=pltpu.CompilerParams(vmem_limit_bytes=32 * 1024 * 1024),
        name="solve",
    )(place, mid, near, far, sums, adjoint, to_near, to_far, from_near, from_far, w_in, w_out, w_gate, w_inc)
    return (
        estimate.reshape(DAYS, ROWS, LANES),
        cell_state.reshape(HID, ROWS, LANES),
    )


def solution(mesh):
    return jax.shard_map(
        on_device,
        mesh=mesh,
        in_specs=(
            P(None, "lat", "lon"),
            P(),
            P(),
            P(),
            P(),
            P(),
            P(),
            P(("lon", "lat")),
            P(None, ("lon", "lat")),
            P(("lon", "lat"), None),
            P(("lon", "lat")),
            P(("lon", "lat")),
            P(("lon", "lat")),
        ),
        out_specs=(P(None, "lat", "lon"), P(None, "lat", "lon")),
        check_vma=False,
    )
```

```python
import jax
import jax.numpy as jnp
from jax import lax
from jax.experimental import pallas as pl
from jax.experimental.pallas import tpu as pltpu
from jax.sharding import PartitionSpec as P

DAYS = 5
ROWS = 16
COLS = 128
LANES = 128
HID = 64
TRACK = 512
HALO = 8
BASES = 25
CHUNK = 2048
FIRST = 7
STRIP = 30
TILES = 37
GROUP = 4
F32 = jnp.float32
BF16 = jnp.bfloat16


def nt_dot(left, right):
    return lax.dot_general(left, right, (((1,), (1,)), ((), ())), preferred_element_type=F32)


def lane_roll(value, shift):
    return pltpu.roll(value, shift % value.shape[1], 1)


def strip_place(row):
    return (row + 6) // 4, (row + 6) % 4 * 32


def day_rows(near_ref, mid_ref, far_ref, even, row):
    if 0 <= row < ROWS:
        picked = mid_ref[pl.ds(row, DAYS, stride=ROWS), :]
    else:
        place = pl.ds(row + HALO if row < 0 else row - ROWS, DAYS, stride=HALO)
        near, far = near_ref[place, :], far_ref[place, :]
        picked = jnp.where(even, far, near) if row < 0 else jnp.where(even, near, far)
    return jnp.concatenate([picked, jnp.zeros((8 - DAYS, LANES), F32)], axis=0)


def adjoint_terms(sums_ref, base, here, above):
    low = pl.ds(5 * base, 8)
    high = pl.ds(LANES + 5 * base, 8)
    here_right = lane_roll(here, -1)
    above_right = lane_roll(above, -1)
    s01 = sums_ref[1, low, :]
    s02 = sums_ref[2, low, :]
    s03 = sums_ref[3, low, :]
    s12 = sums_ref[2, high, :]
    s13 = sums_ref[3, high, :]
    s23 = sums_ref[6, low, :]
    g0 = sums_ref[0, low, :] * here + s01 * here_right + s02 * above + s03 * above_right - sums_ref[4, low, :]
    g1 = s01 * here + sums_ref[1, high, :] * here_right + s12 * above + s13 * above_right - sums_ref[4, high, :]
    g2 = s02 * here + s12 * here_right + sums_ref[5, low, :] * above + s23 * above_right - sums_ref[7, low, :]
    g3 = s03 * here + s13 * here_right + s23 * above + sums_ref[6, high, :] * above_right - sums_ref[7, high, :]
    return g0 + lane_roll(g1, 1), g2 + lane_roll(g3, 1)


def track_kernel(
    place_ref, value_ref, weight_ref, tile_ref, time_ref, row_ref, col_ref, state_ref, out_ref, to_near_ref, to_far_ref
):
    latitude = tile_ref[...] * ROWS + row_ref[...]
    keys = [time_ref[...].astype(F32), latitude.astype(F32), col_ref[...].astype(F32)]
    block = jnp.concatenate([value_ref[...], weight_ref[...]] + keys, axis=0)
    twice = jnp.concatenate([block, block], axis=0).astype(BF16)
    for k in range(out_ref.shape[0] // 16):
        out_ref[16 * k : 16 * k + 16, :] = twice
    even = place_ref[0] % 2 == 0
    for day in range(DAYS):
        lower = state_ref[ROWS * day : ROWS * day + HALO, :]
        upper = state_ref[ROWS * (day + 1) - HALO : ROWS * (day + 1), :]
        to_near_ref[HALO * day : HALO * day + HALO, :] = jnp.where(even, upper, lower)
        to_far_ref[HALO * day : HALO * day + HALO, :] = jnp.where(even, lower, upper)


def prepare_kernel(gate_ref, gate_bias_ref, in_ref, in_bias_ref, out_ref, inc_ref, w_gate_ref, w_in_ref, w_out_ref, w_inc_ref):
    def rows_of(ref, k):
        return jnp.concatenate([ref[k].astype(F32)[0:DAYS], jnp.zeros((8 - DAYS, ref.shape[2]), F32)], axis=0)

    def bias_rows(bias):
        high = bias.astype(BF16).astype(F32)
        middle = (bias - high).astype(BF16).astype(F32)
        low = bias - high - middle
        return jnp.concatenate([high, middle, low, jnp.zeros((5, bias.shape[1]), F32)], axis=0)

    pieces = [rows_of(gate_ref, k) for k in range(9)] + [bias_rows(gate_bias_ref[...])]
    pieces += [gate_ref[k].astype(F32)[DAYS:] for k in range(9)]
    whole = jnp.concatenate(pieces + [jnp.zeros((768 - 656, 4 * HID), F32)], axis=0)
    for k in range(6):
        block = whole[128 * k : 128 * k + 128]
        first = lane_roll(block[:, 0:128], HID) * 0.5
        second = block[:, 128:256]
        lane = lax.broadcasted_iota(jnp.int32, (128, 128), 1)
        second = jnp.where(lane < HID, 0.5 * second, second)
        w_gate_ref[0:128, 128 * k : 128 * k + 128] = first.T.astype(BF16)
        w_gate_ref[128:256, 128 * k : 128 * k + 128] = second.T.astype(BF16)
    narrow = jnp.concatenate([rows_of(in_ref, k) for k in range(9)] + [bias_rows(in_bias_ref[...])], axis=0)
    narrow = jnp.concatenate([narrow, jnp.zeros((48, HID), F32)], axis=0)
    narrow = jnp.concatenate([narrow, jnp.zeros((128, 128 - HID), F32)], axis=1)
    w_in_ref[...] = narrow.T[0:HID].astype(BF16)
    spread = [rows_of(out_ref, k) for k in range(9)]
    w_out_ref[...] = jnp.concatenate(spread + [jnp.zeros((8, HID), F32)], axis=0).astype(BF16)
    w_inc_ref[...] = jnp.concatenate(
        [inc_ref[...].astype(F32), jnp.zeros((16 - DAYS, HID), F32)], axis=0
    ).astype(BF16)


EAST_FIELDS = ((4, 1), (1, 0), (1, 1), (2, 1), (3, 1), (7, 1), (3, 0), (6, 0), (6, 1))
WEST_FIELDS = ((4, 0), (0, 0), (1, 0), (2, 0), (3, 0), (7, 0), (2, 1), (5, 0), (6, 0))
EAST_LANES = ((0, 1, 2, 3, 4), (5, 6, 4, 7, 8))
WEST_LANES = ((0, 1, 2, 3, 4), (5, 3, 6, 7, 8))


def build_kernel(
    place_ref, track_ref, mid_ref, near_ref, far_ref, sums_ref, adjoint_ref, to_far_ref, to_near_ref, rw_ref, cw_ref
):
    base_row = (place_ref[0] * ROWS - 5).astype(F32)
    even_lat = place_ref[0] % 2 == 0
    even_lon = place_ref[1] % 2 == 0
    entry = lax.broadcasted_iota(jnp.int32, (LANES, TRACK), 0).astype(F32).astype(BF16)
    nothing = jnp.zeros((LANES, TRACK), BF16)

    def spread(row):
        part = jnp.broadcast_to(row, (16, TRACK)).astype(BF16)
        return jnp.concatenate([part] * 8, axis=0)

    per_chunk = CHUNK // TRACK
    chunks = track_ref.shape[0] * TRACK // (8 * CHUNK)
    for chunk in range(chunks):
        slot = chunk % 2
        for pair in range(per_chunk // 2):
            first_row = chunk * per_chunk * 8 + pair * 16
            both = track_ref[first_row : first_row + 16, :].astype(F32)
            for part in range(2):
                block = both[8 * part : 8 * part + 8]
                at = (2 * pair + part) * TRACK
                offset = block[6:7] - base_row
                within = (offset >= 0.0) & (offset < float(BASES))
                row_hit = entry == spread(jnp.where(within, offset * 5.0 + block[5:6], -1.0))
                col_hit = entry == spread(block[7:8])
                for k in range(5):
                    source = (1 + k) % 5
                    value = spread(block[source : source + 1])
                    if k < 4:
                        rw_ref[slot, 128 * k : 128 * k + 128, at : at + TRACK] = jnp.where(row_hit, value, nothing)
                    cw_ref[slot, 128 * k : 128 * k + 128, at : at + TRACK] = jnp.where(col_hit, value, nothing)
        first = nt_dot(rw_ref[slot, 0:256, :], cw_ref[slot])
        second = nt_dot(rw_ref[slot, 256:512, :], cw_ref[slot, 256:640, :])
        for k in range(8):
            total = first[:, 128 * k : 128 * k + 128] if k < 5 else second[:, 128 * k - 640 : 128 * k - 512]
            sums_ref[k] = total if chunk == 0 else sums_ref[k] + total

    lane = lax.broadcasted_iota(jnp.int32, (8, LANES), 1)
    zero = jnp.zeros((8, LANES), F32)
    east, west = zero, zero
    carried = zero
    for row in range(-6, ROWS + 6):
        part, place = strip_place(row)
        here = day_rows(near_ref, mid_ref, far_ref, even_lat, row)
        picked = lane // 8 == place // 8
        east = jnp.where(picked, lane_roll(here, place - 120), east)
        west = jnp.where(picked, lane_roll(here, place), west)
        if -5 <= row <= 19:
            above = day_rows(near_ref, mid_ref, far_ref, even_lat, row + 1)
            now, later = adjoint_terms(sums_ref, row + 5, here, above)
            if row > -5:
                total = carried + now
                adjoint_ref[row + 4] = total
                picked = lane // 8 == place // 8 + 1
                east = jnp.where(picked, lane_roll(total, place + 8 - 120), east)
                west = jnp.where(picked, lane_roll(total, place + 8), west)
            carried = later
        if -2 <= row <= ROWS:
            for k in range(9):
                target = place + 16 + k
                array, half = EAST_FIELDS[k]
                piece = sums_ref[array, pl.ds(LANES * half + 5 * (row + 5), 8), :]
                east = jnp.where(lane == target, lane_roll(piece, target - (COLS - 2)), east)
                array, half = WEST_FIELDS[k]
                piece = sums_ref[array, pl.ds(LANES * half + 5 * (row + 5), 8), :]
                west = jnp.where(lane == target, lane_roll(piece, target), west)
        if place == 96:
            to_near_ref[8 * part : 8 * part + 8, :] = jnp.where(even_lon, east, west)
            to_far_ref[8 * part : 8 * part + 8, :] = jnp.where(even_lon, west, east)
            east, west = zero, zero


def row_mask(place_ref, lat_count, row):
    row = row + place_ref[0] * ROWS
    return (row >= 0) & (row < lat_count * ROWS)


def tile(index, count=1):
    return slice(index * LANES, (index + count) * LANES)


def at(row):
    return tile(row + FIRST)


def ones_rows():
    return jnp.where(lax.broadcasted_iota(jnp.int32, (8, LANES), 0) < 3, 1.0, 0.0).astype(F32)


def spread_terms(spread_ref, row):
    columns = []
    for b in range(3):
        terms = [spread_ref[8 * (3 * a + b) : 8 * (3 * a + b) + 8, at(row + a - 1)] for a in range(3)]
        columns.append(terms[0] + terms[1] + terms[2])
    return columns


def first_kernel(
    place_ref, mid_ref, near_ref, far_ref, w_in_ref, w_out_ref, out_ref, est_ref, minus_ref, plus_ref, window_ref, spread_ref, *, lat_count
):
    even_lat = place_ref[0] % 2 == 0
    for row in range(-6, 22):
        value = day_rows(near_ref, mid_ref, far_ref, even_lat, row)
        est_ref[:, at(row)] = value
        minus_ref[:, at(row)] = lane_roll(value, 1)
        plus_ref[:, at(row)] = lane_roll(value, -1)
    ones = ones_rows()
    for row in range(-5, 21):
        pieces = [source[:, at(row + a)] for a in (-1, 0, 1) for source in (minus_ref, est_ref, plus_ref)]
        window_ref[:, at(row)] = jnp.concatenate(pieces + [ones], axis=0).astype(BF16)
    groups = [(-5, 5), (0, 4), (4, 4), (8, 4), (12, 4), (16, 5)]
    for row, count in groups:
        where = tile(row + FIRST, count)
        value = jnp.dot(w_in_ref[:, 0:80], window_ref[:, where], preferred_element_type=F32)
        value = jnp.maximum(value, 0.0)
        if row < 0 or row >= ROWS:
            flags = [
                jnp.where(row_mask(place_ref, lat_count, row + k), jnp.ones((1, LANES), F32), 0.0) for k in range(count)
            ]
            value = value * jnp.concatenate(flags, axis=1)
        spread_ref[:, where] = jnp.dot(w_out_ref[...], value.astype(BF16), preferred_element_type=F32)
    for row in range(-4, 20):
        columns = spread_terms(spread_ref, row)
        term = columns[1] + lane_roll(columns[0], 1) + lane_roll(columns[2], -1)
        out_ref[row + 4] = est_ref[:, at(row)] - term


def solve_kernel(
    place_ref,
    mid_ref,
    near_ref,
    far_ref,
    sums_ref,
    adjoint_ref,
    first_ref,
    own_far_ref,
    own_near_ref,
    from_far_ref,
    from_near_ref,
    w_in_ref,
    w_out_ref,
    w_gate_ref,
    w_inc_ref,
    est_out_ref,
    cell_out_ref,
    est_ref,
    grad_ref,
    minus_ref,
    plus_ref,
    mask_ref,
    window_ref,
    spread_ref,
    cell_ref,
    hidden_ref,
    hid_minus_ref,
    hid_plus_ref,
    *,
    lat_count,
):
    lat = place_ref[0]
    even_lat = lat % 2 == 0
    even_lon = place_ref[1] % 2 == 0
    lane = lax.broadcasted_iota(jnp.int32, (8, LANES), 1)
    zero = jnp.zeros((8, LANES), F32)
    strips = slice(STRIP * LANES, TILES * LANES)
    strip_width = (TILES - STRIP) * LANES
    strip_lane = lax.broadcasted_iota(jnp.int32, (8, strip_width), 1)

    def within(row):
        return row_mask(place_ref, lat_count, row)

    def left(main, strip, row):
        part, place = strip_place(row)
        edge = lane_roll(strip[:, tile(part)], -(place + 7))
        return jnp.where(lane[: main.shape[0]] == 0, edge, lane_roll(main, 1))

    def right(main, strip, row):
        part, place = strip_place(row)
        edge = lane_roll(strip[:, tile(part)], 127 - (place + 24))
        return jnp.where(lane[: main.shape[0]] == 127, edge, lane_roll(main, -1))

    est_ref[:, at(-7)] = zero
    est_ref[:, at(22)] = zero
    for row in range(-6, 22):
        est_ref[:, at(row)] = day_rows(near_ref, mid_ref, far_ref, even_lat, row)
    quarter = (lane % 32) // 8
    from_west, from_east, adjoint_strip = [], [], []
    for part in range(TILES - STRIP):
        rows = slice(8 * part, 8 * part + 8)
        own_east = jnp.where(even_lon, own_near_ref[rows, :], own_far_ref[rows, :])
        own_west = jnp.where(even_lon, own_far_ref[rows, :], own_near_ref[rows, :])
        west = jnp.where(even_lon, from_far_ref[rows, :], from_near_ref[rows, :])
        east = jnp.where(even_lon, from_near_ref[rows, :], from_far_ref[rows, :])
        from_west.append(west)
        from_east.append(east)

        def join(first, second, third, fourth):
            return jnp.where(
                quarter < 2, jnp.where(quarter == 0, first, second), jnp.where(quarter == 2, third, fourth)
            )

        est_ref[:, tile(STRIP + part)] = join(west, lane_roll(own_west, 8), lane_roll(own_east, 16), lane_roll(east, 24))
        adjoint_strip.append(join(lane_roll(west, -8), own_west, lane_roll(own_east, 8), lane_roll(east, 16)))
    from_west = jnp.concatenate(from_west, axis=1)
    from_east = jnp.concatenate(from_east, axis=1)
    adjoint_strip = jnp.concatenate(adjoint_strip, axis=1)
    for row in range(-7, 23):
        mask_ref[:, at(row)] = jnp.where(within(row), jnp.ones((8, LANES), F32), 0.0)
    mask_ref[:, strips] = jnp.where(within(strip_lane // 32 - 6), 1.0, 0.0)

    ones = ones_rows()

    def windows(ref, first_row, last_row, with_strips):
        strip = ref[:, strips]
        for row in range(first_row - 1, last_row + 2) if first_row <= last_row else ():
            main = ref[:, at(row)]
            minus_ref[:, at(row)] = left(main, strip, row)
            plus_ref[:, at(row)] = right(main, strip, row)
        for row in range(first_row, last_row + 1):
            pieces = [source[:, at(row + a)] for a in (-1, 0, 1) for source in (minus_ref, ref, plus_ref)]
            window_ref[:, at(row)] = jnp.concatenate(pieces + [ones], axis=0).astype(BF16)
        if with_strips:
            pieces = []
            shifts = (lane_roll(strip, 1), strip, lane_roll(strip, -1))
            for a in (-1, 0, 1):
                pieces += [lane_roll(value, -32 * a) if a else value for value in shifts]
            pieces.append(jnp.concatenate([ones] * (TILES - STRIP), axis=1))
            window_ref[:, strips] = jnp.concatenate(pieces, axis=0).astype(BF16)

    def pieces_of(first_row, last_row):
        runs = [(first_row + FIRST, last_row + 1 + FIRST), (STRIP, TILES)]
        return [tile(t, min(GROUP, end - t)) for start, end in runs for t in range(start, end, GROUP)]

    def gradient(first_row, last_row, low, high):
        windows(est_ref, low, high, True)
        for where in pieces_of(low, high):
            value = jnp.dot(w_in_ref[:, 0:80], window_ref[:, where], preferred_element_type=F32)
            value = jnp.maximum(value, 0.0) * mask_ref[0:1, where]
            spread_ref[:, where] = jnp.dot(w_out_ref[...], value.astype(BF16), preferred_element_type=F32)
        totals = []
        for b in range(3):
            total = None
            for a in range(3):
                k = 8 * (3 * a + b)
                piece = spread_ref[k : k + 8, strips]
                piece = lane_roll(piece, 32 - 32 * a) if a != 1 else piece
                total = piece if total is None else total + piece
            totals.append(total)
        strip = est_ref[:, strips] - (totals[1] + lane_roll(totals[0], 1) + lane_roll(totals[2], -1))
        grad_ref[:, strips] = strip
        for row in range(first_row, last_row + 1):
            columns = spread_terms(spread_ref, row)
            term = columns[1] + left(columns[0], totals[0], row) + right(columns[2], totals[2], row)
            grad_ref[:, at(row)] = est_ref[:, at(row)] - term
        return strip

    strip = gradient(0, -1, 0, -1)
    for row in range(-4, 20):
        part, place = strip_place(row)
        edges = strip[:, tile(part)]
        total = jnp.where(
            lane < 2,
            lane_roll(edges, -(place + 8)),
            jnp.where(lane >= 126, lane_roll(edges, 126 - (place + 22)), first_ref[row + 4]),
        )
        total = total + adjoint_ref[row + 4]
        grad_ref[:, at(row)] = total if 0 <= row < ROWS else total * mask_ref[:, at(row)]
    grad_ref[:, strips] = (strip + adjoint_strip) * mask_ref[:, strips]
    windows(grad_ref, -3, 18, True)
    for where in pieces_of(-3, 18):
        sums = jnp.dot(w_gate_ref[HID:, 0:80], window_ref[:, where], preferred_element_type=F32)
        gate_in = 0.5 * jnp.tanh(sums[0:HID]) + 0.5
        gate_out = 0.5 * jnp.tanh(sums[HID : 2 * HID]) + 0.5
        cell = gate_in * jnp.tanh(sums[2 * HID : 3 * HID])
        hidden = (gate_out * jnp.tanh(cell) * mask_ref[0:1, where]).astype(BF16)
        cell_ref[:, where] = cell
        hidden_ref[:, where] = hidden
        update = jnp.dot(w_inc_ref[...], hidden, preferred_element_type=F32)
        est_ref[:, where] -= update[0:8]

    lane64 = lax.broadcasted_iota(jnp.int32, (HID, LANES), 1)
    for row in range(-1, ROWS + 1):
        part, place = strip_place(row)
        main = hidden_ref[:, at(row)].astype(F32)
        strip = hidden_ref[:, tile(STRIP + part)].astype(F32)
        hid_minus_ref[:, at(row)] = jnp.where(
            lane64 == 0, lane_roll(strip, -(place + 7)), lane_roll(main, 1)
        ).astype(BF16)
        hid_plus_ref[:, at(row)] = jnp.where(
            lane64 == 127, lane_roll(strip, 127 - (place + 24)), lane_roll(main, -1)
        ).astype(BF16)
    gradient(-1, 16, -2, 17)
    carried = zero
    for row in range(-2, ROWS + 1):
        now, later = adjoint_terms(sums_ref, row + 5, est_ref[:, at(row)], est_ref[:, at(row + 1)])
        if row > -2:
            total = grad_ref[:, at(row)] + carried + now
            grad_ref[:, at(row)] = total if 0 <= row < ROWS else total * mask_ref[:, at(row)]
        carried = later
    here = est_ref[:, strips]
    above = lane_roll(here, -32)

    def edge_term(source, lane_at, lanes, e0, e1, e2, e3):
        d, f0, f1, f2, f3 = [lane_roll(source, lane_at - (16 + k)) for k in lanes]
        return f0 * e0 + f1 * e1 + f2 * e2 + f3 * e3 - d

    west = (lane_roll(here, 1), here, lane_roll(above, 1), above)
    east = (here, lane_roll(here, -1), above, lane_roll(above, -1))
    extra_w = edge_term(from_west, 7, EAST_LANES[0], *west) + lane_roll(
        edge_term(from_west, 7, EAST_LANES[1], *west), 32
    )
    extra_e = edge_term(from_east, 24, WEST_LANES[0], *east) + lane_roll(
        edge_term(from_east, 24, WEST_LANES[1], *east), 32
    )
    grad_ref[:, strips] = (
        grad_ref[:, strips] + jnp.where(strip_lane % 32 < 16, extra_w, extra_e)
    ) * mask_ref[:, strips]
    windows(grad_ref, 0, ROWS - 1, False)
    for row in range(0, ROWS, 2):
        pieces = [window_ref[:, tile(row + FIRST, 2)]]
        for a in (-1, 0, 1):
            for source in (hid_minus_ref, hidden_ref, hid_plus_ref):
                pieces.append(source[:, tile(row + a + FIRST, 2)])
        sums = jnp.dot(w_gate_ref[:, 0:656], jnp.concatenate(pieces, axis=0), preferred_element_type=F32)
        old = cell_ref[:, tile(row + FIRST, 2)]
        forget = 0.5 * jnp.tanh(sums[0:HID]) + 0.5
        gate_in = 0.5 * jnp.tanh(sums[HID : 2 * HID]) + 0.5
        gate_out = 0.5 * jnp.tanh(sums[2 * HID : 3 * HID]) + 0.5
        cell = forget * old + gate_in * jnp.tanh(sums[3 * HID :])
        hidden = gate_out * jnp.tanh(cell)
        update = jnp.dot(w_inc_ref[...], hidden.astype(BF16), preferred_element_type=F32)
        for k in range(2):
            cell_out_ref[pl.ds(row + k, HID, stride=ROWS), :] = cell[:, tile(k)]
            final = est_ref[:, at(row + k)] - update[0:8, tile(k)]
            est_out_ref[pl.ds(row + k, DAYS, stride=ROWS), :] = final[0:DAYS]


def swap(value, axis, first, count, periodic):
    last = count if periodic else count - 1
    pairs = [(i, (i + 1) % count) for i in range(first, last, 2)]
    return lax.ppermute(value, axis, pairs + [(target, source) for source, target in pairs])


def on_device(
    state,
    prior_in,
    prior_bias,
    prior_out,
    lstm_weight,
    lstm_bias,
    lstm_out,
    obs_value,
    obs_weight,
    obs_tile,
    obs_time,
    obs_row,
    obs_col,
):
    lat_count = lax.axis_size("lat")
    lon_count = lax.axis_size("lon")
    lat = lax.axis_index("lat").astype(jnp.int32)
    lon = lax.axis_index("lon").astype(jnp.int32)
    place = jnp.stack([lat, lon])
    mid = state.reshape(DAYS * ROWS, LANES)

    smem = pl.BlockSpec(memory_space=pltpu.SMEM)
    vmem = pl.BlockSpec(memory_space=pltpu.VMEM)
    track, lat_near, lat_far = pl.pallas_call(
        track_kernel,
        out_shape=(
            jax.ShapeDtypeStruct((lat_count * 8, TRACK), BF16),
            jax.ShapeDtypeStruct((DAYS * HALO, LANES), F32),
            jax.ShapeDtypeStruct((DAYS * HALO, LANES), F32),
        ),
        in_specs=[smem] + [vmem] * 7,
        out_specs=(vmem, vmem, vmem),
        cost_estimate=pl.CostEstimate(flops=100_000, bytes_accessed=150_000, transcendentals=0),
        name="track",
    )(
        place,
        obs_value.reshape(1, TRACK),
        obs_weight,
        obs_tile.reshape(1, TRACK),
        obs_time.reshape(1, TRACK),
        obs_row.reshape(1, TRACK),
        obs_col.reshape(1, TRACK),
        mid,
    )
    gathered = lax.all_to_all(
        track.reshape(lat_count, 8, TRACK), "lat", split_axis=0, concat_axis=0, tiled=True
    ).reshape(lat_count * 8, TRACK)
    far = swap(lat_far, "lat", 1, lat_count, False)
    near = swap(lat_near, "lat", 0, lat_count, False)
    w_gate, w_in, w_out, w_inc = pl.pallas_call(
        prepare_kernel,
        out_shape=(
            jax.ShapeDtypeStruct((4 * HID, 768), BF16),
            jax.ShapeDtypeStruct((HID, LANES), BF16),
            jax.ShapeDtypeStruct((80, HID), BF16),
            jax.ShapeDtypeStruct((16, HID), BF16),
        ),
        in_specs=[vmem] * 6,
        out_specs=(vmem,) * 4,
        compiler_params=pltpu.CompilerParams(vmem_limit_bytes=16 * 1024 * 1024),
        cost_estimate=pl.CostEstimate(flops=2_000_000, bytes_accessed=1_500_000, transcendentals=0),
        name="prepare",
    )(
        jnp.transpose(lstm_weight, (0, 2, 1)),
        lstm_bias.reshape(1, 4 * HID),
        jnp.transpose(prior_in, (0, 2, 1)),
        prior_bias.reshape(1, HID),
        prior_out,
        lstm_out,
    )
    width = TILES * LANES
    main_width = STRIP * LANES

    def first(*refs):
        first_kernel(*refs, lat_count=lat_count)

    started = pl.pallas_call(
        first,
        out_shape=jax.ShapeDtypeStruct((24, 8, LANES), F32),
        in_specs=[smem] + [vmem] * 5,
        out_specs=vmem,
        scratch_shapes=[
            pltpu.VMEM((8, main_width), F32),
            pltpu.VMEM((8, main_width), F32),
            pltpu.VMEM((8, main_width), F32),
            pltpu.VMEM((80, main_width), BF16),
            pltpu.VMEM((80, main_width), F32),
        ],
        compiler_params=pltpu.CompilerParams(vmem_limit_bytes=16 * 1024 * 1024),
        cost_estimate=pl.CostEstimate(flops=2_000_000_000, bytes_accessed=500_000, transcendentals=0),
        name="first",
    )(place, mid, near, far, w_in, w_out)
    sums, adjoint, to_far, to_near = pl.pallas_call(
        build_kernel,
        out_shape=(
            jax.ShapeDtypeStruct((8, 256, LANES), F32),
            jax.ShapeDtypeStruct((24, 8, LANES), F32),
            jax.ShapeDtypeStruct((56, LANES), F32),
            jax.ShapeDtypeStruct((56, LANES), F32),
        ),
        in_specs=[smem, vmem, vmem, vmem, vmem],
        out_specs=(vmem, vmem, vmem, vmem),
        scratch_shapes=[
            pltpu.VMEM((2, 512, CHUNK), BF16),
            pltpu.VMEM((2, 640, CHUNK), BF16),
        ],
        compiler_params=pltpu.CompilerParams(vmem_limit_bytes=32 * 1024 * 1024),
        cost_estimate=pl.CostEstimate(flops=4_000_000_000, bytes_accessed=1_500_000, transcendentals=0),
        name="build",
    )(place, gathered, mid, near, far)

    from_far = swap(to_far, "lon", 1, lon_count, True)
    from_near = swap(to_near, "lon", 0, lon_count, True)

    def solve(*refs):
        solve_kernel(*refs, lat_count=lat_count)

    estimate, cell_state = pl.pallas_call(
        solve,
        out_shape=(
            jax.ShapeDtypeStruct((DAYS * ROWS, LANES), F32),
            jax.ShapeDtypeStruct((HID * ROWS, LANES), F32),
        ),
        in_specs=[smem] + [vmem] * 14,
        out_specs=(vmem, vmem),
        scratch_shapes=[
            pltpu.VMEM((8, width), F32),
            pltpu.VMEM((8, width), F32),
            pltpu.VMEM((8, width), F32),
            pltpu.VMEM((8, width), F32),
            pltpu.VMEM((8, width), F32),
            pltpu.VMEM((80, width), BF16),
            pltpu.VMEM((80, width), F32),
            pltpu.VMEM((HID, width), F32),
            pltpu.VMEM((HID, width), BF16),
            pltpu.VMEM((HID, width), BF16),
            pltpu.VMEM((HID, width), BF16),
        ],
        compiler_params=pltpu.CompilerParams(vmem_limit_bytes=32 * 1024 * 1024),
        name="solve",
    )(place, mid, near, far, sums, adjoint, started, to_far, to_near, from_far, from_near, w_in, w_out, w_gate, w_inc)
    return (
        estimate.reshape(DAYS, ROWS, LANES),
        cell_state.reshape(HID, ROWS, LANES),
    )


def solution(mesh):
    return jax.shard_map(
        on_device,
        mesh=mesh,
        in_specs=(
            P(None, "lat", "lon"),
            P(),
            P(),
            P(),
            P(),
            P(),
            P(),
            P(("lon", "lat")),
            P(None, ("lon", "lat")),
            P(("lon", "lat"), None),
            P(("lon", "lat")),
            P(("lon", "lat")),
            P(("lon", "lat")),
        ),
        out_specs=(P(None, "lat", "lon"), P(None, "lat", "lon")),
        check_vma=False,
    )
```

```python
import jax
import jax.numpy as jnp
from jax import lax
from jax.experimental import pallas as pl
from jax.experimental.pallas import tpu as pltpu
from jax.sharding import PartitionSpec as P

DAYS = 5
ROWS = 16
COLS = 128
LANES = 128
HID = 64
TRACK = 512
HALO = 8
BASES = 25
CHUNK = 2048
FIRST = 7
STRIP = 30
TILES = 37
GROUP = 4
F32 = jnp.float32
BF16 = jnp.bfloat16


def nt_dot(left, right):
    return lax.dot_general(left, right, (((1,), (1,)), ((), ())), preferred_element_type=F32)


def lane_roll(value, shift):
    return pltpu.roll(value, shift % value.shape[1], 1)


def strip_place(row):
    return (row + 6) // 4, (row + 6) % 4 * 32


def day_rows(near_ref, mid_ref, far_ref, even, row):
    if 0 <= row < ROWS:
        picked = mid_ref[pl.ds(row, DAYS, stride=ROWS), :]
    else:
        place = pl.ds(row + HALO if row < 0 else row - ROWS, DAYS, stride=HALO)
        near, far = near_ref[place, :], far_ref[place, :]
        picked = jnp.where(even, far, near) if row < 0 else jnp.where(even, near, far)
    return jnp.concatenate([picked, jnp.zeros((8 - DAYS, LANES), F32)], axis=0)


def adjoint_terms(sums_ref, base, here, above):
    low = pl.ds(5 * base, 8)
    high = pl.ds(LANES + 5 * base, 8)
    here_right = lane_roll(here, -1)
    above_right = lane_roll(above, -1)
    s01 = sums_ref[1, low, :]
    s02 = sums_ref[2, low, :]
    s03 = sums_ref[3, low, :]
    s12 = sums_ref[2, high, :]
    s13 = sums_ref[3, high, :]
    s23 = sums_ref[6, low, :]
    g0 = sums_ref[0, low, :] * here + s01 * here_right + s02 * above + s03 * above_right - sums_ref[4, low, :]
    g1 = s01 * here + sums_ref[1, high, :] * here_right + s12 * above + s13 * above_right - sums_ref[4, high, :]
    g2 = s02 * here + s12 * here_right + sums_ref[5, low, :] * above + s23 * above_right - sums_ref[7, low, :]
    g3 = s03 * here + s13 * here_right + s23 * above + sums_ref[6, high, :] * above_right - sums_ref[7, high, :]
    return g0 + lane_roll(g1, 1), g2 + lane_roll(g3, 1)


def track_kernel(
    value_ref, weight_ref, tile_ref, time_ref, row_ref, col_ref, state_ref, out_ref, to_near_ref, to_far_ref
):
    latitude = tile_ref[...] * ROWS + row_ref[...]
    keys = [time_ref[...].astype(F32), latitude.astype(F32), col_ref[...].astype(F32)]
    block = jnp.concatenate([value_ref[...], weight_ref[...]] + keys, axis=0)
    twice = jnp.concatenate([block, block], axis=0).astype(BF16)
    for k in range(out_ref.shape[0] // 16):
        out_ref[16 * k : 16 * k + 16, :] = twice
    even = lax.axis_index("lat") % 2 == 0
    for day in range(DAYS):
        lower = state_ref[ROWS * day : ROWS * day + HALO, :]
        upper = state_ref[ROWS * (day + 1) - HALO : ROWS * (day + 1), :]
        to_near_ref[HALO * day : HALO * day + HALO, :] = jnp.where(even, upper, lower)
        to_far_ref[HALO * day : HALO * day + HALO, :] = jnp.where(even, lower, upper)


def prepare_kernel(gate_ref, gate_bias_ref, in_ref, in_bias_ref, out_ref, inc_ref, w_gate_ref, w_in_ref, w_out_ref, w_inc_ref):
    def rows_of(ref, k):
        return jnp.concatenate([ref[k].astype(F32)[0:DAYS], jnp.zeros((8 - DAYS, ref.shape[2]), F32)], axis=0)

    def bias_rows(bias):
        high = bias.astype(BF16).astype(F32)
        middle = (bias - high).astype(BF16).astype(F32)
        low = bias - high - middle
        return jnp.concatenate([high, middle, low, jnp.zeros((5, bias.shape[1]), F32)], axis=0)

    pieces = [rows_of(gate_ref, k) for k in range(9)] + [bias_rows(gate_bias_ref[...])]
    pieces += [gate_ref[k].astype(F32)[DAYS:] for k in range(9)]
    whole = jnp.concatenate(pieces + [jnp.zeros((768 - 656, 4 * HID), F32)], axis=0)
    for k in range(6):
        block = whole[128 * k : 128 * k + 128]
        first = lane_roll(block[:, 0:128], HID) * 0.5
        second = block[:, 128:256]
        lane = lax.broadcasted_iota(jnp.int32, (128, 128), 1)
        second = jnp.where(lane < HID, 0.5 * second, second)
        w_gate_ref[0:128, 128 * k : 128 * k + 128] = first.T.astype(BF16)
        w_gate_ref[128:256, 128 * k : 128 * k + 128] = second.T.astype(BF16)
    narrow = jnp.concatenate([rows_of(in_ref, k) for k in range(9)] + [bias_rows(in_bias_ref[...])], axis=0)
    narrow = jnp.concatenate([narrow, jnp.zeros((48, HID), F32)], axis=0)
    narrow = jnp.concatenate([narrow, jnp.zeros((128, 128 - HID), F32)], axis=1)
    w_in_ref[...] = narrow.T[0:HID].astype(BF16)
    spread = [rows_of(out_ref, k) for k in range(9)]
    w_out_ref[...] = jnp.concatenate(spread + [jnp.zeros((8, HID), F32)], axis=0).astype(BF16)
    w_inc_ref[...] = jnp.concatenate(
        [inc_ref[...].astype(F32), jnp.zeros((16 - DAYS, HID), F32)], axis=0
    ).astype(BF16)


EAST_FIELDS = ((4, 1), (1, 0), (1, 1), (2, 1), (3, 1), (7, 1), (3, 0), (6, 0), (6, 1))
WEST_FIELDS = ((4, 0), (0, 0), (1, 0), (2, 0), (3, 0), (7, 0), (2, 1), (5, 0), (6, 0))
EAST_LANES = ((0, 1, 2, 3, 4), (5, 6, 4, 7, 8))
WEST_LANES = ((0, 1, 2, 3, 4), (5, 3, 6, 7, 8))


PRODUCTS = (
    ((0, 512), (384, 640), {(0, 0): (3, 1), (1, 0): (3, 0), (2, 0): (6, 0), (3, 0): (6, 1), (0, 1): (4, 1), (1, 1): (4, 0), (2, 1): (7, 0), (3, 1): (7, 1)}),
    ((0, 256), (128, 384), {(0, 0): (2, 1), (1, 0): (2, 0), (0, 1): (1, 1), (1, 1): (1, 0)}),
    ((128, 384), (0, 256), {(0, 0): (0, 0), (1, 1): (5, 0)}),
)
ROW_WEIGHTS = (1, 0, 2, 3)
COL_WEIGHTS = (0, 2, 1, 3, -1)


def sums_kernel(track_ref, sums_ref, rw_ref, cw_ref):
    base_row = (lax.axis_index("lat") * ROWS - 5).astype(F32)
    entry = lax.broadcasted_iota(jnp.int32, (LANES, TRACK), 0).astype(F32).astype(BF16)
    nothing = jnp.zeros((LANES, TRACK), BF16)

    def spread(row):
        part = jnp.broadcast_to(row, (16, TRACK)).astype(BF16)
        return jnp.concatenate([part] * 8, axis=0)

    per_chunk = CHUNK // TRACK
    chunks = track_ref.shape[0] * TRACK // (8 * CHUNK)
    for chunk in range(chunks):
        slot = chunk % 2
        for pair in range(per_chunk // 2):
            first_row = chunk * per_chunk * 8 + pair * 16
            both = track_ref[first_row : first_row + 16, :].astype(F32)
            for part in range(2):
                block = both[8 * part : 8 * part + 8]
                start = (2 * pair + part) * TRACK
                offset = block[6:7] - base_row
                within = (offset >= 0.0) & (offset < float(BASES))
                row_hit = entry == spread(jnp.where(within, offset * 5.0 + block[5:6], -1.0))
                col_hit = entry == spread(block[7:8])
                for source in range(5):
                    value = spread(block[source : source + 1])
                    if source > 0:
                        k = ROW_WEIGHTS.index(source - 1)
                        rw_ref[slot, 128 * k : 128 * k + 128, start : start + TRACK] = jnp.where(row_hit, value, nothing)
                    k = COL_WEIGHTS.index(source - 1)
                    cw_ref[slot, 128 * k : 128 * k + 128, start : start + TRACK] = jnp.where(col_hit, value, nothing)
        for (row0, row1), (col0, col1), blocks in PRODUCTS:
            product = nt_dot(rw_ref[slot, row0:row1, :], cw_ref[slot, col0:col1, :])
            for (i, j), (array, half) in blocks.items():
                total = product[128 * i : 128 * i + 128, 128 * j : 128 * j + 128]
                rows = slice(LANES * half, LANES * half + LANES)
                sums_ref[array, rows, :] = total if chunk == 0 else sums_ref[array, rows, :] + total


def edges_kernel(mid_ref, near_ref, far_ref, sums_ref, adjoint_ref, to_far_ref, to_near_ref):
    even_lat = lax.axis_index("lat") % 2 == 0
    even_lon = lax.axis_index("lon") % 2 == 0
    lane = lax.broadcasted_iota(jnp.int32, (8, LANES), 1)
    zero = jnp.zeros((8, LANES), F32)
    east, west = zero, zero
    carried = zero
    for row in range(-6, ROWS + 6):
        part, place = strip_place(row)
        here = day_rows(near_ref, mid_ref, far_ref, even_lat, row)
        picked = lane // 8 == place // 8
        east = jnp.where(picked, lane_roll(here, place - 120), east)
        west = jnp.where(picked, lane_roll(here, place), west)
        if -5 <= row <= 19:
            above = day_rows(near_ref, mid_ref, far_ref, even_lat, row + 1)
            now, later = adjoint_terms(sums_ref, row + 5, here, above)
            if row > -5:
                total = carried + now
                adjoint_ref[row + 4] = total
                picked = lane // 8 == place // 8 + 1
                east = jnp.where(picked, lane_roll(total, place + 8 - 120), east)
                west = jnp.where(picked, lane_roll(total, place + 8), west)
            carried = later
        if -2 <= row <= ROWS:
            for k in range(9):
                target = place + 16 + k
                array, half = EAST_FIELDS[k]
                piece = sums_ref[array, pl.ds(LANES * half + 5 * (row + 5), 8), :]
                east = jnp.where(lane == target, lane_roll(piece, target - (COLS - 2)), east)
                array, half = WEST_FIELDS[k]
                piece = sums_ref[array, pl.ds(LANES * half + 5 * (row + 5), 8), :]
                west = jnp.where(lane == target, lane_roll(piece, target), west)
        if place == 96:
            to_near_ref[8 * part : 8 * part + 8, :] = jnp.where(even_lon, east, west)
            to_far_ref[8 * part : 8 * part + 8, :] = jnp.where(even_lon, west, east)
            east, west = zero, zero


def row_mask(lat_count, row):
    row = row + lax.axis_index("lat") * ROWS
    return (row >= 0) & (row < lat_count * ROWS)


def tile(index, count=1):
    return slice(index * LANES, (index + count) * LANES)


def at(row):
    return tile(row + FIRST)


def ones_rows():
    return jnp.where(lax.broadcasted_iota(jnp.int32, (8, LANES), 0) < 3, 1.0, 0.0).astype(F32)


def spread_terms(spread_ref, row):
    columns = []
    for b in range(3):
        terms = [spread_ref[8 * (3 * a + b) : 8 * (3 * a + b) + 8, at(row + a - 1)] for a in range(3)]
        columns.append(terms[0] + terms[1] + terms[2])
    return columns


def first_kernel(
    mid_ref, near_ref, far_ref, w_in_ref, w_out_ref, out_ref, est_ref, minus_ref, plus_ref, window_ref, spread_ref, *, lat_count
):
    even_lat = lax.axis_index("lat") % 2 == 0
    for row in range(-6, 22):
        value = day_rows(near_ref, mid_ref, far_ref, even_lat, row)
        est_ref[:, at(row)] = value
        minus_ref[:, at(row)] = lane_roll(value, 1)
        plus_ref[:, at(row)] = lane_roll(value, -1)
    ones = ones_rows()
    for row in range(-5, 21):
        pieces = [source[:, at(row + a)] for a in (-1, 0, 1) for source in (minus_ref, est_ref, plus_ref)]
        window_ref[:, at(row)] = jnp.concatenate(pieces + [ones], axis=0).astype(BF16)
    groups = [(-5, 5), (0, 4), (4, 4), (8, 4), (12, 4), (16, 5)]
    for row, count in groups:
        where = tile(row + FIRST, count)
        value = jnp.dot(w_in_ref[:, 0:80], window_ref[:, where], preferred_element_type=F32)
        value = jnp.maximum(value, 0.0)
        if row < 0 or row >= ROWS:
            flags = [
                jnp.where(row_mask(lat_count, row + k), jnp.ones((1, LANES), F32), 0.0) for k in range(count)
            ]
            value = value * jnp.concatenate(flags, axis=1)
        spread_ref[:, where] = jnp.dot(w_out_ref[...], value.astype(BF16), preferred_element_type=F32)
    for row in range(-4, 20):
        columns = spread_terms(spread_ref, row)
        term = columns[1] + lane_roll(columns[0], 1) + lane_roll(columns[2], -1)
        out_ref[row + 4] = est_ref[:, at(row)] - term


def solve_kernel(
    mid_ref,
    near_ref,
    far_ref,
    sums_ref,
    adjoint_ref,
    first_ref,
    own_far_ref,
    own_near_ref,
    from_far_ref,
    from_near_ref,
    w_in_ref,
    w_out_ref,
    w_gate_ref,
    w_inc_ref,
    est_out_ref,
    cell_out_ref,
    est_ref,
    grad_ref,
    minus_ref,
    plus_ref,
    mask_ref,
    window_ref,
    spread_ref,
    cell_ref,
    hidden_ref,
    hid_minus_ref,
    hid_plus_ref,
    *,
    lat_count,
):
    even_lat = lax.axis_index("lat") % 2 == 0
    even_lon = lax.axis_index("lon") % 2 == 0
    lane = lax.broadcasted_iota(jnp.int32, (8, LANES), 1)
    zero = jnp.zeros((8, LANES), F32)
    strips = slice(STRIP * LANES, TILES * LANES)
    strip_width = (TILES - STRIP) * LANES
    strip_lane = lax.broadcasted_iota(jnp.int32, (8, strip_width), 1)

    def within(row):
        return row_mask(lat_count, row)

    def left(main, strip, row):
        part, place = strip_place(row)
        edge = lane_roll(strip[:, tile(part)], -(place + 7))
        return jnp.where(lane[: main.shape[0]] == 0, edge, lane_roll(main, 1))

    def right(main, strip, row):
        part, place = strip_place(row)
        edge = lane_roll(strip[:, tile(part)], 127 - (place + 24))
        return jnp.where(lane[: main.shape[0]] == 127, edge, lane_roll(main, -1))

    est_ref[:, at(-7)] = zero
    est_ref[:, at(22)] = zero
    for row in range(-6, 22):
        est_ref[:, at(row)] = day_rows(near_ref, mid_ref, far_ref, even_lat, row)
    quarter = (lane % 32) // 8
    from_west, from_east, adjoint_strip = [], [], []
    for part in range(TILES - STRIP):
        rows = slice(8 * part, 8 * part + 8)
        own_east = jnp.where(even_lon, own_near_ref[rows, :], own_far_ref[rows, :])
        own_west = jnp.where(even_lon, own_far_ref[rows, :], own_near_ref[rows, :])
        west = jnp.where(even_lon, from_far_ref[rows, :], from_near_ref[rows, :])
        east = jnp.where(even_lon, from_near_ref[rows, :], from_far_ref[rows, :])
        from_west.append(west)
        from_east.append(east)

        def join(first, second, third, fourth):
            return jnp.where(
                quarter < 2, jnp.where(quarter == 0, first, second), jnp.where(quarter == 2, third, fourth)
            )

        est_ref[:, tile(STRIP + part)] = join(west, lane_roll(own_west, 8), lane_roll(own_east, 16), lane_roll(east, 24))
        adjoint_strip.append(join(lane_roll(west, -8), own_west, lane_roll(own_east, 8), lane_roll(east, 16)))
    from_west = jnp.concatenate(from_west, axis=1)
    from_east = jnp.concatenate(from_east, axis=1)
    adjoint_strip = jnp.concatenate(adjoint_strip, axis=1)
    for row in range(-7, 23):
        mask_ref[:, at(row)] = jnp.where(within(row), jnp.ones((8, LANES), F32), 0.0)
    mask_ref[:, strips] = jnp.where(within(strip_lane // 32 - 6), 1.0, 0.0)

    ones = ones_rows()

    def windows(ref, first_row, last_row, with_strips):
        strip = ref[:, strips]
        for row in range(first_row - 1, last_row + 2) if first_row <= last_row else ():
            main = ref[:, at(row)]
            minus_ref[:, at(row)] = left(main, strip, row)
            plus_ref[:, at(row)] = right(main, strip, row)
        for row in range(first_row, last_row + 1):
            pieces = [source[:, at(row + a)] for a in (-1, 0, 1) for source in (minus_ref, ref, plus_ref)]
            window_ref[:, at(row)] = jnp.concatenate(pieces + [ones], axis=0).astype(BF16)
        if with_strips:
            pieces = []
            shifts = (lane_roll(strip, 1), strip, lane_roll(strip, -1))
            for a in (-1, 0, 1):
                pieces += [lane_roll(value, -32 * a) if a else value for value in shifts]
            pieces.append(jnp.concatenate([ones] * (TILES - STRIP), axis=1))
            window_ref[:, strips] = jnp.concatenate(pieces, axis=0).astype(BF16)

    def pieces_of(first_row, last_row):
        runs = [(first_row + FIRST, last_row + 1 + FIRST), (STRIP, TILES)]
        return [tile(t, min(GROUP, end - t)) for start, end in runs for t in range(start, end, GROUP)]

    def gradient(first_row, last_row, low, high):
        windows(est_ref, low, high, True)
        for where in pieces_of(low, high):
            value = jnp.dot(w_in_ref[:, 0:80], window_ref[:, where], preferred_element_type=F32)
            value = jnp.maximum(value, 0.0) * mask_ref[0:1, where]
            spread_ref[:, where] = jnp.dot(w_out_ref[...], value.astype(BF16), preferred_element_type=F32)
        totals = []
        for b in range(3):
            total = None
            for a in range(3):
                k = 8 * (3 * a + b)
                piece = spread_ref[k : k + 8, strips]
                piece = lane_roll(piece, 32 - 32 * a) if a != 1 else piece
                total = piece if total is None else total + piece
            totals.append(total)
        strip = est_ref[:, strips] - (totals[1] + lane_roll(totals[0], 1) + lane_roll(totals[2], -1))
        grad_ref[:, strips] = strip
        for row in range(first_row, last_row + 1):
            columns = spread_terms(spread_ref, row)
            term = columns[1] + left(columns[0], totals[0], row) + right(columns[2], totals[2], row)
            grad_ref[:, at(row)] = est_ref[:, at(row)] - term
        return strip

    strip = gradient(0, -1, 0, -1)
    for row in range(-4, 20):
        part, place = strip_place(row)
        edges = strip[:, tile(part)]
        total = jnp.where(
            lane < 2,
            lane_roll(edges, -(place + 8)),
            jnp.where(lane >= 126, lane_roll(edges, 126 - (place + 22)), first_ref[row + 4]),
        )
        total = total + adjoint_ref[row + 4]
        grad_ref[:, at(row)] = total if 0 <= row < ROWS else total * mask_ref[:, at(row)]
    grad_ref[:, strips] = (strip + adjoint_strip) * mask_ref[:, strips]
    windows(grad_ref, -3, 18, True)
    for where in pieces_of(-3, 18):
        sums = jnp.dot(w_gate_ref[HID:, 0:80], window_ref[:, where], preferred_element_type=F32)
        gate_in = 0.5 * jnp.tanh(sums[0:HID]) + 0.5
        gate_out = 0.5 * jnp.tanh(sums[HID : 2 * HID]) + 0.5
        cell = gate_in * jnp.tanh(sums[2 * HID : 3 * HID])
        hidden = (gate_out * jnp.tanh(cell) * mask_ref[0:1, where]).astype(BF16)
        cell_ref[:, where] = cell
        hidden_ref[:, where] = hidden
        update = jnp.dot(w_inc_ref[...], hidden, preferred_element_type=F32)
        est_ref[:, where] -= update[0:8]

    lane64 = lax.broadcasted_iota(jnp.int32, (HID, LANES), 1)
    for row in range(-1, ROWS + 1):
        part, place = strip_place(row)
        main = hidden_ref[:, at(row)].astype(F32)
        strip = hidden_ref[:, tile(STRIP + part)].astype(F32)
        hid_minus_ref[:, at(row)] = jnp.where(
            lane64 == 0, lane_roll(strip, -(place + 7)), lane_roll(main, 1)
        ).astype(BF16)
        hid_plus_ref[:, at(row)] = jnp.where(
            lane64 == 127, lane_roll(strip, 127 - (place + 24)), lane_roll(main, -1)
        ).astype(BF16)
    gradient(-1, 16, -2, 17)
    carried = zero
    for row in range(-2, ROWS + 1):
        now, later = adjoint_terms(sums_ref, row + 5, est_ref[:, at(row)], est_ref[:, at(row + 1)])
        if row > -2:
            total = grad_ref[:, at(row)] + carried + now
            grad_ref[:, at(row)] = total if 0 <= row < ROWS else total * mask_ref[:, at(row)]
        carried = later
    here = est_ref[:, strips]
    above = lane_roll(here, -32)

    def edge_term(source, lane_at, lanes, e0, e1, e2, e3):
        d, f0, f1, f2, f3 = [lane_roll(source, lane_at - (16 + k)) for k in lanes]
        return f0 * e0 + f1 * e1 + f2 * e2 + f3 * e3 - d

    west = (lane_roll(here, 1), here, lane_roll(above, 1), above)
    east = (here, lane_roll(here, -1), above, lane_roll(above, -1))
    extra_w = edge_term(from_west, 7, EAST_LANES[0], *west) + lane_roll(
        edge_term(from_west, 7, EAST_LANES[1], *west), 32
    )
    extra_e = edge_term(from_east, 24, WEST_LANES[0], *east) + lane_roll(
        edge_term(from_east, 24, WEST_LANES[1], *east), 32
    )
    grad_ref[:, strips] = (
        grad_ref[:, strips] + jnp.where(strip_lane % 32 < 16, extra_w, extra_e)
    ) * mask_ref[:, strips]
    windows(grad_ref, 0, ROWS - 1, False)
    for row in range(0, ROWS, 2):
        pieces = [window_ref[:, tile(row + FIRST, 2)]]
        for a in (-1, 0, 1):
            for source in (hid_minus_ref, hidden_ref, hid_plus_ref):
                pieces.append(source[:, tile(row + a + FIRST, 2)])
        sums = jnp.dot(w_gate_ref[:, 0:656], jnp.concatenate(pieces, axis=0), preferred_element_type=F32)
        old = cell_ref[:, tile(row + FIRST, 2)]
        forget = 0.5 * jnp.tanh(sums[0:HID]) + 0.5
        gate_in = 0.5 * jnp.tanh(sums[HID : 2 * HID]) + 0.5
        gate_out = 0.5 * jnp.tanh(sums[2 * HID : 3 * HID]) + 0.5
        cell = forget * old + gate_in * jnp.tanh(sums[3 * HID :])
        hidden = gate_out * jnp.tanh(cell)
        update = jnp.dot(w_inc_ref[...], hidden.astype(BF16), preferred_element_type=F32)
        for k in range(2):
            cell_out_ref[pl.ds(row + k, HID, stride=ROWS), :] = cell[:, tile(k)]
            final = est_ref[:, at(row + k)] - update[0:8, tile(k)]
            est_out_ref[pl.ds(row + k, DAYS, stride=ROWS), :] = final[0:DAYS]


def swap(value, axis, first, count, periodic):
    last = count if periodic else count - 1
    pairs = [(i, (i + 1) % count) for i in range(first, last, 2)]
    return lax.ppermute(value, axis, pairs + [(target, source) for source, target in pairs])


def on_device(
    state,
    prior_in,
    prior_bias,
    prior_out,
    lstm_weight,
    lstm_bias,
    lstm_out,
    obs_value,
    obs_weight,
    obs_tile,
    obs_time,
    obs_row,
    obs_col,
):
    lat_count = lax.axis_size("lat")
    lon_count = lax.axis_size("lon")
    mid = state.reshape(DAYS * ROWS, LANES)

    vmem = pl.BlockSpec(memory_space=pltpu.VMEM)
    track, lat_near, lat_far = pl.pallas_call(
        track_kernel,
        out_shape=(
            jax.ShapeDtypeStruct((lat_count * 8, TRACK), BF16),
            jax.ShapeDtypeStruct((DAYS * HALO, LANES), F32),
            jax.ShapeDtypeStruct((DAYS * HALO, LANES), F32),
        ),
        in_specs=[vmem] * 7,
        out_specs=(vmem, vmem, vmem),
        cost_estimate=pl.CostEstimate(flops=100_000, bytes_accessed=150_000, transcendentals=0),
        name="track",
    )(
        obs_value.reshape(1, TRACK),
        obs_weight,
        obs_tile.reshape(1, TRACK),
        obs_time.reshape(1, TRACK),
        obs_row.reshape(1, TRACK),
        obs_col.reshape(1, TRACK),
        mid,
    )
    gathered = lax.all_to_all(
        track.reshape(lat_count, 8, TRACK), "lat", split_axis=0, concat_axis=0, tiled=True
    ).reshape(lat_count * 8, TRACK)
    far = swap(lat_far, "lat", 1, lat_count, False)
    near = swap(lat_near, "lat", 0, lat_count, False)
    w_gate, w_in, w_out, w_inc = pl.pallas_call(
        prepare_kernel,
        out_shape=(
            jax.ShapeDtypeStruct((4 * HID, 768), BF16),
            jax.ShapeDtypeStruct((HID, LANES), BF16),
            jax.ShapeDtypeStruct((80, HID), BF16),
            jax.ShapeDtypeStruct((16, HID), BF16),
        ),
        in_specs=[vmem] * 6,
        out_specs=(vmem,) * 4,
        compiler_params=pltpu.CompilerParams(vmem_limit_bytes=16 * 1024 * 1024),
        cost_estimate=pl.CostEstimate(flops=2_000_000, bytes_accessed=1_500_000, transcendentals=0),
        name="prepare",
    )(
        jnp.transpose(lstm_weight, (0, 2, 1)),
        lstm_bias.reshape(1, 4 * HID),
        jnp.transpose(prior_in, (0, 2, 1)),
        prior_bias.reshape(1, HID),
        prior_out,
        lstm_out,
    )
    width = TILES * LANES
    main_width = STRIP * LANES

    def first(*refs):
        first_kernel(*refs, lat_count=lat_count)

    started = pl.pallas_call(
        first,
        out_shape=jax.ShapeDtypeStruct((24, 8, LANES), F32),
        in_specs=[vmem] * 5,
        out_specs=vmem,
        scratch_shapes=[
            pltpu.VMEM((8, main_width), F32),
            pltpu.VMEM((8, main_width), F32),
            pltpu.VMEM((8, main_width), F32),
            pltpu.VMEM((80, main_width), BF16),
            pltpu.VMEM((80, main_width), F32),
        ],
        compiler_params=pltpu.CompilerParams(vmem_limit_bytes=16 * 1024 * 1024),
        cost_estimate=pl.CostEstimate(flops=2_000_000_000, bytes_accessed=500_000, transcendentals=0),
        name="first",
    )(mid, near, far, w_in, w_out)
    sums = pl.pallas_call(
        sums_kernel,
        out_shape=jax.ShapeDtypeStruct((8, 256, LANES), F32),
        in_specs=[vmem],
        out_specs=vmem,
        scratch_shapes=[
            pltpu.VMEM((2, 512, CHUNK), BF16),
            pltpu.VMEM((2, 640, CHUNK), BF16),
        ],
        compiler_params=pltpu.CompilerParams(vmem_limit_bytes=32 * 1024 * 1024),
        cost_estimate=pl.CostEstimate(flops=4_000_000_000, bytes_accessed=1_500_000, transcendentals=0),
        name="sums",
    )(gathered)
    adjoint, to_far, to_near = pl.pallas_call(
        edges_kernel,
        out_shape=(
            jax.ShapeDtypeStruct((24, 8, LANES), F32),
            jax.ShapeDtypeStruct((56, LANES), F32),
            jax.ShapeDtypeStruct((56, LANES), F32),
        ),
        in_specs=[vmem] * 4,
        out_specs=(vmem, vmem, vmem),
        compiler_params=pltpu.CompilerParams(vmem_limit_bytes=16 * 1024 * 1024),
        cost_estimate=pl.CostEstimate(flops=1_000_000, bytes_accessed=1_500_000, transcendentals=0),
        name="edges",
    )(mid, near, far, sums)

    from_far = swap(to_far, "lon", 1, lon_count, True)
    from_near = swap(to_near, "lon", 0, lon_count, True)

    def solve(*refs):
        solve_kernel(*refs, lat_count=lat_count)

    estimate, cell_state = pl.pallas_call(
        solve,
        out_shape=(
            jax.ShapeDtypeStruct((DAYS * ROWS, LANES), F32),
            jax.ShapeDtypeStruct((HID * ROWS, LANES), F32),
        ),
        in_specs=[vmem] * 14,
        out_specs=(vmem, vmem),
        scratch_shapes=[
            pltpu.VMEM((8, width), F32),
            pltpu.VMEM((8, width), F32),
            pltpu.VMEM((8, width), F32),
            pltpu.VMEM((8, width), F32),
            pltpu.VMEM((8, width), F32),
            pltpu.VMEM((80, width), BF16),
            pltpu.VMEM((80, width), F32),
            pltpu.VMEM((HID, width), F32),
            pltpu.VMEM((HID, width), BF16),
            pltpu.VMEM((HID, width), BF16),
            pltpu.VMEM((HID, width), BF16),
        ],
        compiler_params=pltpu.CompilerParams(vmem_limit_bytes=32 * 1024 * 1024),
        name="solve",
    )(mid, near, far, sums, adjoint, started, to_far, to_near, from_far, from_near, w_in, w_out, w_gate, w_inc)
    return (
        estimate.reshape(DAYS, ROWS, LANES),
        cell_state.reshape(HID, ROWS, LANES),
    )


def solution(mesh):
    return jax.shard_map(
        on_device,
        mesh=mesh,
        in_specs=(
            P(None, "lat", "lon"),
            P(),
            P(),
            P(),
            P(),
            P(),
            P(),
            P(("lon", "lat")),
            P(None, ("lon", "lat")),
            P(("lon", "lat"), None),
            P(("lon", "lat")),
            P(("lon", "lat")),
            P(("lon", "lat")),
        ),
        out_specs=(P(None, "lat", "lon"), P(None, "lat", "lon")),
        check_vma=False,
    )
```

```python
import jax
import jax.numpy as jnp
from jax import lax
from jax.experimental import pallas as pl
from jax.experimental.pallas import tpu as pltpu
from jax.sharding import PartitionSpec as P

DAYS = 5
ROWS = 16
COLS = 128
LANES = 128
HID = 64
TRACK = 512
SENT = 384
ALWAYS = 256
HALO = 8
BASES = 25
CHUNK = 2048
FIRST = 7
STRIP = 30
TILES = 37
GROUP = 4
F32 = jnp.float32
BF16 = jnp.bfloat16


def nt_dot(left, right):
    return lax.dot_general(left, right, (((1,), (1,)), ((), ())), preferred_element_type=F32)


def lane_roll(value, shift):
    return pltpu.roll(value, shift % value.shape[1], 1)


def strip_place(row):
    return (row + 6) // 4, (row + 6) % 4 * 32


def day_rows(near_ref, mid_ref, far_ref, even, row):
    if 0 <= row < ROWS:
        picked = mid_ref[pl.ds(row, DAYS, stride=ROWS), :]
    else:
        place = pl.ds(row + HALO if row < 0 else row - ROWS, DAYS, stride=HALO)
        near, far = near_ref[place, :], far_ref[place, :]
        picked = jnp.where(even, far, near) if row < 0 else jnp.where(even, near, far)
    return jnp.concatenate([picked, jnp.zeros((8 - DAYS, LANES), F32)], axis=0)


PLACES = {
    "00": (0, 0), "01": (1, 0), "02": (2, 0), "03": (3, 0), "d0": (4, 0), "11": (1, 1), "12": (2, 1), "13": (3, 1), "d1": (4, 1),
    "22": (5, 0), "23": (6, 0), "d2": (7, 0), "33": (6, 1), "d3": (7, 1),
}


def base_sums(sums_ref, row):
    first = 5 * (row + 5)
    return {name: sums_ref[array, pl.ds(LANES * half + first, 8), :] for name, (array, half) in PLACES.items()}


def adjoint_terms(s, here, above):
    here_right = lane_roll(here, -1)
    above_right = lane_roll(above, -1)
    g0 = s["00"] * here + s["01"] * here_right + s["02"] * above + s["03"] * above_right - s["d0"]
    g1 = s["01"] * here + s["11"] * here_right + s["12"] * above + s["13"] * above_right - s["d1"]
    g2 = s["02"] * here + s["12"] * here_right + s["22"] * above + s["23"] * above_right - s["d2"]
    g3 = s["03"] * here + s["13"] * here_right + s["23"] * above + s["33"] * above_right - s["d3"]
    return g0 + lane_roll(g1, 1), g2 + lane_roll(g3, 1)


def edge_factors(now, before):
    east = (now["d1"] + before["d3"], now["11"] + before["33"], now["01"] + before["23"], now["13"], now["12"], now["03"])
    west = (now["d0"] + before["d2"], now["00"] + before["22"], now["01"] + before["23"], now["02"], now["03"], now["12"])
    return east, west


def track_kernel(
    value_ref, weight_ref, tile_ref, time_ref, row_ref, col_ref, state_ref, out_ref, to_near_ref, to_far_ref
):
    latitude = tile_ref[...] * ROWS + row_ref[...]
    keys = [time_ref[...].astype(F32), latitude.astype(F32), col_ref[...].astype(F32)]
    block = jnp.concatenate([value_ref[...], weight_ref[...]] + keys, axis=0)
    count = out_ref.shape[0] // 8
    number = lax.broadcasted_iota(jnp.int32, (1, TRACK), 1).astype(F32)
    key = block[6:7] * float(TRACK) + number
    key_down = jnp.broadcast_to(key, (LANES, TRACK)).T[:, 0:1]
    rank = jnp.sum(jnp.where(key_down < key, 1.0, 0.0), axis=0, keepdims=True)
    target = lax.broadcasted_iota(jnp.int32, (TRACK, TRACK), 0).astype(F32)
    chosen = jnp.where(target == rank, 1.0, 0.0).astype(BF16)
    ordered = nt_dot(jnp.concatenate([block, block], axis=0).astype(BF16), chosen)[0:8]
    for pair in range(count // 2):
        turned = []
        for k in (2 * pair, 2 * pair + 1):
            skipped = jnp.sum(jnp.where(block[6:7] < float(ROWS * k - 5), 1, 0))
            turned.append(pltpu.roll(ordered, jnp.where(skipped == 0, 0, TRACK - skipped), 1)[:, 0:SENT])
        out_ref[16 * pair : 16 * pair + 16, :] = jnp.concatenate(turned, axis=0).astype(BF16)
    even = lax.axis_index("lat") % 2 == 0
    for day in range(DAYS):
        lower = state_ref[ROWS * day : ROWS * day + HALO, :]
        upper = state_ref[ROWS * (day + 1) - HALO : ROWS * (day + 1), :]
        to_near_ref[HALO * day : HALO * day + HALO, :] = jnp.where(even, upper, lower)
        to_far_ref[HALO * day : HALO * day + HALO, :] = jnp.where(even, lower, upper)


def prepare_kernel(gate_ref, gate_bias_ref, in_ref, in_bias_ref, out_ref, inc_ref, w_gate_ref, w_in_ref, w_out_ref, w_inc_ref):
    def rows_of(ref, k):
        return jnp.concatenate([ref[k].astype(F32)[0:DAYS], jnp.zeros((8 - DAYS, ref.shape[2]), F32)], axis=0)

    def bias_rows(bias):
        high = bias.astype(BF16).astype(F32)
        middle = (bias - high).astype(BF16).astype(F32)
        low = bias - high - middle
        return jnp.concatenate([high, middle, low, jnp.zeros((5, bias.shape[1]), F32)], axis=0)

    pieces = [rows_of(gate_ref, k) for k in range(9)] + [bias_rows(gate_bias_ref[...])]
    pieces += [gate_ref[k].astype(F32)[DAYS:] for k in range(9)]
    whole = jnp.concatenate(pieces + [jnp.zeros((768 - 656, 4 * HID), F32)], axis=0)
    for k in range(6):
        block = whole[128 * k : 128 * k + 128]
        first = lane_roll(block[:, 0:128], HID) * 0.5
        second = block[:, 128:256]
        lane = lax.broadcasted_iota(jnp.int32, (128, 128), 1)
        second = jnp.where(lane < HID, 0.5 * second, second)
        w_gate_ref[0:128, 128 * k : 128 * k + 128] = first.T.astype(BF16)
        w_gate_ref[128:256, 128 * k : 128 * k + 128] = second.T.astype(BF16)
    narrow = jnp.concatenate([rows_of(in_ref, k) for k in range(9)] + [bias_rows(in_bias_ref[...])], axis=0)
    narrow = jnp.concatenate([narrow, jnp.zeros((48, HID), F32)], axis=0)
    narrow = jnp.concatenate([narrow, jnp.zeros((128, 128 - HID), F32)], axis=1)
    w_in_ref[...] = narrow.T[0:HID].astype(BF16)
    spread = [rows_of(out_ref, k) for k in range(9)]
    w_out_ref[...] = jnp.concatenate(spread + [jnp.zeros((8, HID), F32)], axis=0).astype(BF16)
    w_inc_ref[...] = jnp.concatenate(
        [inc_ref[...].astype(F32), jnp.zeros((16 - DAYS, HID), F32)], axis=0
    ).astype(BF16)


PRODUCTS = (
    ((0, 512), (384, 640), {(0, 0): (3, 1), (1, 0): (3, 0), (2, 0): (6, 0), (3, 0): (6, 1), (0, 1): (4, 1), (1, 1): (4, 0), (2, 1): (7, 0), (3, 1): (7, 1)}),
    ((0, 256), (128, 384), {(0, 0): (2, 1), (1, 0): (2, 0), (0, 1): (1, 1), (1, 1): (1, 0)}),
    ((128, 384), (0, 256), {(0, 0): (0, 0), (1, 1): (5, 0)}),
)
ROW_WEIGHTS = (1, 0, 2, 3)
COL_WEIGHTS = (0, 2, 1, 3, -1)


def sums_kernel(track_ref, sums_ref, rw_ref, cw_ref):
    base_row = (lax.axis_index("lat") * ROWS - 5).astype(F32)

    def accumulate(chunk, lanes, sources, fresh):
        slot = chunk % 2
        width = lanes.stop - lanes.start
        filled = 2 * len(sources) * width
        entry = lax.broadcasted_iota(jnp.int32, (LANES, width), 0).astype(F32).astype(BF16)
        nothing = jnp.zeros((LANES, width), BF16)

        def spread(row):
            part = jnp.broadcast_to(row, (16, width)).astype(BF16)
            return jnp.concatenate([part] * 8, axis=0)

        for index, pair in enumerate(sources):
            both = track_ref[16 * pair : 16 * pair + 16, lanes].astype(F32)
            for part in range(2):
                block = both[8 * part : 8 * part + 8]
                start = (2 * index + part) * width
                offset = block[6:7] - base_row
                within = (offset >= 0.0) & (offset < float(BASES))
                row_hit = entry == spread(jnp.where(within, offset * 5.0 + block[5:6], -1.0))
                col_hit = entry == spread(block[7:8])
                for source in range(5):
                    value = spread(block[source : source + 1])
                    if source > 0:
                        k = ROW_WEIGHTS.index(source - 1)
                        rw_ref[slot, 128 * k : 128 * k + 128, start : start + width] = jnp.where(row_hit, value, nothing)
                    k = COL_WEIGHTS.index(source - 1)
                    cw_ref[slot, 128 * k : 128 * k + 128, start : start + width] = jnp.where(col_hit, value, nothing)
        for (row0, row1), (col0, col1), blocks in PRODUCTS:
            product = nt_dot(rw_ref[slot, row0:row1, 0:filled], cw_ref[slot, col0:col1, 0:filled])
            for (i, j), (array, half) in blocks.items():
                total = product[128 * i : 128 * i + 128, 128 * j : 128 * j + 128]
                rows = slice(LANES * half, LANES * half + LANES)
                sums_ref[array, rows, :] = total if fresh else sums_ref[array, rows, :] + total

    pairs = track_ref.shape[0] // 16
    size = CHUNK // (2 * ALWAYS)
    for chunk, first in enumerate(range(0, pairs, size)):
        accumulate(chunk, slice(0, ALWAYS), range(first, min(first + size, pairs)), chunk == 0)
    rest = track_ref[:, ALWAYS:SENT].astype(F32) - base_row
    row_kind = lax.broadcasted_iota(jnp.int32, rest.shape, 0) % 8
    needed = jnp.max(jnp.where((row_kind == 6) & (rest >= 0.0) & (rest < float(BASES)), 1.0, 0.0))

    @pl.when(needed > 0.0)
    def _():
        for first in range(0, pairs, 2 * size):
            accumulate(0, slice(ALWAYS, SENT), range(first, min(first + 2 * size, pairs)), False)


def edges_kernel(mid_ref, near_ref, far_ref, sums_ref, adjoint_ref, to_far_ref, to_near_ref):
    even_lat = lax.axis_index("lat") % 2 == 0
    even_lon = lax.axis_index("lon") % 2 == 0
    lane = lax.broadcasted_iota(jnp.int32, (8, LANES), 1)
    zero = jnp.zeros((8, LANES), F32)
    east, west = zero, zero
    carried = zero
    for row in range(-6, ROWS + 6):
        part, place = strip_place(row)
        here = day_rows(near_ref, mid_ref, far_ref, even_lat, row)
        picked = lane // 8 == place // 8
        east = jnp.where(picked, lane_roll(here, place - 120), east)
        west = jnp.where(picked, lane_roll(here, place), west)
        if -5 <= row <= 19:
            above = day_rows(near_ref, mid_ref, far_ref, even_lat, row + 1)
            sums = base_sums(sums_ref, row)
            now, later = adjoint_terms(sums, here, above)
            if row > -5:
                total = carried + now
                adjoint_ref[row + 4] = total
                picked = lane // 8 == place // 8 + 1
                east = jnp.where(picked, lane_roll(total, place + 8 - 120), east)
                west = jnp.where(picked, lane_roll(total, place + 8), west)
            if -2 <= row <= ROWS:
                for k, (last, first) in enumerate(zip(*edge_factors(sums, before))):
                    target = place + 16 + k
                    east = jnp.where(lane == target, lane_roll(last, target - (COLS - 2)), east)
                    west = jnp.where(lane == target, lane_roll(first, target), west)
            carried = later
            before = sums
        if place == 96:
            to_near_ref[8 * part : 8 * part + 8, :] = jnp.where(even_lon, east, west)
            to_far_ref[8 * part : 8 * part + 8, :] = jnp.where(even_lon, west, east)
            east, west = zero, zero


def row_mask(lat_count, row):
    row = row + lax.axis_index("lat") * ROWS
    return (row >= 0) & (row < lat_count * ROWS)


def tile(index, count=1):
    return slice(index * LANES, (index + count) * LANES)


def at(row):
    return tile(row + FIRST)


def ones_rows():
    return jnp.where(lax.broadcasted_iota(jnp.int32, (8, LANES), 0) < 3, 1.0, 0.0).astype(F32)


def spread_terms(spread_ref, row):
    columns = []
    for b in range(3):
        terms = [spread_ref[8 * (3 * a + b) : 8 * (3 * a + b) + 8, at(row + a - 1)] for a in range(3)]
        columns.append(terms[0] + terms[1] + terms[2])
    return columns


def first_kernel(
    mid_ref, near_ref, far_ref, w_in_ref, w_out_ref, out_ref, est_ref, minus_ref, plus_ref, window_ref, spread_ref, *, lat_count
):
    even_lat = lax.axis_index("lat") % 2 == 0
    for row in range(-6, 22):
        value = day_rows(near_ref, mid_ref, far_ref, even_lat, row)
        est_ref[:, at(row)] = value
        minus_ref[:, at(row)] = lane_roll(value, 1)
        plus_ref[:, at(row)] = lane_roll(value, -1)
    ones = ones_rows()
    for row in range(-5, 21):
        pieces = [source[:, at(row + a)] for a in (-1, 0, 1) for source in (minus_ref, est_ref, plus_ref)]
        window_ref[:, at(row)] = jnp.concatenate(pieces + [ones], axis=0).astype(BF16)
    groups = [(-5, 5), (0, 4), (4, 4), (8, 4), (12, 4), (16, 5)]
    for row, count in groups:
        where = tile(row + FIRST, count)
        value = jnp.dot(w_in_ref[:, 0:80], window_ref[:, where], preferred_element_type=F32)
        value = jnp.maximum(value, 0.0)
        if row < 0 or row >= ROWS:
            flags = [
                jnp.where(row_mask(lat_count, row + k), jnp.ones((1, LANES), F32), 0.0) for k in range(count)
            ]
            value = value * jnp.concatenate(flags, axis=1)
        spread_ref[:, where] = jnp.dot(w_out_ref[...], value.astype(BF16), preferred_element_type=F32)
    for row in range(-4, 20):
        columns = spread_terms(spread_ref, row)
        term = columns[1] + lane_roll(columns[0], 1) + lane_roll(columns[2], -1)
        out_ref[row + 4] = est_ref[:, at(row)] - term


def solve_kernel(
    mid_ref,
    near_ref,
    far_ref,
    sums_ref,
    adjoint_ref,
    first_ref,
    own_far_ref,
    own_near_ref,
    from_far_ref,
    from_near_ref,
    w_in_ref,
    w_out_ref,
    w_gate_ref,
    w_inc_ref,
    est_out_ref,
    cell_out_ref,
    est_ref,
    grad_ref,
    minus_ref,
    plus_ref,
    mask_ref,
    window_ref,
    spread_ref,
    cell_ref,
    hidden_ref,
    hid_minus_ref,
    hid_plus_ref,
    *,
    lat_count,
):
    even_lat = lax.axis_index("lat") % 2 == 0
    even_lon = lax.axis_index("lon") % 2 == 0
    lane = lax.broadcasted_iota(jnp.int32, (8, LANES), 1)
    zero = jnp.zeros((8, LANES), F32)
    strips = slice(STRIP * LANES, TILES * LANES)
    strip_width = (TILES - STRIP) * LANES
    strip_lane = lax.broadcasted_iota(jnp.int32, (8, strip_width), 1)

    def within(row):
        return row_mask(lat_count, row)

    def left(main, strip, row):
        part, place = strip_place(row)
        edge = lane_roll(strip[:, tile(part)], -(place + 7))
        return jnp.where(lane[: main.shape[0]] == 0, edge, lane_roll(main, 1))

    def right(main, strip, row):
        part, place = strip_place(row)
        edge = lane_roll(strip[:, tile(part)], 127 - (place + 24))
        return jnp.where(lane[: main.shape[0]] == 127, edge, lane_roll(main, -1))

    est_ref[:, at(-7)] = zero
    est_ref[:, at(22)] = zero
    for row in range(-6, 22):
        est_ref[:, at(row)] = day_rows(near_ref, mid_ref, far_ref, even_lat, row)
    quarter = (lane % 32) // 8
    from_west, from_east, adjoint_strip = [], [], []
    for part in range(TILES - STRIP):
        rows = slice(8 * part, 8 * part + 8)
        own_east = jnp.where(even_lon, own_near_ref[rows, :], own_far_ref[rows, :])
        own_west = jnp.where(even_lon, own_far_ref[rows, :], own_near_ref[rows, :])
        west = jnp.where(even_lon, from_far_ref[rows, :], from_near_ref[rows, :])
        east = jnp.where(even_lon, from_near_ref[rows, :], from_far_ref[rows, :])
        from_west.append(west)
        from_east.append(east)

        def join(first, second, third, fourth):
            return jnp.where(
                quarter < 2, jnp.where(quarter == 0, first, second), jnp.where(quarter == 2, third, fourth)
            )

        est_ref[:, tile(STRIP + part)] = join(west, lane_roll(own_west, 8), lane_roll(own_east, 16), lane_roll(east, 24))
        adjoint_strip.append(join(lane_roll(west, -8), own_west, lane_roll(own_east, 8), lane_roll(east, 16)))
    from_west = jnp.concatenate(from_west, axis=1)
    from_east = jnp.concatenate(from_east, axis=1)
    adjoint_strip = jnp.concatenate(adjoint_strip, axis=1)
    for row in range(-7, 23):
        mask_ref[:, at(row)] = jnp.where(within(row), jnp.ones((8, LANES), F32), 0.0)
    mask_ref[:, strips] = jnp.where(within(strip_lane // 32 - 6), 1.0, 0.0)

    ones = ones_rows()

    def windows(ref, first_row, last_row, with_strips):
        strip = ref[:, strips]
        for row in range(first_row - 1, last_row + 2) if first_row <= last_row else ():
            main = ref[:, at(row)]
            minus_ref[:, at(row)] = left(main, strip, row)
            plus_ref[:, at(row)] = right(main, strip, row)
        for row in range(first_row, last_row + 1):
            pieces = [source[:, at(row + a)] for a in (-1, 0, 1) for source in (minus_ref, ref, plus_ref)]
            window_ref[:, at(row)] = jnp.concatenate(pieces + [ones], axis=0).astype(BF16)
        if with_strips:
            pieces = []
            shifts = (lane_roll(strip, 1), strip, lane_roll(strip, -1))
            for a in (-1, 0, 1):
                pieces += [lane_roll(value, -32 * a) if a else value for value in shifts]
            pieces.append(jnp.concatenate([ones] * (TILES - STRIP), axis=1))
            window_ref[:, strips] = jnp.concatenate(pieces, axis=0).astype(BF16)

    def pieces_of(first_row, last_row):
        runs = [(first_row + FIRST, last_row + 1 + FIRST), (STRIP, TILES)]
        return [tile(t, min(GROUP, end - t)) for start, end in runs for t in range(start, end, GROUP)]

    def gradient(first_row, last_row, low, high):
        windows(est_ref, low, high, True)
        for where in pieces_of(low, high):
            value = jnp.dot(w_in_ref[:, 0:80], window_ref[:, where], preferred_element_type=F32)
            value = jnp.maximum(value, 0.0) * mask_ref[0:1, where]
            spread_ref[:, where] = jnp.dot(w_out_ref[...], value.astype(BF16), preferred_element_type=F32)
        totals = []
        for b in range(3):
            total = None
            for a in range(3):
                k = 8 * (3 * a + b)
                piece = spread_ref[k : k + 8, strips]
                piece = lane_roll(piece, 32 - 32 * a) if a != 1 else piece
                total = piece if total is None else total + piece
            totals.append(total)
        strip = est_ref[:, strips] - (totals[1] + lane_roll(totals[0], 1) + lane_roll(totals[2], -1))
        grad_ref[:, strips] = strip
        for row in range(first_row, last_row + 1):
            columns = spread_terms(spread_ref, row)
            term = columns[1] + left(columns[0], totals[0], row) + right(columns[2], totals[2], row)
            grad_ref[:, at(row)] = est_ref[:, at(row)] - term
        return strip

    strip = gradient(0, -1, 0, -1)
    for row in range(-4, 20):
        part, place = strip_place(row)
        edges = strip[:, tile(part)]
        total = jnp.where(
            lane < 2,
            lane_roll(edges, -(place + 8)),
            jnp.where(lane >= 126, lane_roll(edges, 126 - (place + 22)), first_ref[row + 4]),
        )
        total = total + adjoint_ref[row + 4]
        grad_ref[:, at(row)] = total if 0 <= row < ROWS else total * mask_ref[:, at(row)]
    grad_ref[:, strips] = (strip + adjoint_strip) * mask_ref[:, strips]
    windows(grad_ref, -3, 18, True)
    for where in pieces_of(-3, 18):
        sums = jnp.dot(w_gate_ref[HID:, 0:80], window_ref[:, where], preferred_element_type=F32)
        gate_in = 0.5 * jnp.tanh(sums[0:HID]) + 0.5
        gate_out = 0.5 * jnp.tanh(sums[HID : 2 * HID]) + 0.5
        cell = gate_in * jnp.tanh(sums[2 * HID : 3 * HID])
        hidden = (gate_out * jnp.tanh(cell) * mask_ref[0:1, where]).astype(BF16)
        cell_ref[:, where] = cell
        hidden_ref[:, where] = hidden
        update = jnp.dot(w_inc_ref[...], hidden, preferred_element_type=F32)
        est_ref[:, where] -= update[0:8]

    lane64 = lax.broadcasted_iota(jnp.int32, (HID, LANES), 1)
    for row in range(-1, ROWS + 1):
        part, place = strip_place(row)
        main = hidden_ref[:, at(row)]
        strip = hidden_ref[:, tile(STRIP + part)]
        hid_minus_ref[:, at(row)] = jnp.where(lane64 == 0, lane_roll(strip, -(place + 7)), lane_roll(main, 1))
        hid_plus_ref[:, at(row)] = jnp.where(lane64 == 127, lane_roll(strip, 127 - (place + 24)), lane_roll(main, -1))
    gradient(-1, 16, -2, 17)
    carried = zero
    for row in range(-2, ROWS + 1):
        now, later = adjoint_terms(base_sums(sums_ref, row), est_ref[:, at(row)], est_ref[:, at(row + 1)])
        if row > -2:
            total = grad_ref[:, at(row)] + carried + now
            grad_ref[:, at(row)] = total if 0 <= row < ROWS else total * mask_ref[:, at(row)]
        carried = later
    here = est_ref[:, strips]
    above = lane_roll(here, -32)

    def edge_term(source, lane_at, inner):
        constant, own, beside, up, up_beside, down_beside = [lane_roll(source, lane_at - (16 + k)) for k in range(6)]
        here_beside = lane_roll(here, inner)
        total = own * here + beside * here_beside + up * above + up_beside * lane_roll(above, inner) - constant
        return total + lane_roll(up * here + down_beside * here_beside, 32)

    extra_w = edge_term(from_west, 7, 1)
    extra_e = edge_term(from_east, 24, -1)
    grad_ref[:, strips] = (
        grad_ref[:, strips] + jnp.where(strip_lane % 32 < 16, extra_w, extra_e)
    ) * mask_ref[:, strips]
    windows(grad_ref, 0, ROWS - 1, False)
    for row in range(0, ROWS, 2):
        pieces = [window_ref[:, tile(row + FIRST, 2)]]
        for a in (-1, 0, 1):
            for source in (hid_minus_ref, hidden_ref, hid_plus_ref):
                pieces.append(source[:, tile(row + a + FIRST, 2)])
        sums = jnp.dot(w_gate_ref[:, 0:656], jnp.concatenate(pieces, axis=0), preferred_element_type=F32)
        old = cell_ref[:, tile(row + FIRST, 2)]
        forget = 0.5 * jnp.tanh(sums[0:HID]) + 0.5
        gate_in = 0.5 * jnp.tanh(sums[HID : 2 * HID]) + 0.5
        gate_out = 0.5 * jnp.tanh(sums[2 * HID : 3 * HID]) + 0.5
        cell = forget * old + gate_in * jnp.tanh(sums[3 * HID :])
        hidden = gate_out * jnp.tanh(cell)
        update = jnp.dot(w_inc_ref[...], hidden.astype(BF16), preferred_element_type=F32)
        for k in range(2):
            cell_out_ref[pl.ds(row + k, HID, stride=ROWS), :] = cell[:, tile(k)]
            final = est_ref[:, at(row + k)] - update[0:8, tile(k)]
            est_out_ref[pl.ds(row + k, DAYS, stride=ROWS), :] = final[0:DAYS]


def swap(value, axis, first, count, periodic):
    last = count if periodic else count - 1
    pairs = [(i, (i + 1) % count) for i in range(first, last, 2)]
    return lax.ppermute(value, axis, pairs + [(target, source) for source, target in pairs])


def on_device(
    state,
    prior_in,
    prior_bias,
    prior_out,
    lstm_weight,
    lstm_bias,
    lstm_out,
    obs_value,
    obs_weight,
    obs_tile,
    obs_time,
    obs_row,
    obs_col,
):
    lat_count = lax.axis_size("lat")
    lon_count = lax.axis_size("lon")
    mid = state.reshape(DAYS * ROWS, LANES)

    vmem = pl.BlockSpec(memory_space=pltpu.VMEM)
    track, lat_near, lat_far = pl.pallas_call(
        track_kernel,
        out_shape=(
            jax.ShapeDtypeStruct((lat_count * 8, SENT), BF16),
            jax.ShapeDtypeStruct((DAYS * HALO, LANES), F32),
            jax.ShapeDtypeStruct((DAYS * HALO, LANES), F32),
        ),
        in_specs=[vmem] * 7,
        out_specs=(vmem, vmem, vmem),
        compiler_params=pltpu.CompilerParams(vmem_limit_bytes=16 * 1024 * 1024),
        cost_estimate=pl.CostEstimate(flops=100_000, bytes_accessed=150_000, transcendentals=0),
        name="track",
    )(
        obs_value.reshape(1, TRACK),
        obs_weight,
        obs_tile.reshape(1, TRACK),
        obs_time.reshape(1, TRACK),
        obs_row.reshape(1, TRACK),
        obs_col.reshape(1, TRACK),
        mid,
    )
    gathered = lax.all_to_all(
        track.reshape(lat_count, 8, SENT), "lat", split_axis=0, concat_axis=0, tiled=True
    ).reshape(lat_count * 8, SENT)
    far = swap(lat_far, "lat", 1, lat_count, False)
    near = swap(lat_near, "lat", 0, lat_count, False)
    w_gate, w_in, w_out, w_inc = pl.pallas_call(
        prepare_kernel,
        out_shape=(
            jax.ShapeDtypeStruct((4 * HID, 768), BF16),
            jax.ShapeDtypeStruct((HID, LANES), BF16),
            jax.ShapeDtypeStruct((80, HID), BF16),
            jax.ShapeDtypeStruct((16, HID), BF16),
        ),
        in_specs=[vmem] * 6,
        out_specs=(vmem,) * 4,
        compiler_params=pltpu.CompilerParams(vmem_limit_bytes=16 * 1024 * 1024),
        cost_estimate=pl.CostEstimate(flops=2_000_000, bytes_accessed=1_500_000, transcendentals=0),
        name="prepare",
    )(
        jnp.transpose(lstm_weight, (0, 2, 1)),
        lstm_bias.reshape(1, 4 * HID),
        jnp.transpose(prior_in, (0, 2, 1)),
        prior_bias.reshape(1, HID),
        prior_out,
        lstm_out,
    )
    width = TILES * LANES
    main_width = STRIP * LANES

    def first(*refs):
        first_kernel(*refs, lat_count=lat_count)

    started = pl.pallas_call(
        first,
        out_shape=jax.ShapeDtypeStruct((24, 8, LANES), F32),
        in_specs=[vmem] * 5,
        out_specs=vmem,
        scratch_shapes=[
            pltpu.VMEM((8, main_width), F32),
            pltpu.VMEM((8, main_width), F32),
            pltpu.VMEM((8, main_width), F32),
            pltpu.VMEM((80, main_width), BF16),
            pltpu.VMEM((80, main_width), F32),
        ],
        compiler_params=pltpu.CompilerParams(vmem_limit_bytes=16 * 1024 * 1024),
        cost_estimate=pl.CostEstimate(flops=2_000_000_000, bytes_accessed=500_000, transcendentals=0),
        name="first",
    )(mid, near, far, w_in, w_out)
    sums = pl.pallas_call(
        sums_kernel,
        out_shape=jax.ShapeDtypeStruct((8, 256, LANES), F32),
        in_specs=[vmem],
        out_specs=vmem,
        scratch_shapes=[
            pltpu.VMEM((2, 512, CHUNK), BF16),
            pltpu.VMEM((2, 640, CHUNK), BF16),
        ],
        compiler_params=pltpu.CompilerParams(vmem_limit_bytes=32 * 1024 * 1024),
        cost_estimate=pl.CostEstimate(flops=4_000_000_000, bytes_accessed=1_500_000, transcendentals=0),
        name="sums",
    )(gathered)
    adjoint, to_far, to_near = pl.pallas_call(
        edges_kernel,
        out_shape=(
            jax.ShapeDtypeStruct((24, 8, LANES), F32),
            jax.ShapeDtypeStruct((56, LANES), F32),
            jax.ShapeDtypeStruct((56, LANES), F32),
        ),
        in_specs=[vmem] * 4,
        out_specs=(vmem, vmem, vmem),
        compiler_params=pltpu.CompilerParams(vmem_limit_bytes=16 * 1024 * 1024),
        cost_estimate=pl.CostEstimate(flops=1_000_000, bytes_accessed=1_500_000, transcendentals=0),
        name="edges",
    )(mid, near, far, sums)

    from_far = swap(to_far, "lon", 1, lon_count, True)
    from_near = swap(to_near, "lon", 0, lon_count, True)

    def solve(*refs):
        solve_kernel(*refs, lat_count=lat_count)

    estimate, cell_state = pl.pallas_call(
        solve,
        out_shape=(
            jax.ShapeDtypeStruct((DAYS * ROWS, LANES), F32),
            jax.ShapeDtypeStruct((HID * ROWS, LANES), F32),
        ),
        in_specs=[vmem] * 14,
        out_specs=(vmem, vmem),
        scratch_shapes=[
            pltpu.VMEM((8, width), F32),
            pltpu.VMEM((8, width), F32),
            pltpu.VMEM((8, width), F32),
            pltpu.VMEM((8, width), F32),
            pltpu.VMEM((8, width), F32),
            pltpu.VMEM((80, width), BF16),
            pltpu.VMEM((80, width), F32),
            pltpu.VMEM((HID, width), F32),
            pltpu.VMEM((HID, width), BF16),
            pltpu.VMEM((HID, width), BF16),
            pltpu.VMEM((HID, width), BF16),
        ],
        compiler_params=pltpu.CompilerParams(vmem_limit_bytes=32 * 1024 * 1024),
        name="solve",
    )(mid, near, far, sums, adjoint, started, to_far, to_near, from_far, from_near, w_in, w_out, w_gate, w_inc)
    return (
        estimate.reshape(DAYS, ROWS, LANES),
        cell_state.reshape(HID, ROWS, LANES),
    )


def solution(mesh):
    return jax.shard_map(
        on_device,
        mesh=mesh,
        in_specs=(
            P(None, "lat", "lon"),
            P(),
            P(),
            P(),
            P(),
            P(),
            P(),
            P(("lon", "lat")),
            P(None, ("lon", "lat")),
            P(("lon", "lat"), None),
            P(("lon", "lat")),
            P(("lon", "lat")),
            P(("lon", "lat")),
        ),
        out_specs=(P(None, "lat", "lon"), P(None, "lat", "lon")),
        check_vma=False,
    )
```

```python
import jax
import jax.numpy as jnp
from jax import lax
from jax.experimental import pallas as pl
from jax.experimental.pallas import tpu as pltpu
from jax.sharding import PartitionSpec as P

DAYS = 5
ROWS = 16
COLS = 128
LANES = 128
HID = 64
TRACK = 512
SENT = 384
ALWAYS = 256
HALO = 8
BASES = 25
CHUNK = 2048
FIRST = 7
STRIP = 30
TILES = 37
GROUP = 4
F32 = jnp.float32
BF16 = jnp.bfloat16


def nt_dot(left, right):
    return lax.dot_general(left, right, (((1,), (1,)), ((), ())), preferred_element_type=F32)


def lane_roll(value, shift):
    return pltpu.roll(value, shift % value.shape[1], 1)


def strip_place(row):
    return (row + 6) // 4, (row + 6) % 4 * 32


def day_rows(near_ref, mid_ref, far_ref, even, row):
    if 0 <= row < ROWS:
        picked = mid_ref[pl.ds(row, DAYS, stride=ROWS), :]
    else:
        place = pl.ds(row + HALO if row < 0 else row - ROWS, DAYS, stride=HALO)
        near, far = near_ref[place, :], far_ref[place, :]
        picked = jnp.where(even, far, near) if row < 0 else jnp.where(even, near, far)
    return jnp.concatenate([picked, jnp.zeros((8 - DAYS, LANES), F32)], axis=0)


PLACES = {
    "00": (0, 0), "01": (1, 0), "02": (2, 0), "03": (3, 0), "d0": (4, 0), "11": (1, 1), "12": (2, 1), "13": (3, 1), "d1": (4, 1),
    "22": (5, 0), "23": (6, 0), "d2": (7, 0), "33": (6, 1), "d3": (7, 1),
}


def base_sums(sums_ref, row):
    first = 5 * (row + 5) + jnp.minimum(lax.axis_index("lat"), 0)
    return {name: sums_ref[array, pl.ds(LANES * half + first, 8), :] for name, (array, half) in PLACES.items()}


def adjoint_terms(s, here, above):
    here_right = lane_roll(here, -1)
    above_right = lane_roll(above, -1)
    g0 = s["00"] * here + s["01"] * here_right + s["02"] * above + s["03"] * above_right - s["d0"]
    g1 = s["01"] * here + s["11"] * here_right + s["12"] * above + s["13"] * above_right - s["d1"]
    g2 = s["02"] * here + s["12"] * here_right + s["22"] * above + s["23"] * above_right - s["d2"]
    g3 = s["03"] * here + s["13"] * here_right + s["23"] * above + s["33"] * above_right - s["d3"]
    return g0 + lane_roll(g1, 1), g2 + lane_roll(g3, 1)


def edge_factors(now, before):
    east = (now["d1"] + before["d3"], now["11"] + before["33"], now["01"] + before["23"], now["13"], now["12"], now["03"])
    west = (now["d0"] + before["d2"], now["00"] + before["22"], now["01"] + before["23"], now["02"], now["03"], now["12"])
    return east, west


def track_kernel(
    value_ref, weight_ref, tile_ref, time_ref, row_ref, col_ref, state_ref, out_ref, to_near_ref, to_far_ref
):
    latitude = tile_ref[...] * ROWS + row_ref[...]
    keys = [time_ref[...].astype(F32), latitude.astype(F32), col_ref[...].astype(F32)]
    block = jnp.concatenate([value_ref[...], weight_ref[...]] + keys, axis=0)
    count = out_ref.shape[0] // 8
    number = lax.broadcasted_iota(jnp.int32, (1, TRACK), 1).astype(F32)
    key = block[6:7] * float(TRACK) + number
    key_down = jnp.broadcast_to(key, (LANES, TRACK)).T[:, 0:1]
    rank = jnp.sum(jnp.where(key_down < key, 1.0, 0.0), axis=0, keepdims=True)
    target = lax.broadcasted_iota(jnp.int32, (TRACK, TRACK), 0).astype(F32)
    chosen = jnp.where(target == rank, 1.0, 0.0).astype(BF16)
    ordered = nt_dot(jnp.concatenate([block, block], axis=0).astype(BF16), chosen)[0:8]
    for pair in range(count // 2):
        turned = []
        for k in (2 * pair, 2 * pair + 1):
            skipped = jnp.sum(jnp.where(block[6:7] < float(ROWS * k - 5), 1, 0))
            turned.append(pltpu.roll(ordered, jnp.where(skipped == 0, 0, TRACK - skipped), 1)[:, 0:SENT])
        out_ref[16 * pair : 16 * pair + 16, :] = jnp.concatenate(turned, axis=0).astype(BF16)
    even = lax.axis_index("lat") % 2 == 0
    for day in range(DAYS):
        lower = state_ref[ROWS * day : ROWS * day + HALO, :]
        upper = state_ref[ROWS * (day + 1) - HALO : ROWS * (day + 1), :]
        to_near_ref[HALO * day : HALO * day + HALO, :] = jnp.where(even, upper, lower)
        to_far_ref[HALO * day : HALO * day + HALO, :] = jnp.where(even, lower, upper)


def prepare_kernel(gate_ref, gate_bias_ref, in_ref, in_bias_ref, out_ref, inc_ref, w_gate_ref, w_in_ref, w_out_ref, w_inc_ref):
    def rows_of(ref, k):
        return jnp.concatenate([ref[k].astype(F32)[0:DAYS], jnp.zeros((8 - DAYS, ref.shape[2]), F32)], axis=0)

    def bias_rows(bias):
        high = bias.astype(BF16).astype(F32)
        middle = (bias - high).astype(BF16).astype(F32)
        low = bias - high - middle
        return jnp.concatenate([high, middle, low, jnp.zeros((5, bias.shape[1]), F32)], axis=0)

    pieces = [rows_of(gate_ref, k) for k in range(9)] + [bias_rows(gate_bias_ref[...])]
    pieces += [gate_ref[k].astype(F32)[DAYS:] for k in range(9)]
    whole = jnp.concatenate(pieces + [jnp.zeros((768 - 656, 4 * HID), F32)], axis=0)
    for k in range(6):
        block = whole[128 * k : 128 * k + 128]
        first = lane_roll(block[:, 0:128], HID) * 0.5
        second = block[:, 128:256]
        lane = lax.broadcasted_iota(jnp.int32, (128, 128), 1)
        second = jnp.where(lane < HID, 0.5 * second, second)
        w_gate_ref[0:128, 128 * k : 128 * k + 128] = first.T.astype(BF16)
        w_gate_ref[128:256, 128 * k : 128 * k + 128] = second.T.astype(BF16)
    narrow = jnp.concatenate([rows_of(in_ref, k) for k in range(9)] + [bias_rows(in_bias_ref[...])], axis=0)
    narrow = jnp.concatenate([narrow, jnp.zeros((48, HID), F32)], axis=0)
    narrow = jnp.concatenate([narrow, jnp.zeros((128, 128 - HID), F32)], axis=1)
    w_in_ref[...] = narrow.T[0:HID].astype(BF16)
    spread = [rows_of(out_ref, k) for k in range(9)]
    w_out_ref[...] = jnp.concatenate(spread + [jnp.zeros((8, HID), F32)], axis=0).astype(BF16)
    w_inc_ref[...] = jnp.concatenate(
        [inc_ref[...].astype(F32), jnp.zeros((16 - DAYS, HID), F32)], axis=0
    ).astype(BF16)


PRODUCTS = (
    ((0, 512), (384, 640), {(0, 0): (3, 1), (1, 0): (3, 0), (2, 0): (6, 0), (3, 0): (6, 1), (0, 1): (4, 1), (1, 1): (4, 0), (2, 1): (7, 0), (3, 1): (7, 1)}),
    ((0, 256), (128, 384), {(0, 0): (2, 1), (1, 0): (2, 0), (0, 1): (1, 1), (1, 1): (1, 0)}),
    ((128, 384), (0, 256), {(0, 0): (0, 0), (1, 1): (5, 0)}),
)
ROW_WEIGHTS = (1, 0, 2, 3)
COL_WEIGHTS = (0, 2, 1, 3, -1)


def sums_kernel(track_ref, sums_ref, rw_ref, cw_ref):
    base_row = (lax.axis_index("lat") * ROWS - 5).astype(F32)

    def accumulate(chunk, lanes, sources, fresh):
        slot = chunk % 2
        width = lanes.stop - lanes.start
        filled = 2 * len(sources) * width
        entry = lax.broadcasted_iota(jnp.int32, (LANES, width), 0).astype(F32).astype(BF16)
        nothing = jnp.zeros((LANES, width), BF16)

        def spread(row):
            part = jnp.broadcast_to(row, (16, width)).astype(BF16)
            return jnp.concatenate([part] * 8, axis=0)

        for index, pair in enumerate(sources):
            both = track_ref[16 * pair : 16 * pair + 16, lanes].astype(F32)
            for part in range(2):
                block = both[8 * part : 8 * part + 8]
                start = (2 * index + part) * width
                offset = block[6:7] - base_row
                within = (offset >= 0.0) & (offset < float(BASES))
                row_hit = entry == spread(jnp.where(within, offset * 5.0 + block[5:6], -1.0))
                col_hit = entry == spread(block[7:8])
                for source in range(5):
                    value = spread(block[source : source + 1])
                    if source > 0:
                        k = ROW_WEIGHTS.index(source - 1)
                        rw_ref[slot, 128 * k : 128 * k + 128, start : start + width] = jnp.where(row_hit, value, nothing)
                    k = COL_WEIGHTS.index(source - 1)
                    cw_ref[slot, 128 * k : 128 * k + 128, start : start + width] = jnp.where(col_hit, value, nothing)
        for (row0, row1), (col0, col1), blocks in PRODUCTS:
            product = nt_dot(rw_ref[slot, row0:row1, 0:filled], cw_ref[slot, col0:col1, 0:filled])
            for (i, j), (array, half) in blocks.items():
                total = product[128 * i : 128 * i + 128, 128 * j : 128 * j + 128]
                rows = slice(LANES * half, LANES * half + LANES)
                sums_ref[array, rows, :] = total if fresh else sums_ref[array, rows, :] + total

    pairs = track_ref.shape[0] // 16
    size = CHUNK // (2 * ALWAYS)
    for chunk, first in enumerate(range(0, pairs, size)):
        accumulate(chunk, slice(0, ALWAYS), range(first, min(first + size, pairs)), chunk == 0)
    rest = track_ref[:, ALWAYS:SENT].astype(F32) - base_row
    row_kind = lax.broadcasted_iota(jnp.int32, rest.shape, 0) % 8
    needed = jnp.max(jnp.where((row_kind == 6) & (rest >= 0.0) & (rest < float(BASES)), 1.0, 0.0))

    @pl.when(needed > 0.0)
    def _():
        for first in range(0, pairs, 2 * size):
            accumulate(0, slice(ALWAYS, SENT), range(first, min(first + 2 * size, pairs)), False)


def edges_kernel(mid_ref, near_ref, far_ref, sums_ref, adjoint_ref, to_far_ref, to_near_ref, field_ref):
    even_lat = lax.axis_index("lat") % 2 == 0
    even_lon = lax.axis_index("lon") % 2 == 0
    lane = lax.broadcasted_iota(jnp.int32, (8, LANES), 1)
    zero = jnp.zeros((8, LANES), F32)
    east, west = zero, zero
    carried = zero
    for row in range(-6, ROWS + 6):
        field_ref[row + 6] = day_rows(near_ref, mid_ref, far_ref, even_lat, row)
    for row in range(-6, ROWS + 6):
        part, place = strip_place(row)
        here = field_ref[row + 6]
        picked = lane // 8 == place // 8
        east = jnp.where(picked, lane_roll(here, place - 120), east)
        west = jnp.where(picked, lane_roll(here, place), west)
        if -5 <= row <= 19:
            above = field_ref[row + 7]
            sums = base_sums(sums_ref, row)
            now, later = adjoint_terms(sums, here, above)
            if row > -5:
                total = carried + now
                adjoint_ref[row + 4] = total
                picked = lane // 8 == place // 8 + 1
                east = jnp.where(picked, lane_roll(total, place + 8 - 120), east)
                west = jnp.where(picked, lane_roll(total, place + 8), west)
            if -2 <= row <= ROWS:
                for k, (last, first) in enumerate(zip(*edge_factors(sums, before))):
                    target = place + 16 + k
                    east = jnp.where(lane == target, lane_roll(last, target - (COLS - 2)), east)
                    west = jnp.where(lane == target, lane_roll(first, target), west)
            carried = later
            before = sums
        if place == 96:
            to_near_ref[8 * part : 8 * part + 8, :] = jnp.where(even_lon, east, west)
            to_far_ref[8 * part : 8 * part + 8, :] = jnp.where(even_lon, west, east)
            east, west = zero, zero


def row_mask(lat_count, row):
    row = row + lax.axis_index("lat") * ROWS
    return (row >= 0) & (row < lat_count * ROWS)


def tile(index, count=1):
    return slice(index * LANES, (index + count) * LANES)


def at(row):
    return tile(row + FIRST)


def ones_rows():
    return jnp.where(lax.broadcasted_iota(jnp.int32, (8, LANES), 0) < 3, 1.0, 0.0).astype(F32)


def spread_terms(spread_ref, row):
    columns = []
    for b in range(3):
        terms = [spread_ref[8 * (3 * a + b) : 8 * (3 * a + b) + 8, at(row + a - 1)] for a in range(3)]
        columns.append(terms[0] + terms[1] + terms[2])
    return columns


def first_kernel(
    field_ref, w_in_ref, w_out_ref, out_ref, est_ref, minus_ref, plus_ref, window_ref, spread_ref, *, lat_count
):
    for row in range(-6, 22):
        value = field_ref[row + 6]
        est_ref[:, at(row)] = value
        minus_ref[:, at(row)] = lane_roll(value, 1)
        plus_ref[:, at(row)] = lane_roll(value, -1)
    ones = ones_rows()
    for row in range(-5, 21):
        pieces = [source[:, at(row + a)] for a in (-1, 0, 1) for source in (minus_ref, est_ref, plus_ref)]
        window_ref[:, at(row)] = jnp.concatenate(pieces + [ones], axis=0).astype(BF16)
    groups = [(-5, 5), (0, 4), (4, 4), (8, 4), (12, 4), (16, 5)]
    for row, count in groups:
        where = tile(row + FIRST, count)
        value = jnp.dot(w_in_ref[:, 0:80], window_ref[:, where], preferred_element_type=F32)
        value = jnp.maximum(value, 0.0)
        if row < 0 or row >= ROWS:
            flags = [
                jnp.where(row_mask(lat_count, row + k), jnp.ones((1, LANES), F32), 0.0) for k in range(count)
            ]
            value = value * jnp.concatenate(flags, axis=1)
        spread_ref[:, where] = jnp.dot(w_out_ref[...], value.astype(BF16), preferred_element_type=F32)
    for row in range(-4, 20):
        columns = spread_terms(spread_ref, row)
        term = columns[1] + lane_roll(columns[0], 1) + lane_roll(columns[2], -1)
        out_ref[row + 4] = est_ref[:, at(row)] - term


def solve_kernel(
    field_ref,
    sums_ref,
    adjoint_ref,
    first_ref,
    own_far_ref,
    own_near_ref,
    from_far_ref,
    from_near_ref,
    w_in_ref,
    w_out_ref,
    w_gate_ref,
    w_inc_ref,
    est_out_ref,
    cell_out_ref,
    est_ref,
    grad_ref,
    minus_ref,
    plus_ref,
    mask_ref,
    window_ref,
    spread_ref,
    cell_ref,
    hidden_ref,
    hid_minus_ref,
    hid_plus_ref,
    *,
    lat_count,
):
    even_lon = lax.axis_index("lon") % 2 == 0
    lane = lax.broadcasted_iota(jnp.int32, (8, LANES), 1)
    zero = jnp.zeros((8, LANES), F32)
    strips = slice(STRIP * LANES, TILES * LANES)
    strip_width = (TILES - STRIP) * LANES
    strip_lane = lax.broadcasted_iota(jnp.int32, (8, strip_width), 1)

    def within(row):
        return row_mask(lat_count, row)

    def left(main, strip, row):
        part, place = strip_place(row)
        edge = lane_roll(strip[:, tile(part)], -(place + 7))
        return jnp.where(lane[: main.shape[0]] == 0, edge, lane_roll(main, 1))

    def right(main, strip, row):
        part, place = strip_place(row)
        edge = lane_roll(strip[:, tile(part)], 127 - (place + 24))
        return jnp.where(lane[: main.shape[0]] == 127, edge, lane_roll(main, -1))

    est_ref[:, at(-7)] = zero
    est_ref[:, at(22)] = zero
    for row in range(-6, 22):
        est_ref[:, at(row)] = field_ref[row + 6]
    quarter = (lane % 32) // 8
    from_west, from_east, adjoint_strip = [], [], []
    for part in range(TILES - STRIP):
        rows = slice(8 * part, 8 * part + 8)
        own_east = jnp.where(even_lon, own_near_ref[rows, :], own_far_ref[rows, :])
        own_west = jnp.where(even_lon, own_far_ref[rows, :], own_near_ref[rows, :])
        west = jnp.where(even_lon, from_far_ref[rows, :], from_near_ref[rows, :])
        east = jnp.where(even_lon, from_near_ref[rows, :], from_far_ref[rows, :])
        from_west.append(west)
        from_east.append(east)

        def join(first, second, third, fourth):
            return jnp.where(
                quarter < 2, jnp.where(quarter == 0, first, second), jnp.where(quarter == 2, third, fourth)
            )

        est_ref[:, tile(STRIP + part)] = join(west, lane_roll(own_west, 8), lane_roll(own_east, 16), lane_roll(east, 24))
        adjoint_strip.append(join(lane_roll(west, -8), own_west, lane_roll(own_east, 8), lane_roll(east, 16)))
    from_west = jnp.concatenate(from_west, axis=1)
    from_east = jnp.concatenate(from_east, axis=1)
    adjoint_strip = jnp.concatenate(adjoint_strip, axis=1)
    for row in range(-7, 23):
        mask_ref[:, at(row)] = jnp.where(within(row), jnp.ones((8, LANES), F32), 0.0)
    mask_ref[:, strips] = jnp.where(within(strip_lane // 32 - 6), 1.0, 0.0)

    ones = ones_rows()

    def windows(ref, first_row, last_row, with_strips):
        strip = ref[:, strips]
        for row in range(first_row - 1, last_row + 2) if first_row <= last_row else ():
            main = ref[:, at(row)]
            minus_ref[:, at(row)] = left(main, strip, row)
            plus_ref[:, at(row)] = right(main, strip, row)
        for row in range(first_row, last_row + 1):
            pieces = [source[:, at(row + a)] for a in (-1, 0, 1) for source in (minus_ref, ref, plus_ref)]
            window_ref[:, at(row)] = jnp.concatenate(pieces + [ones], axis=0).astype(BF16)
        if with_strips:
            pieces = []
            shifts = (lane_roll(strip, 1), strip, lane_roll(strip, -1))
            for a in (-1, 0, 1):
                pieces += [lane_roll(value, -32 * a) if a else value for value in shifts]
            pieces.append(jnp.concatenate([ones] * (TILES - STRIP), axis=1))
            window_ref[:, strips] = jnp.concatenate(pieces, axis=0).astype(BF16)

    def pieces_of(first_row, last_row):
        runs = [(first_row + FIRST, last_row + 1 + FIRST), (STRIP, TILES)]
        return [tile(t, min(GROUP, end - t)) for start, end in runs for t in range(start, end, GROUP)]

    def gradient(first_row, last_row, low, high):
        windows(est_ref, low, high, True)
        for where in pieces_of(low, high):
            value = jnp.dot(w_in_ref[:, 0:80], window_ref[:, where], preferred_element_type=F32)
            value = jnp.maximum(value, 0.0) * mask_ref[0:1, where]
            spread_ref[:, where] = jnp.dot(w_out_ref[...], value.astype(BF16), preferred_element_type=F32)
        totals = []
        for b in range(3):
            total = None
            for a in range(3):
                k = 8 * (3 * a + b)
                piece = spread_ref[k : k + 8, strips]
                piece = lane_roll(piece, 32 - 32 * a) if a != 1 else piece
                total = piece if total is None else total + piece
            totals.append(total)
        strip = est_ref[:, strips] - (totals[1] + lane_roll(totals[0], 1) + lane_roll(totals[2], -1))
        grad_ref[:, strips] = strip
        for row in range(first_row, last_row + 1):
            columns = spread_terms(spread_ref, row)
            term = columns[1] + left(columns[0], totals[0], row) + right(columns[2], totals[2], row)
            grad_ref[:, at(row)] = est_ref[:, at(row)] - term
        return strip

    strip = gradient(0, -1, 0, -1)
    for row in range(-4, 20):
        part, place = strip_place(row)
        edges = strip[:, tile(part)]
        total = jnp.where(
            lane < 2,
            lane_roll(edges, -(place + 8)),
            jnp.where(lane >= 126, lane_roll(edges, 126 - (place + 22)), first_ref[row + 4]),
        )
        total = total + adjoint_ref[row + 4]
        grad_ref[:, at(row)] = total if 0 <= row < ROWS else total * mask_ref[:, at(row)]
    grad_ref[:, strips] = (strip + adjoint_strip) * mask_ref[:, strips]
    windows(grad_ref, -3, 18, True)
    for where in pieces_of(-3, 18):
        sums = jnp.dot(w_gate_ref[HID:, 0:80], window_ref[:, where], preferred_element_type=F32)
        gate_in = 0.5 * jnp.tanh(sums[0:HID]) + 0.5
        gate_out = 0.5 * jnp.tanh(sums[HID : 2 * HID]) + 0.5
        cell = gate_in * jnp.tanh(sums[2 * HID : 3 * HID])
        hidden = (gate_out * jnp.tanh(cell) * mask_ref[0:1, where]).astype(BF16)
        cell_ref[:, where] = cell
        hidden_ref[:, where] = hidden
        update = jnp.dot(w_inc_ref[...], hidden, preferred_element_type=F32)
        est_ref[:, where] -= update[0:8]

    lane64 = lax.broadcasted_iota(jnp.int32, (HID, LANES), 1)
    for row in range(-1, ROWS + 1):
        part, place = strip_place(row)
        main = hidden_ref[:, at(row)]
        strip = hidden_ref[:, tile(STRIP + part)]
        hid_minus_ref[:, at(row)] = jnp.where(lane64 == 0, lane_roll(strip, -(place + 7)), lane_roll(main, 1))
        hid_plus_ref[:, at(row)] = jnp.where(lane64 == 127, lane_roll(strip, 127 - (place + 24)), lane_roll(main, -1))
    gradient(-1, 16, -2, 17)
    carried = zero
    for row in range(-2, ROWS + 1):
        now, later = adjoint_terms(base_sums(sums_ref, row), est_ref[:, at(row)], est_ref[:, at(row + 1)])
        if row > -2:
            total = grad_ref[:, at(row)] + carried + now
            grad_ref[:, at(row)] = total if 0 <= row < ROWS else total * mask_ref[:, at(row)]
        carried = later
    here = est_ref[:, strips]
    above = lane_roll(here, -32)

    def edge_term(source, lane_at, inner):
        constant, own, beside, up, up_beside, down_beside = [lane_roll(source, lane_at - (16 + k)) for k in range(6)]
        here_beside = lane_roll(here, inner)
        total = own * here + beside * here_beside + up * above + up_beside * lane_roll(above, inner) - constant
        return total + lane_roll(up * here + down_beside * here_beside, 32)

    extra_w = edge_term(from_west, 7, 1)
    extra_e = edge_term(from_east, 24, -1)
    grad_ref[:, strips] = (
        grad_ref[:, strips] + jnp.where(strip_lane % 32 < 16, extra_w, extra_e)
    ) * mask_ref[:, strips]
    windows(grad_ref, 0, ROWS - 1, False)
    for row in range(0, ROWS, 2):
        pieces = [window_ref[:, tile(row + FIRST, 2)]]
        for a in (-1, 0, 1):
            for source in (hid_minus_ref, hidden_ref, hid_plus_ref):
                pieces.append(source[:, tile(row + a + FIRST, 2)])
        sums = jnp.dot(w_gate_ref[:, 0:656], jnp.concatenate(pieces, axis=0), preferred_element_type=F32)
        old = cell_ref[:, tile(row + FIRST, 2)]
        forget = 0.5 * jnp.tanh(sums[0:HID]) + 0.5
        gate_in = 0.5 * jnp.tanh(sums[HID : 2 * HID]) + 0.5
        gate_out = 0.5 * jnp.tanh(sums[2 * HID : 3 * HID]) + 0.5
        cell = forget * old + gate_in * jnp.tanh(sums[3 * HID :])
        hidden = gate_out * jnp.tanh(cell)
        update = jnp.dot(w_inc_ref[...], hidden.astype(BF16), preferred_element_type=F32)
        for k in range(2):
            cell_out_ref[pl.ds(row + k, HID, stride=ROWS), :] = cell[:, tile(k)]
            final = est_ref[:, at(row + k)] - update[0:8, tile(k)]
            est_out_ref[pl.ds(row + k, DAYS, stride=ROWS), :] = final[0:DAYS]


def swap(value, axis, first, count, periodic):
    last = count if periodic else count - 1
    pairs = [(i, (i + 1) % count) for i in range(first, last, 2)]
    return lax.ppermute(value, axis, pairs + [(target, source) for source, target in pairs])


def on_device(
    state,
    prior_in,
    prior_bias,
    prior_out,
    lstm_weight,
    lstm_bias,
    lstm_out,
    obs_value,
    obs_weight,
    obs_tile,
    obs_time,
    obs_row,
    obs_col,
):
    lat_count = lax.axis_size("lat")
    lon_count = lax.axis_size("lon")
    mid = state.reshape(DAYS * ROWS, LANES)

    vmem = pl.BlockSpec(memory_space=pltpu.VMEM)
    track, lat_near, lat_far = pl.pallas_call(
        track_kernel,
        out_shape=(
            jax.ShapeDtypeStruct((lat_count * 8, SENT), BF16),
            jax.ShapeDtypeStruct((DAYS * HALO, LANES), F32),
            jax.ShapeDtypeStruct((DAYS * HALO, LANES), F32),
        ),
        in_specs=[vmem] * 7,
        out_specs=(vmem, vmem, vmem),
        cost_estimate=pl.CostEstimate(flops=100_000, bytes_accessed=150_000, transcendentals=0),
        name="track",
    )(
        obs_value.reshape(1, TRACK),
        obs_weight,
        obs_tile.reshape(1, TRACK),
        obs_time.reshape(1, TRACK),
        obs_row.reshape(1, TRACK),
        obs_col.reshape(1, TRACK),
        mid,
    )
    gathered = lax.all_to_all(
        track.reshape(lat_count, 8, SENT), "lat", split_axis=0, concat_axis=0, tiled=True
    ).reshape(lat_count * 8, SENT)
    far = swap(lat_far, "lat", 1, lat_count, False)
    near = swap(lat_near, "lat", 0, lat_count, False)
    w_gate, w_in, w_out, w_inc = pl.pallas_call(
        prepare_kernel,
        out_shape=(
            jax.ShapeDtypeStruct((4 * HID, 768), BF16),
            jax.ShapeDtypeStruct((HID, LANES), BF16),
            jax.ShapeDtypeStruct((80, HID), BF16),
            jax.ShapeDtypeStruct((16, HID), BF16),
        ),
        in_specs=[vmem] * 6,
        out_specs=(vmem,) * 4,
        cost_estimate=pl.CostEstimate(flops=2_000_000, bytes_accessed=1_500_000, transcendentals=0),
        name="prepare",
    )(
        jnp.transpose(lstm_weight, (0, 2, 1)),
        lstm_bias.reshape(1, 4 * HID),
        jnp.transpose(prior_in, (0, 2, 1)),
        prior_bias.reshape(1, HID),
        prior_out,
        lstm_out,
    )
    sums = pl.pallas_call(
        sums_kernel,
        out_shape=jax.ShapeDtypeStruct((8, 256, LANES), F32),
        in_specs=[vmem],
        out_specs=vmem,
        scratch_shapes=[
            pltpu.VMEM((2, 512, CHUNK), BF16),
            pltpu.VMEM((2, 640, CHUNK), BF16),
        ],
        compiler_params=pltpu.CompilerParams(vmem_limit_bytes=32 * 1024 * 1024),
        cost_estimate=pl.CostEstimate(flops=4_000_000_000, bytes_accessed=1_500_000, transcendentals=0),
        name="sums",
    )(gathered)
    adjoint, to_far, to_near, field = pl.pallas_call(
        edges_kernel,
        out_shape=(
            jax.ShapeDtypeStruct((24, 8, LANES), F32),
            jax.ShapeDtypeStruct((56, LANES), F32),
            jax.ShapeDtypeStruct((56, LANES), F32),
            jax.ShapeDtypeStruct((28, 8, LANES), F32),
        ),
        in_specs=[vmem] * 4,
        out_specs=(vmem, vmem, vmem, vmem),
        compiler_params=pltpu.CompilerParams(vmem_limit_bytes=16 * 1024 * 1024),
        cost_estimate=pl.CostEstimate(flops=1_000_000, bytes_accessed=1_500_000, transcendentals=0),
        name="edges",
    )(mid, near, far, sums)

    width = TILES * LANES
    main_width = STRIP * LANES

    def first(*refs):
        first_kernel(*refs, lat_count=lat_count)

    started = pl.pallas_call(
        first,
        out_shape=jax.ShapeDtypeStruct((24, 8, LANES), F32),
        in_specs=[vmem] * 3,
        out_specs=vmem,
        scratch_shapes=[
            pltpu.VMEM((8, main_width), F32),
            pltpu.VMEM((8, main_width), F32),
            pltpu.VMEM((8, main_width), F32),
            pltpu.VMEM((80, main_width), BF16),
            pltpu.VMEM((80, main_width), F32),
        ],
        compiler_params=pltpu.CompilerParams(vmem_limit_bytes=16 * 1024 * 1024),
        cost_estimate=pl.CostEstimate(flops=2_000_000_000, bytes_accessed=500_000, transcendentals=0),
        name="first",
    )(field, w_in, w_out)
    from_far = swap(to_far, "lon", 1, lon_count, True)
    from_near = swap(to_near, "lon", 0, lon_count, True)

    def solve(*refs):
        solve_kernel(*refs, lat_count=lat_count)

    estimate, cell_state = pl.pallas_call(
        solve,
        out_shape=(
            jax.ShapeDtypeStruct((DAYS * ROWS, LANES), F32),
            jax.ShapeDtypeStruct((HID * ROWS, LANES), F32),
        ),
        in_specs=[vmem] * 12,
        out_specs=(vmem, vmem),
        scratch_shapes=[
            pltpu.VMEM((8, width), F32),
            pltpu.VMEM((8, width), F32),
            pltpu.VMEM((8, width), F32),
            pltpu.VMEM((8, width), F32),
            pltpu.VMEM((8, width), F32),
            pltpu.VMEM((80, width), BF16),
            pltpu.VMEM((80, width), F32),
            pltpu.VMEM((HID, width), F32),
            pltpu.VMEM((HID, width), BF16),
            pltpu.VMEM((HID, width), BF16),
            pltpu.VMEM((HID, width), BF16),
        ],
        compiler_params=pltpu.CompilerParams(vmem_limit_bytes=32 * 1024 * 1024),
        name="solve",
    )(field, sums, adjoint, started, to_far, to_near, from_far, from_near, w_in, w_out, w_gate, w_inc)
    return (
        estimate.reshape(DAYS, ROWS, LANES),
        cell_state.reshape(HID, ROWS, LANES),
    )


def solution(mesh):
    return jax.shard_map(
        on_device,
        mesh=mesh,
        in_specs=(
            P(None, "lat", "lon"),
            P(),
            P(),
            P(),
            P(),
            P(),
            P(),
            P(("lon", "lat")),
            P(None, ("lon", "lat")),
            P(("lon", "lat"), None),
            P(("lon", "lat")),
            P(("lon", "lat")),
            P(("lon", "lat")),
        ),
        out_specs=(P(None, "lat", "lon"), P(None, "lat", "lon")),
        check_vma=False,
    )
```

```python
import jax
import jax.numpy as jnp
from jax import lax
from jax.experimental import pallas as pl
from jax.experimental.pallas import tpu as pltpu
from jax.sharding import PartitionSpec as P

DAYS = 5
ROWS = 16
COLS = 128
LANES = 128
HID = 64
TRACK = 512
SENT = 384
ALWAYS = 256
HALO = 8
BASES = 25
CHUNK = 2048
FIRST = 7
STRIP = 30
TILES = 37
GROUP = 4
F32 = jnp.float32
BF16 = jnp.bfloat16


def nt_dot(left, right):
    return lax.dot_general(left, right, (((1,), (1,)), ((), ())), preferred_element_type=F32)


def lane_roll(value, shift):
    return pltpu.roll(value, shift % value.shape[1], 1)


def strip_place(row):
    return (row + 6) // 4, (row + 6) % 4 * 32


def day_rows(near_ref, mid_ref, far_ref, even, row):
    if 0 <= row < ROWS:
        picked = mid_ref[pl.ds(row, DAYS, stride=ROWS), :]
    else:
        place = pl.ds(row + HALO if row < 0 else row - ROWS, DAYS, stride=HALO)
        near, far = near_ref[place, :], far_ref[place, :]
        picked = jnp.where(even, far, near) if row < 0 else jnp.where(even, near, far)
    return jnp.concatenate([picked, jnp.zeros((8 - DAYS, LANES), F32)], axis=0)


PLACES = {
    "00": (0, 0), "01": (1, 0), "02": (2, 0), "03": (3, 0), "d0": (4, 0), "11": (1, 1), "12": (2, 1), "13": (3, 1), "d1": (4, 1),
    "22": (5, 0), "23": (6, 0), "d2": (7, 0), "33": (6, 1), "d3": (7, 1),
}


def base_sums(sums_ref, row):
    first = 5 * (row + 5) + jnp.minimum(lax.axis_index("lat"), 0)
    return {name: sums_ref[array, pl.ds(LANES * half + first, 8), :] for name, (array, half) in PLACES.items()}


def adjoint_terms(s, here, above):
    here_right = lane_roll(here, -1)
    above_right = lane_roll(above, -1)
    g0 = s["00"] * here + s["01"] * here_right + s["02"] * above + s["03"] * above_right - s["d0"]
    g1 = s["01"] * here + s["11"] * here_right + s["12"] * above + s["13"] * above_right - s["d1"]
    g2 = s["02"] * here + s["12"] * here_right + s["22"] * above + s["23"] * above_right - s["d2"]
    g3 = s["03"] * here + s["13"] * here_right + s["23"] * above + s["33"] * above_right - s["d3"]
    return g0 + lane_roll(g1, 1), g2 + lane_roll(g3, 1)


FACTOR_LANES = (16, 17, 20, 21, 24, 25)


def edge_factors(now, before):
    east = (now["d1"] + before["d3"], now["11"] + before["33"], now["01"] + before["23"], now["13"], now["12"], now["03"])
    west = (now["d0"] + before["d2"], now["00"] + before["22"], now["01"] + before["23"], now["02"], now["03"], now["12"])
    return east, west


def track_kernel(
    value_ref, weight_ref, tile_ref, time_ref, row_ref, col_ref, state_ref, out_ref, to_near_ref, to_far_ref
):
    latitude = tile_ref[...] * ROWS + row_ref[...]
    keys = [time_ref[...].astype(F32), latitude.astype(F32), col_ref[...].astype(F32)]
    block = jnp.concatenate([value_ref[...], weight_ref[...]] + keys, axis=0)
    count = out_ref.shape[0] // 8
    number = lax.broadcasted_iota(jnp.int32, (1, TRACK), 1).astype(F32)
    key = block[6:7] * float(TRACK) + number
    key_down = jnp.broadcast_to(key, (LANES, TRACK)).T[:, 0:1]
    rank = jnp.sum(jnp.where(key_down < key, 1.0, 0.0), axis=0, keepdims=True)
    target = lax.broadcasted_iota(jnp.int32, (TRACK, TRACK), 0).astype(F32)
    chosen = jnp.where(target == rank, 1.0, 0.0).astype(BF16)
    ordered = nt_dot(jnp.concatenate([block, block], axis=0).astype(BF16), chosen)[0:8]
    for pair in range(count // 2):
        turned = []
        for k in (2 * pair, 2 * pair + 1):
            skipped = jnp.sum(jnp.where(block[6:7] < float(ROWS * k - 5), 1, 0))
            turned.append(pltpu.roll(ordered, jnp.where(skipped == 0, 0, TRACK - skipped), 1)[:, 0:SENT])
        out_ref[16 * pair : 16 * pair + 16, :] = jnp.concatenate(turned, axis=0).astype(BF16)
    even = lax.axis_index("lat") % 2 == 0
    for day in range(DAYS):
        lower = state_ref[ROWS * day : ROWS * day + HALO, :]
        upper = state_ref[ROWS * (day + 1) - HALO : ROWS * (day + 1), :]
        to_near_ref[HALO * day : HALO * day + HALO, :] = jnp.where(even, upper, lower)
        to_far_ref[HALO * day : HALO * day + HALO, :] = jnp.where(even, lower, upper)


def prepare_kernel(gate_ref, gate_bias_ref, in_ref, in_bias_ref, out_ref, inc_ref, w_gate_ref, w_in_ref, w_out_ref, w_inc_ref):
    def rows_of(ref, k):
        return jnp.concatenate([ref[k].astype(F32)[0:DAYS], jnp.zeros((8 - DAYS, ref.shape[2]), F32)], axis=0)

    def bias_rows(bias):
        high = bias.astype(BF16).astype(F32)
        middle = (bias - high).astype(BF16).astype(F32)
        low = bias - high - middle
        return jnp.concatenate([high, middle, low, jnp.zeros((5, bias.shape[1]), F32)], axis=0)

    pieces = [rows_of(gate_ref, k) for k in range(9)] + [bias_rows(gate_bias_ref[...])]
    pieces += [gate_ref[k].astype(F32)[DAYS:] for k in range(9)]
    whole = jnp.concatenate(pieces + [jnp.zeros((768 - 656, 4 * HID), F32)], axis=0)
    for k in range(6):
        block = whole[128 * k : 128 * k + 128]
        first = lane_roll(block[:, 0:128], HID) * 0.5
        second = block[:, 128:256]
        lane = lax.broadcasted_iota(jnp.int32, (128, 128), 1)
        second = jnp.where(lane < HID, 0.5 * second, second)
        w_gate_ref[0:128, 128 * k : 128 * k + 128] = first.T.astype(BF16)
        w_gate_ref[128:256, 128 * k : 128 * k + 128] = second.T.astype(BF16)
    narrow = jnp.concatenate([rows_of(in_ref, k) for k in range(9)] + [bias_rows(in_bias_ref[...])], axis=0)
    narrow = jnp.concatenate([narrow, jnp.zeros((48, HID), F32)], axis=0)
    narrow = jnp.concatenate([narrow, jnp.zeros((128, 128 - HID), F32)], axis=1)
    w_in_ref[...] = narrow.T[0:HID].astype(BF16)
    spread = [rows_of(out_ref, k) for k in range(9)]
    w_out_ref[...] = jnp.concatenate(spread + [jnp.zeros((8, HID), F32)], axis=0).astype(BF16)
    w_inc_ref[...] = jnp.concatenate(
        [inc_ref[...].astype(F32), jnp.zeros((16 - DAYS, HID), F32)], axis=0
    ).astype(BF16)


PRODUCTS = (
    ((0, 512), (384, 640), {(0, 0): (3, 1), (1, 0): (3, 0), (2, 0): (6, 0), (3, 0): (6, 1), (0, 1): (4, 1), (1, 1): (4, 0), (2, 1): (7, 0), (3, 1): (7, 1)}),
    ((0, 256), (128, 384), {(0, 0): (2, 1), (1, 0): (2, 0), (0, 1): (1, 1), (1, 1): (1, 0)}),
    ((128, 384), (0, 256), {(0, 0): (0, 0), (1, 1): (5, 0)}),
)
ROW_WEIGHTS = (1, 0, 2, 3)
COL_WEIGHTS = (0, 2, 1, 3, -1)


def sums_kernel(track_ref, sums_ref, rw_ref, cw_ref):
    base_row = (lax.axis_index("lat") * ROWS - 5).astype(F32)

    def accumulate(chunk, lanes, sources, fresh):
        slot = chunk % 2
        width = lanes.stop - lanes.start
        filled = 2 * len(sources) * width
        entry = lax.broadcasted_iota(jnp.int32, (LANES, width), 0).astype(F32).astype(BF16)
        nothing = jnp.zeros((LANES, width), BF16)

        def spread(row):
            part = jnp.broadcast_to(row, (16, width)).astype(BF16)
            return jnp.concatenate([part] * 8, axis=0)

        for index, pair in enumerate(sources):
            both = track_ref[16 * pair : 16 * pair + 16, lanes].astype(F32)
            for part in range(2):
                block = both[8 * part : 8 * part + 8]
                start = (2 * index + part) * width
                offset = block[6:7] - base_row
                within = (offset >= 0.0) & (offset < float(BASES))
                row_hit = entry == spread(jnp.where(within, offset * 5.0 + block[5:6], -1.0))
                col_hit = entry == spread(block[7:8])
                for source in range(5):
                    value = spread(block[source : source + 1])
                    if source > 0:
                        k = ROW_WEIGHTS.index(source - 1)
                        rw_ref[slot, 128 * k : 128 * k + 128, start : start + width] = jnp.where(row_hit, value, nothing)
                    k = COL_WEIGHTS.index(source - 1)
                    cw_ref[slot, 128 * k : 128 * k + 128, start : start + width] = jnp.where(col_hit, value, nothing)
        for (row0, row1), (col0, col1), blocks in PRODUCTS:
            product = nt_dot(rw_ref[slot, row0:row1, 0:filled], cw_ref[slot, col0:col1, 0:filled])
            for (i, j), (array, half) in blocks.items():
                total = product[128 * i : 128 * i + 128, 128 * j : 128 * j + 128]
                rows = slice(LANES * half, LANES * half + LANES)
                sums_ref[array, rows, :] = total if fresh else sums_ref[array, rows, :] + total

    pairs = track_ref.shape[0] // 16
    size = CHUNK // (2 * ALWAYS)
    for chunk, first in enumerate(range(0, pairs, size)):
        accumulate(chunk, slice(0, ALWAYS), range(first, min(first + size, pairs)), chunk == 0)
    rest = track_ref[:, ALWAYS:SENT].astype(F32) - base_row
    row_kind = lax.broadcasted_iota(jnp.int32, rest.shape, 0) % 8
    needed = jnp.max(jnp.where((row_kind == 6) & (rest >= 0.0) & (rest < float(BASES)), 1.0, 0.0))

    @pl.when(needed > 0.0)
    def _():
        for first in range(0, pairs, 2 * size):
            accumulate(0, slice(ALWAYS, SENT), range(first, min(first + 2 * size, pairs)), False)


def edges_kernel(mid_ref, near_ref, far_ref, sums_ref, adjoint_ref, to_far_ref, to_near_ref, field_ref):
    even_lat = lax.axis_index("lat") % 2 == 0
    even_lon = lax.axis_index("lon") % 2 == 0
    lane = lax.broadcasted_iota(jnp.int32, (8, LANES), 1)
    zero = jnp.zeros((8, LANES), F32)
    east, west, factors = zero, zero, zero
    carried = zero
    for row in range(-6, ROWS + 6):
        field_ref[row + 6] = day_rows(near_ref, mid_ref, far_ref, even_lat, row)
    for row in range(-6, ROWS + 6):
        part, place = strip_place(row)
        here = field_ref[row + 6]
        picked = lane // 8 == place // 8
        east = jnp.where(picked, lane_roll(here, place - 120), east)
        west = jnp.where(picked, lane_roll(here, place), west)
        if -5 <= row <= 19:
            above = field_ref[row + 7]
            sums = base_sums(sums_ref, row)
            now, later = adjoint_terms(sums, here, above)
            if row > -5:
                total = carried + now
                adjoint_ref[row + 4] = total
                picked = lane // 8 == place // 8 + 1
                east = jnp.where(picked, lane_roll(total, place + 8 - 120), east)
                west = jnp.where(picked, lane_roll(total, place + 8), west)
            if -2 <= row <= ROWS:
                for k, (last, first) in enumerate(zip(*edge_factors(sums, before))):
                    target = place + FACTOR_LANES[k]
                    both = lane_roll(jnp.where(lane < 64, first, last), target - (COLS - 2))
                    factors = jnp.where((lane == target) | (lane == target + 2), both, factors)
            carried = later
            before = sums
        if place == 96:
            east = jnp.where(lane % 32 >= 16, factors, east)
            west = jnp.where(lane % 32 >= 16, factors, west)
            factors = zero
            to_near_ref[8 * part : 8 * part + 8, :] = jnp.where(even_lon, east, west)
            to_far_ref[8 * part : 8 * part + 8, :] = jnp.where(even_lon, west, east)
            east, west = zero, zero


def row_mask(lat_count, row):
    row = row + lax.axis_index("lat") * ROWS
    return (row >= 0) & (row < lat_count * ROWS)


def tile(index, count=1):
    return slice(index * LANES, (index + count) * LANES)


def at(row):
    return tile(row + FIRST)


def ones_rows():
    return jnp.where(lax.broadcasted_iota(jnp.int32, (8, LANES), 0) < 3, 1.0, 0.0).astype(F32)


def spread_terms(spread_ref, row):
    columns = []
    for b in range(3):
        terms = [spread_ref[8 * (3 * a + b) : 8 * (3 * a + b) + 8, at(row + a - 1)] for a in range(3)]
        columns.append(terms[0] + terms[1] + terms[2])
    return columns


def first_kernel(
    field_ref, w_in_ref, w_out_ref, out_ref, est_ref, minus_ref, plus_ref, window_ref, spread_ref, *, lat_count
):
    for row in range(-6, 22):
        value = field_ref[row + 6]
        est_ref[:, at(row)] = value
        minus_ref[:, at(row)] = lane_roll(value, 1)
        plus_ref[:, at(row)] = lane_roll(value, -1)
    ones = ones_rows()
    for row in range(-5, 21):
        pieces = [source[:, at(row + a)] for a in (-1, 0, 1) for source in (minus_ref, est_ref, plus_ref)]
        window_ref[:, at(row)] = jnp.concatenate(pieces + [ones], axis=0).astype(BF16)
    groups = [(-5, 5), (0, 4), (4, 4), (8, 4), (12, 4), (16, 5)]
    for row, count in groups:
        where = tile(row + FIRST, count)
        value = jnp.dot(w_in_ref[:, 0:80], window_ref[:, where], preferred_element_type=F32)
        value = jnp.maximum(value, 0.0)
        if row < 0 or row >= ROWS:
            flags = [
                jnp.where(row_mask(lat_count, row + k), jnp.ones((1, LANES), F32), 0.0) for k in range(count)
            ]
            value = value * jnp.concatenate(flags, axis=1)
        spread_ref[:, where] = jnp.dot(w_out_ref[...], value.astype(BF16), preferred_element_type=F32)
    for row in range(-4, 20):
        columns = spread_terms(spread_ref, row)
        term = columns[1] + lane_roll(columns[0], 1) + lane_roll(columns[2], -1)
        out_ref[row + 4] = est_ref[:, at(row)] - term


def solve_kernel(
    field_ref,
    sums_ref,
    adjoint_ref,
    first_ref,
    own_far_ref,
    own_near_ref,
    from_far_ref,
    from_near_ref,
    w_in_ref,
    w_out_ref,
    w_gate_ref,
    w_inc_ref,
    est_out_ref,
    cell_out_ref,
    est_ref,
    grad_ref,
    minus_ref,
    plus_ref,
    mask_ref,
    window_ref,
    spread_ref,
    cell_ref,
    hidden_ref,
    hid_minus_ref,
    hid_plus_ref,
    *,
    lat_count,
):
    even_lon = lax.axis_index("lon") % 2 == 0
    lane = lax.broadcasted_iota(jnp.int32, (8, LANES), 1)
    zero = jnp.zeros((8, LANES), F32)
    strips = slice(STRIP * LANES, TILES * LANES)
    strip_width = (TILES - STRIP) * LANES
    strip_lane = lax.broadcasted_iota(jnp.int32, (8, strip_width), 1)

    def within(row):
        return row_mask(lat_count, row)

    def left(main, strip, row):
        part, place = strip_place(row)
        edge = lane_roll(strip[:, tile(part)], -(place + 7))
        return jnp.where(lane[: main.shape[0]] == 0, edge, lane_roll(main, 1))

    def right(main, strip, row):
        part, place = strip_place(row)
        edge = lane_roll(strip[:, tile(part)], 127 - (place + 24))
        return jnp.where(lane[: main.shape[0]] == 127, edge, lane_roll(main, -1))

    est_ref[:, at(-7)] = zero
    est_ref[:, at(22)] = zero
    for row in range(-6, 22):
        est_ref[:, at(row)] = field_ref[row + 6]
    quarter = (lane % 32) // 8
    from_west, from_east, adjoint_strip = [], [], []
    for part in range(TILES - STRIP):
        rows = slice(8 * part, 8 * part + 8)
        own_east = jnp.where(even_lon, own_near_ref[rows, :], own_far_ref[rows, :])
        own_west = jnp.where(even_lon, own_far_ref[rows, :], own_near_ref[rows, :])
        west = jnp.where(even_lon, from_far_ref[rows, :], from_near_ref[rows, :])
        east = jnp.where(even_lon, from_near_ref[rows, :], from_far_ref[rows, :])
        from_west.append(west)
        from_east.append(east)

        def join(first, second, third, fourth):
            return jnp.where(
                quarter < 2, jnp.where(quarter == 0, first, second), jnp.where(quarter == 2, third, fourth)
            )

        est_ref[:, tile(STRIP + part)] = join(west, lane_roll(own_west, 8), lane_roll(own_east, 16), lane_roll(east, 24))
        adjoint_strip.append(join(lane_roll(west, -8), own_west, lane_roll(own_east, 8), lane_roll(east, 16)))
    from_west = jnp.concatenate(from_west, axis=1)
    from_east = jnp.concatenate(from_east, axis=1)
    adjoint_strip = jnp.concatenate(adjoint_strip, axis=1)
    for row in range(-7, 23):
        mask_ref[:, at(row)] = jnp.where(within(row), jnp.ones((8, LANES), F32), 0.0)
    mask_ref[:, strips] = jnp.where(within(strip_lane // 32 - 6), 1.0, 0.0)

    ones = ones_rows()

    def windows(ref, first_row, last_row, with_strips):
        strip = ref[:, strips]
        for row in range(first_row - 1, last_row + 2) if first_row <= last_row else ():
            main = ref[:, at(row)]
            minus_ref[:, at(row)] = left(main, strip, row)
            plus_ref[:, at(row)] = right(main, strip, row)
        for row in range(first_row, last_row + 1):
            pieces = [source[:, at(row + a)] for a in (-1, 0, 1) for source in (minus_ref, ref, plus_ref)]
            window_ref[:, at(row)] = jnp.concatenate(pieces + [ones], axis=0).astype(BF16)
        if with_strips:
            pieces = []
            shifts = (lane_roll(strip, 1), strip, lane_roll(strip, -1))
            for a in (-1, 0, 1):
                pieces += [lane_roll(value, -32 * a) if a else value for value in shifts]
            pieces.append(jnp.concatenate([ones] * (TILES - STRIP), axis=1))
            window_ref[:, strips] = jnp.concatenate(pieces, axis=0).astype(BF16)

    def pieces_of(first_row, last_row):
        runs = [(first_row + FIRST, last_row + 1 + FIRST), (STRIP, TILES)]
        return [tile(t, min(GROUP, end - t)) for start, end in runs for t in range(start, end, GROUP)]

    def gradient(first_row, last_row, low, high):
        windows(est_ref, low, high, True)
        for where in pieces_of(low, high):
            value = jnp.dot(w_in_ref[:, 0:80], window_ref[:, where], preferred_element_type=F32)
            value = jnp.maximum(value, 0.0) * mask_ref[0:1, where]
            spread_ref[:, where] = jnp.dot(w_out_ref[...], value.astype(BF16), preferred_element_type=F32)
        totals = []
        for b in range(3):
            total = None
            for a in range(3):
                k = 8 * (3 * a + b)
                piece = spread_ref[k : k + 8, strips]
                piece = lane_roll(piece, 32 - 32 * a) if a != 1 else piece
                total = piece if total is None else total + piece
            totals.append(total)
        strip = est_ref[:, strips] - (totals[1] + lane_roll(totals[0], 1) + lane_roll(totals[2], -1))
        grad_ref[:, strips] = strip
        for row in range(first_row, last_row + 1):
            columns = spread_terms(spread_ref, row)
            term = columns[1] + left(columns[0], totals[0], row) + right(columns[2], totals[2], row)
            grad_ref[:, at(row)] = est_ref[:, at(row)] - term
        return strip

    strip = gradient(0, -1, 0, -1)
    for row in range(-4, 20):
        part, place = strip_place(row)
        edges = strip[:, tile(part)]
        total = jnp.where(
            lane < 2,
            lane_roll(edges, -(place + 8)),
            jnp.where(lane >= 126, lane_roll(edges, 126 - (place + 22)), first_ref[row + 4]),
        )
        total = total + adjoint_ref[row + 4]
        grad_ref[:, at(row)] = total if 0 <= row < ROWS else total * mask_ref[:, at(row)]
    grad_ref[:, strips] = (strip + adjoint_strip) * mask_ref[:, strips]
    windows(grad_ref, -3, 18, True)
    for where in pieces_of(-3, 18):
        sums = jnp.dot(w_gate_ref[HID:, 0:80], window_ref[:, where], preferred_element_type=F32)
        gate_in = 0.5 * jnp.tanh(sums[0:HID]) + 0.5
        gate_out = 0.5 * jnp.tanh(sums[HID : 2 * HID]) + 0.5
        cell = gate_in * jnp.tanh(sums[2 * HID : 3 * HID])
        hidden = (gate_out * jnp.tanh(cell) * mask_ref[0:1, where]).astype(BF16)
        cell_ref[:, where] = cell
        hidden_ref[:, where] = hidden
        update = jnp.dot(w_inc_ref[...], hidden, preferred_element_type=F32)
        est_ref[:, where] -= update[0:8]

    lane64 = lax.broadcasted_iota(jnp.int32, (HID, LANES), 1)
    for row in range(-1, ROWS + 1):
        part, place = strip_place(row)
        main = hidden_ref[:, at(row)]
        strip = hidden_ref[:, tile(STRIP + part)]
        hid_minus_ref[:, at(row)] = jnp.where(lane64 == 0, lane_roll(strip, -(place + 7)), lane_roll(main, 1))
        hid_plus_ref[:, at(row)] = jnp.where(lane64 == 127, lane_roll(strip, 127 - (place + 24)), lane_roll(main, -1))
    gradient(-1, 16, -2, 17)
    carried = zero
    for row in range(-2, ROWS + 1):
        now, later = adjoint_terms(base_sums(sums_ref, row), est_ref[:, at(row)], est_ref[:, at(row + 1)])
        if row > -2:
            total = grad_ref[:, at(row)] + carried + now
            grad_ref[:, at(row)] = total if 0 <= row < ROWS else total * mask_ref[:, at(row)]
        carried = later
    here = est_ref[:, strips]
    above = lane_roll(here, -32)

    def edge_term(source, lane_at, inner):
        constant, own, beside, up, up_beside, down_beside = [lane_roll(source, lane_at - k) for k in FACTOR_LANES]
        here_beside = lane_roll(here, inner)
        total = own * here + beside * here_beside + up * above + up_beside * lane_roll(above, inner) - constant
        return total + lane_roll(up * here + down_beside * here_beside, 32)

    extra_w = edge_term(from_west, 7, 1)
    extra_e = edge_term(from_east, 24 - 2, -1)
    grad_ref[:, strips] = (
        grad_ref[:, strips] + jnp.where(strip_lane % 32 < 16, extra_w, extra_e)
    ) * mask_ref[:, strips]
    windows(grad_ref, 0, ROWS - 1, False)
    for row in range(0, ROWS, 2):
        pieces = [window_ref[:, tile(row + FIRST, 2)]]
        for a in (-1, 0, 1):
            for source in (hid_minus_ref, hidden_ref, hid_plus_ref):
                pieces.append(source[:, tile(row + a + FIRST, 2)])
        sums = jnp.dot(w_gate_ref[:, 0:656], jnp.concatenate(pieces, axis=0), preferred_element_type=F32)
        old = cell_ref[:, tile(row + FIRST, 2)]
        forget = 0.5 * jnp.tanh(sums[0:HID]) + 0.5
        gate_in = 0.5 * jnp.tanh(sums[HID : 2 * HID]) + 0.5
        gate_out = 0.5 * jnp.tanh(sums[2 * HID : 3 * HID]) + 0.5
        cell = forget * old + gate_in * jnp.tanh(sums[3 * HID :])
        hidden = gate_out * jnp.tanh(cell)
        update = jnp.dot(w_inc_ref[...], hidden.astype(BF16), preferred_element_type=F32)
        for k in range(2):
            cell_out_ref[pl.ds(row + k, HID, stride=ROWS), :] = cell[:, tile(k)]
            final = est_ref[:, at(row + k)] - update[0:8, tile(k)]
            est_out_ref[pl.ds(row + k, DAYS, stride=ROWS), :] = final[0:DAYS]


def swap(value, axis, first, count, periodic):
    last = count if periodic else count - 1
    pairs = [(i, (i + 1) % count) for i in range(first, last, 2)]
    return lax.ppermute(value, axis, pairs + [(target, source) for source, target in pairs])


def on_device(
    state,
    prior_in,
    prior_bias,
    prior_out,
    lstm_weight,
    lstm_bias,
    lstm_out,
    obs_value,
    obs_weight,
    obs_tile,
    obs_time,
    obs_row,
    obs_col,
):
    lat_count = lax.axis_size("lat")
    lon_count = lax.axis_size("lon")
    mid = state.reshape(DAYS * ROWS, LANES)

    vmem = pl.BlockSpec(memory_space=pltpu.VMEM)
    track, lat_near, lat_far = pl.pallas_call(
        track_kernel,
        out_shape=(
            jax.ShapeDtypeStruct((lat_count * 8, SENT), BF16),
            jax.ShapeDtypeStruct((DAYS * HALO, LANES), F32),
            jax.ShapeDtypeStruct((DAYS * HALO, LANES), F32),
        ),
        in_specs=[vmem] * 7,
        out_specs=(vmem, vmem, vmem),
        cost_estimate=pl.CostEstimate(flops=100_000, bytes_accessed=150_000, transcendentals=0),
        name="track",
    )(
        obs_value.reshape(1, TRACK),
        obs_weight,
        obs_tile.reshape(1, TRACK),
        obs_time.reshape(1, TRACK),
        obs_row.reshape(1, TRACK),
        obs_col.reshape(1, TRACK),
        mid,
    )
    gathered = lax.all_to_all(
        track.reshape(lat_count, 8, SENT), "lat", split_axis=0, concat_axis=0, tiled=True
    ).reshape(lat_count * 8, SENT)
    far = swap(lat_far, "lat", 1, lat_count, False)
    near = swap(lat_near, "lat", 0, lat_count, False)
    w_gate, w_in, w_out, w_inc = pl.pallas_call(
        prepare_kernel,
        out_shape=(
            jax.ShapeDtypeStruct((4 * HID, 768), BF16),
            jax.ShapeDtypeStruct((HID, LANES), BF16),
            jax.ShapeDtypeStruct((80, HID), BF16),
            jax.ShapeDtypeStruct((16, HID), BF16),
        ),
        in_specs=[vmem] * 6,
        out_specs=(vmem,) * 4,
        compiler_params=pltpu.CompilerParams(vmem_limit_bytes=16 * 1024 * 1024),
        cost_estimate=pl.CostEstimate(flops=2_000_000, bytes_accessed=1_500_000, transcendentals=0),
        name="prepare",
    )(
        jnp.transpose(lstm_weight, (0, 2, 1)),
        lstm_bias.reshape(1, 4 * HID),
        jnp.transpose(prior_in, (0, 2, 1)),
        prior_bias.reshape(1, HID),
        prior_out,
        lstm_out,
    )
    sums = pl.pallas_call(
        sums_kernel,
        out_shape=jax.ShapeDtypeStruct((8, 256, LANES), F32),
        in_specs=[vmem],
        out_specs=vmem,
        scratch_shapes=[
            pltpu.VMEM((2, 512, CHUNK), BF16),
            pltpu.VMEM((2, 640, CHUNK), BF16),
        ],
        compiler_params=pltpu.CompilerParams(vmem_limit_bytes=32 * 1024 * 1024),
        cost_estimate=pl.CostEstimate(flops=4_000_000_000, bytes_accessed=1_500_000, transcendentals=0),
        name="sums",
    )(gathered)
    adjoint, to_far, to_near, field = pl.pallas_call(
        edges_kernel,
        out_shape=(
            jax.ShapeDtypeStruct((24, 8, LANES), F32),
            jax.ShapeDtypeStruct((56, LANES), F32),
            jax.ShapeDtypeStruct((56, LANES), F32),
            jax.ShapeDtypeStruct((28, 8, LANES), F32),
        ),
        in_specs=[vmem] * 4,
        out_specs=(vmem, vmem, vmem, vmem),
        compiler_params=pltpu.CompilerParams(vmem_limit_bytes=16 * 1024 * 1024),
        cost_estimate=pl.CostEstimate(flops=1_000_000, bytes_accessed=1_500_000, transcendentals=0),
        name="edges",
    )(mid, near, far, sums)

    width = TILES * LANES
    main_width = STRIP * LANES

    def first(*refs):
        first_kernel(*refs, lat_count=lat_count)

    started = pl.pallas_call(
        first,
        out_shape=jax.ShapeDtypeStruct((24, 8, LANES), F32),
        in_specs=[vmem] * 3,
        out_specs=vmem,
        scratch_shapes=[
            pltpu.VMEM((8, main_width), F32),
            pltpu.VMEM((8, main_width), F32),
            pltpu.VMEM((8, main_width), F32),
            pltpu.VMEM((80, main_width), BF16),
            pltpu.VMEM((80, main_width), F32),
        ],
        compiler_params=pltpu.CompilerParams(vmem_limit_bytes=16 * 1024 * 1024),
        cost_estimate=pl.CostEstimate(flops=2_000_000_000, bytes_accessed=500_000, transcendentals=0),
        name="first",
    )(field, w_in, w_out)
    from_far = swap(to_far, "lon", 1, lon_count, True)
    from_near = swap(to_near, "lon", 0, lon_count, True)

    def solve(*refs):
        solve_kernel(*refs, lat_count=lat_count)

    estimate, cell_state = pl.pallas_call(
        solve,
        out_shape=(
            jax.ShapeDtypeStruct((DAYS * ROWS, LANES), F32),
            jax.ShapeDtypeStruct((HID * ROWS, LANES), F32),
        ),
        in_specs=[vmem] * 12,
        out_specs=(vmem, vmem),
        scratch_shapes=[
            pltpu.VMEM((8, width), F32),
            pltpu.VMEM((8, width), F32),
            pltpu.VMEM((8, width), F32),
            pltpu.VMEM((8, width), F32),
            pltpu.VMEM((8, width), F32),
            pltpu.VMEM((80, width), BF16),
            pltpu.VMEM((80, width), F32),
            pltpu.VMEM((HID, width), F32),
            pltpu.VMEM((HID, width), BF16),
            pltpu.VMEM((HID, width), BF16),
            pltpu.VMEM((HID, width), BF16),
        ],
        compiler_params=pltpu.CompilerParams(vmem_limit_bytes=32 * 1024 * 1024),
        name="solve",
    )(field, sums, adjoint, started, to_far, to_near, from_far, from_near, w_in, w_out, w_gate, w_inc)
    return (
        estimate.reshape(DAYS, ROWS, LANES),
        cell_state.reshape(HID, ROWS, LANES),
    )


def solution(mesh):
    return jax.shard_map(
        on_device,
        mesh=mesh,
        in_specs=(
            P(None, "lat", "lon"),
            P(),
            P(),
            P(),
            P(),
            P(),
            P(),
            P(("lon", "lat")),
            P(None, ("lon", "lat")),
            P(("lon", "lat"), None),
            P(("lon", "lat")),
            P(("lon", "lat")),
            P(("lon", "lat")),
        ),
        out_specs=(P(None, "lat", "lon"), P(None, "lat", "lon")),
        check_vma=False,
    )
```

```python
import jax
import jax.numpy as jnp
from jax import lax
from jax.experimental import pallas as pl
from jax.experimental.pallas import tpu as pltpu
from jax.sharding import PartitionSpec as P

DAYS = 5
ROWS = 16
COLS = 128
LANES = 128
HID = 64
TRACK = 512
SENT = 384
ALWAYS = 256
HALO = 8
BASES = 25
CHUNK = 2048
FIRST = 7
STRIP = 30
TILES = 37
GROUP = 4
F32 = jnp.float32
BF16 = jnp.bfloat16


def nt_dot(left, right):
    return lax.dot_general(left, right, (((1,), (1,)), ((), ())), preferred_element_type=F32)


def lane_roll(value, shift):
    return pltpu.roll(value, shift % value.shape[1], 1)


def strip_place(row):
    return (row + 6) // 4, (row + 6) % 4 * 32


def day_rows(near_ref, mid_ref, far_ref, even, row):
    if 0 <= row < ROWS:
        picked = mid_ref[pl.ds(row, DAYS, stride=ROWS), :]
    else:
        place = pl.ds(row + HALO if row < 0 else row - ROWS, DAYS, stride=HALO)
        near, far = near_ref[place, :], far_ref[place, :]
        picked = jnp.where(even, far, near) if row < 0 else jnp.where(even, near, far)
    return jnp.concatenate([picked, jnp.zeros((8 - DAYS, LANES), F32)], axis=0)


PLACES = {
    "00": (0, 0), "01": (1, 0), "02": (2, 0), "03": (3, 0), "d0": (4, 0), "11": (1, 1), "12": (2, 1), "13": (3, 1), "d1": (4, 1),
    "22": (5, 0), "23": (6, 0), "d2": (7, 0), "33": (6, 1), "d3": (7, 1),
}


def base_sums(sums_ref, row):
    first = 5 * (row + 5) + jnp.minimum(lax.axis_index("lat"), 0)
    return {name: sums_ref[array, pl.ds(LANES * half + first, 8), :] for name, (array, half) in PLACES.items()}


def adjoint_terms(s, here, above):
    here_right = lane_roll(here, -1)
    above_right = lane_roll(above, -1)
    g0 = s["00"] * here + s["01"] * here_right + s["02"] * above + s["03"] * above_right - s["d0"]
    g1 = s["01"] * here + s["11"] * here_right + s["12"] * above + s["13"] * above_right - s["d1"]
    g2 = s["02"] * here + s["12"] * here_right + s["22"] * above + s["23"] * above_right - s["d2"]
    g3 = s["03"] * here + s["13"] * here_right + s["23"] * above + s["33"] * above_right - s["d3"]
    return g0 + lane_roll(g1, 1), g2 + lane_roll(g3, 1)


FACTOR_LANES = (16, 17, 20, 21, 24, 25)


def edge_factors(now, before):
    east = (now["d1"] + before["d3"], now["11"] + before["33"], now["01"] + before["23"], now["13"], now["12"], now["03"])
    west = (now["d0"] + before["d2"], now["00"] + before["22"], now["01"] + before["23"], now["02"], now["03"], now["12"])
    return east, west


def track_kernel(
    value_ref, weight_ref, tile_ref, time_ref, row_ref, col_ref, state_ref, out_ref, to_near_ref, to_far_ref
):
    latitude = tile_ref[...] * ROWS + row_ref[...]
    keys = [time_ref[...].astype(F32), latitude.astype(F32), col_ref[...].astype(F32)]
    block = jnp.concatenate([value_ref[...], weight_ref[...]] + keys, axis=0)
    count = out_ref.shape[0] // 8
    number = lax.broadcasted_iota(jnp.int32, (1, TRACK), 1).astype(F32)
    key = block[6:7] * float(TRACK) + number
    key_down = jnp.broadcast_to(key, (LANES, TRACK)).T[:, 0:1]
    rank = jnp.sum(jnp.where(key_down < key, 1.0, 0.0), axis=0, keepdims=True)
    target = lax.broadcasted_iota(jnp.int32, (TRACK, TRACK), 0).astype(F32)
    chosen = jnp.where(target == rank, 1.0, 0.0).astype(BF16)
    ordered = nt_dot(jnp.concatenate([block, block], axis=0).astype(BF16), chosen)[0:8]
    for pair in range(count // 2):
        turned = []
        for k in (2 * pair, 2 * pair + 1):
            skipped = jnp.sum(jnp.where(block[6:7] < float(ROWS * k - 5), 1, 0))
            turned.append(pltpu.roll(ordered, jnp.where(skipped == 0, 0, TRACK - skipped), 1)[:, 0:SENT])
        out_ref[16 * pair : 16 * pair + 16, :] = jnp.concatenate(turned, axis=0).astype(BF16)
    even = lax.axis_index("lat") % 2 == 0
    for day in range(DAYS):
        lower = state_ref[ROWS * day : ROWS * day + HALO, :]
        upper = state_ref[ROWS * (day + 1) - HALO : ROWS * (day + 1), :]
        to_near_ref[HALO * day : HALO * day + HALO, :] = jnp.where(even, upper, lower)
        to_far_ref[HALO * day : HALO * day + HALO, :] = jnp.where(even, lower, upper)


def prepare_kernel(gate_ref, gate_bias_ref, in_ref, in_bias_ref, out_ref, inc_ref, w_gate_ref, w_in_ref, w_out_ref, w_inc_ref):
    def rows_of(ref, k):
        return jnp.concatenate([ref[k].astype(F32)[0:DAYS], jnp.zeros((8 - DAYS, ref.shape[2]), F32)], axis=0)

    def bias_rows(bias):
        high = bias.astype(BF16).astype(F32)
        middle = (bias - high).astype(BF16).astype(F32)
        low = bias - high - middle
        return jnp.concatenate([high, middle, low, jnp.zeros((5, bias.shape[1]), F32)], axis=0)

    pieces = [rows_of(gate_ref, k) for k in range(9)] + [bias_rows(gate_bias_ref[...])]
    pieces += [gate_ref[k].astype(F32)[DAYS:] for k in range(9)]
    whole = jnp.concatenate(pieces + [jnp.zeros((768 - 656, 4 * HID), F32)], axis=0)
    for k in range(6):
        block = whole[128 * k : 128 * k + 128]
        first = lane_roll(block[:, 0:128], HID) * 0.5
        second = block[:, 128:256]
        lane = lax.broadcasted_iota(jnp.int32, (128, 128), 1)
        second = jnp.where(lane < HID, 0.5 * second, second)
        w_gate_ref[0:128, 128 * k : 128 * k + 128] = first.T.astype(BF16)
        w_gate_ref[128:256, 128 * k : 128 * k + 128] = second.T.astype(BF16)
    narrow = jnp.concatenate([rows_of(in_ref, k) for k in range(9)] + [bias_rows(in_bias_ref[...])], axis=0)
    narrow = jnp.concatenate([narrow, jnp.zeros((48, HID), F32)], axis=0)
    narrow = jnp.concatenate([narrow, jnp.zeros((128, 128 - HID), F32)], axis=1)
    w_in_ref[...] = narrow.T[0:HID].astype(BF16)
    spread = [rows_of(out_ref, k) for k in range(9)]
    w_out_ref[...] = jnp.concatenate(spread + [jnp.zeros((8, HID), F32)], axis=0).astype(BF16)
    w_inc_ref[...] = jnp.concatenate(
        [inc_ref[...].astype(F32), jnp.zeros((16 - DAYS, HID), F32)], axis=0
    ).astype(BF16)


PRODUCTS = (
    ((0, 512), (384, 640), {(0, 0): (3, 1), (1, 0): (3, 0), (2, 0): (6, 0), (3, 0): (6, 1), (0, 1): (4, 1), (1, 1): (4, 0), (2, 1): (7, 0), (3, 1): (7, 1)}),
    ((0, 256), (128, 384), {(0, 0): (2, 1), (1, 0): (2, 0), (0, 1): (1, 1), (1, 1): (1, 0)}),
    ((128, 384), (0, 256), {(0, 0): (0, 0), (1, 1): (5, 0)}),
)
ROW_WEIGHTS = (1, 0, 2, 3)
COL_WEIGHTS = (0, 2, 1, 3, -1)


def sums_kernel(track_ref, sums_ref, rw_ref, cw_ref):
    base_row = (lax.axis_index("lat") * ROWS - 5).astype(F32)

    def accumulate(chunk, lanes, sources, fresh):
        slot = chunk % 2
        width = lanes.stop - lanes.start
        filled = 2 * len(sources) * width
        entry = lax.broadcasted_iota(jnp.int32, (LANES, width), 0).astype(F32).astype(BF16)
        nothing = jnp.zeros((LANES, width), BF16)

        def spread(row):
            part = jnp.broadcast_to(row, (16, width)).astype(BF16)
            return jnp.concatenate([part] * 8, axis=0)

        for index, pair in enumerate(sources):
            both = track_ref[16 * pair : 16 * pair + 16, lanes].astype(F32)
            for part in range(2):
                block = both[8 * part : 8 * part + 8]
                start = (2 * index + part) * width
                offset = block[6:7] - base_row
                within = (offset >= 0.0) & (offset < float(BASES))
                row_hit = entry == spread(jnp.where(within, offset * 5.0 + block[5:6], -1.0))
                col_hit = entry == spread(block[7:8])
                for source in range(5):
                    value = spread(block[source : source + 1])
                    if source > 0:
                        k = ROW_WEIGHTS.index(source - 1)
                        rw_ref[slot, 128 * k : 128 * k + 128, start : start + width] = jnp.where(row_hit, value, nothing)
                    k = COL_WEIGHTS.index(source - 1)
                    cw_ref[slot, 128 * k : 128 * k + 128, start : start + width] = jnp.where(col_hit, value, nothing)
        for (row0, row1), (col0, col1), blocks in PRODUCTS:
            product = nt_dot(rw_ref[slot, row0:row1, 0:filled], cw_ref[slot, col0:col1, 0:filled])
            for (i, j), (array, half) in blocks.items():
                total = product[128 * i : 128 * i + 128, 128 * j : 128 * j + 128]
                rows = slice(LANES * half, LANES * half + LANES)
                sums_ref[array, rows, :] = total if fresh else sums_ref[array, rows, :] + total

    pairs = track_ref.shape[0] // 16
    size = CHUNK // (2 * ALWAYS)
    for chunk, first in enumerate(range(0, pairs, size)):
        accumulate(chunk, slice(0, ALWAYS), range(first, min(first + size, pairs)), chunk == 0)
    rest = track_ref[:, ALWAYS:SENT].astype(F32) - base_row
    row_kind = lax.broadcasted_iota(jnp.int32, rest.shape, 0) % 8
    needed = jnp.max(jnp.where((row_kind == 6) & (rest >= 0.0) & (rest < float(BASES)), 1.0, 0.0))

    @pl.when(needed > 0.0)
    def _():
        for first in range(0, pairs, 2 * size):
            accumulate(0, slice(ALWAYS, SENT), range(first, min(first + 2 * size, pairs)), False)


def edges_kernel(mid_ref, near_ref, far_ref, sums_ref, adjoint_ref, to_far_ref, to_near_ref, field_ref):
    even_lat = lax.axis_index("lat") % 2 == 0
    even_lon = lax.axis_index("lon") % 2 == 0
    lane = lax.broadcasted_iota(jnp.int32, (8, LANES), 1)
    zero = jnp.zeros((8, LANES), F32)
    east, west, factors = zero, zero, zero
    carried = zero
    for row in range(-6, ROWS + 6):
        field_ref[row + 6] = day_rows(near_ref, mid_ref, far_ref, even_lat, row)
    for row in range(-6, ROWS + 6):
        part, place = strip_place(row)
        here = field_ref[row + 6]
        picked = lane // 8 == place // 8
        east = jnp.where(picked, lane_roll(here, place - 120), east)
        west = jnp.where(picked, lane_roll(here, place), west)
        if -5 <= row <= 19:
            above = field_ref[row + 7]
            sums = base_sums(sums_ref, row)
            now, later = adjoint_terms(sums, here, above)
            if row > -5:
                total = carried + now
                adjoint_ref[row + 4] = total
                picked = lane // 8 == place // 8 + 1
                east = jnp.where(picked, lane_roll(total, place + 8 - 120), east)
                west = jnp.where(picked, lane_roll(total, place + 8), west)
            if -2 <= row <= ROWS:
                for k, (last, first) in enumerate(zip(*edge_factors(sums, before))):
                    target = place + FACTOR_LANES[k]
                    both = lane_roll(jnp.where(lane < 64, first, last), target - (COLS - 2))
                    factors = jnp.where((lane == target) | (lane == target + 2), both, factors)
            carried = later
            before = sums
        if place == 96:
            east = jnp.where(lane % 32 >= 16, factors, east)
            west = jnp.where(lane % 32 >= 16, factors, west)
            factors = zero
            to_near_ref[8 * part : 8 * part + 8, :] = jnp.where(even_lon, east, west)
            to_far_ref[8 * part : 8 * part + 8, :] = jnp.where(even_lon, west, east)
            east, west = zero, zero


def row_mask(lat_count, row):
    row = row + lax.axis_index("lat") * ROWS
    return (row >= 0) & (row < lat_count * ROWS)


def tile(index, count=1):
    return slice(index * LANES, (index + count) * LANES)


def at(row):
    return tile(row + FIRST)


def ones_rows():
    return jnp.where(lax.broadcasted_iota(jnp.int32, (8, LANES), 0) < 3, 1.0, 0.0).astype(F32)


def spread_terms(spread_ref, row):
    columns = []
    for b in range(3):
        terms = [spread_ref[8 * (3 * a + b) : 8 * (3 * a + b) + 8, at(row + a - 1)] for a in range(3)]
        columns.append(terms[0] + terms[1] + terms[2])
    return columns


def first_kernel(
    field_ref, w_in_ref, w_out_ref, out_ref, est_ref, minus_ref, plus_ref, window_ref, spread_ref, *, lat_count
):
    for row in range(-6, 22):
        value = field_ref[row + 6]
        est_ref[:, at(row)] = value
        minus_ref[:, at(row)] = lane_roll(value, 1)
        plus_ref[:, at(row)] = lane_roll(value, -1)
    ones = ones_rows()
    for row in range(-5, 21):
        pieces = [source[:, at(row + a)] for a in (-1, 0, 1) for source in (minus_ref, est_ref, plus_ref)]
        window_ref[:, at(row)] = jnp.concatenate(pieces + [ones], axis=0).astype(BF16)
    groups = [(-5, 5), (0, 4), (4, 4), (8, 4), (12, 4), (16, 5)]
    for row, count in groups:
        where = tile(row + FIRST, count)
        value = jnp.dot(w_in_ref[:, 0:80], window_ref[:, where], preferred_element_type=F32)
        value = jnp.maximum(value, 0.0)
        if row < 0 or row >= ROWS:
            flags = [
                jnp.where(row_mask(lat_count, row + k), jnp.ones((1, LANES), F32), 0.0) for k in range(count)
            ]
            value = value * jnp.concatenate(flags, axis=1)
        spread_ref[:, where] = jnp.dot(w_out_ref[...], value.astype(BF16), preferred_element_type=F32)
    for row in range(-4, 20):
        columns = spread_terms(spread_ref, row)
        term = columns[1] + lane_roll(columns[0], 1) + lane_roll(columns[2], -1)
        out_ref[row + 4] = est_ref[:, at(row)] - term


def solve_kernel(
    field_ref,
    sums_ref,
    adjoint_ref,
    first_ref,
    own_far_ref,
    own_near_ref,
    from_far_ref,
    from_near_ref,
    w_in_ref,
    w_out_ref,
    w_gate_ref,
    w_inc_ref,
    est_out_ref,
    cell_out_ref,
    est_ref,
    grad_ref,
    minus_ref,
    plus_ref,
    mask_ref,
    window_ref,
    spread_ref,
    cell_ref,
    hidden_ref,
    hid_minus_ref,
    hid_plus_ref,
    *,
    lat_count,
):
    even_lon = lax.axis_index("lon") % 2 == 0
    lane = lax.broadcasted_iota(jnp.int32, (8, LANES), 1)
    zero = jnp.zeros((8, LANES), F32)
    strips = slice(STRIP * LANES, TILES * LANES)
    strip_width = (TILES - STRIP) * LANES
    strip_lane = lax.broadcasted_iota(jnp.int32, (8, strip_width), 1)

    def within(row):
        return row_mask(lat_count, row)

    def edge_lanes(left_strip, right_strip):
        place = lax.broadcasted_iota(jnp.int32, left_strip.shape, 1)
        return jnp.where(place % 32 == 8, lane_roll(right_strip, -16), left_strip)

    def beside(left_main, right_main, edges, place):
        lanes = lax.broadcasted_iota(jnp.int32, left_main.shape, 1)
        edge = lane_roll(edges, 120 - place)
        return (
            lane_roll(jnp.where(lanes == 127, edge, left_main), 1),
            lane_roll(jnp.where(lanes == 0, edge, right_main), -1),
        )

    est_ref[:, at(-7)] = zero
    est_ref[:, at(22)] = zero
    for row in range(-6, 22):
        est_ref[:, at(row)] = field_ref[row + 6]
    quarter = (lane % 32) // 8
    from_west, from_east, adjoint_strip = [], [], []
    for part in range(TILES - STRIP):
        rows = slice(8 * part, 8 * part + 8)
        own_east = jnp.where(even_lon, own_near_ref[rows, :], own_far_ref[rows, :])
        own_west = jnp.where(even_lon, own_far_ref[rows, :], own_near_ref[rows, :])
        west = jnp.where(even_lon, from_far_ref[rows, :], from_near_ref[rows, :])
        east = jnp.where(even_lon, from_near_ref[rows, :], from_far_ref[rows, :])
        from_west.append(west)
        from_east.append(east)

        def join(first, second, third, fourth):
            return jnp.where(
                quarter < 2, jnp.where(quarter == 0, first, second), jnp.where(quarter == 2, third, fourth)
            )

        est_ref[:, tile(STRIP + part)] = join(west, lane_roll(own_west, 8), lane_roll(own_east, 16), lane_roll(east, 24))
        adjoint_strip.append(join(lane_roll(west, -8), own_west, lane_roll(own_east, 8), lane_roll(east, 16)))
    from_west = jnp.concatenate(from_west, axis=1)
    from_east = jnp.concatenate(from_east, axis=1)
    adjoint_strip = jnp.concatenate(adjoint_strip, axis=1)
    for row in range(-7, 23):
        mask_ref[:, at(row)] = jnp.where(within(row), jnp.ones((8, LANES), F32), 0.0)
    mask_ref[:, strips] = jnp.where(within(strip_lane // 32 - 6), 1.0, 0.0)

    ones = ones_rows()

    def windows(ref, first_row, last_row, with_strips):
        strip = ref[:, strips]
        edges = edge_lanes(strip, strip)
        for row in range(first_row - 1, last_row + 2) if first_row <= last_row else ():
            main = ref[:, at(row)]
            part, place = strip_place(row)
            minus_ref[:, at(row)], plus_ref[:, at(row)] = beside(main, main, edges[:, tile(part)], place)
        for row in range(first_row, last_row + 1):
            pieces = [source[:, at(row + a)] for a in (-1, 0, 1) for source in (minus_ref, ref, plus_ref)]
            window_ref[:, at(row)] = jnp.concatenate(pieces + [ones], axis=0).astype(BF16)
        if with_strips:
            pieces = []
            shifts = (lane_roll(strip, 1), strip, lane_roll(strip, -1))
            for a in (-1, 0, 1):
                pieces += [lane_roll(value, -32 * a) if a else value for value in shifts]
            pieces.append(jnp.concatenate([ones] * (TILES - STRIP), axis=1))
            window_ref[:, strips] = jnp.concatenate(pieces, axis=0).astype(BF16)

    def pieces_of(first_row, last_row):
        runs = [(first_row + FIRST, last_row + 1 + FIRST), (STRIP, TILES)]
        return [tile(t, min(GROUP, end - t)) for start, end in runs for t in range(start, end, GROUP)]

    def gradient(first_row, last_row, low, high):
        windows(est_ref, low, high, True)
        for where in pieces_of(low, high):
            value = jnp.dot(w_in_ref[:, 0:80], window_ref[:, where], preferred_element_type=F32)
            value = jnp.maximum(value, 0.0) * mask_ref[0:1, where]
            spread_ref[:, where] = jnp.dot(w_out_ref[...], value.astype(BF16), preferred_element_type=F32)
        totals = []
        for b in range(3):
            total = None
            for a in range(3):
                k = 8 * (3 * a + b)
                piece = spread_ref[k : k + 8, strips]
                piece = lane_roll(piece, 32 - 32 * a) if a != 1 else piece
                total = piece if total is None else total + piece
            totals.append(total)
        strip = est_ref[:, strips] - (totals[1] + lane_roll(totals[0], 1) + lane_roll(totals[2], -1))
        grad_ref[:, strips] = strip
        edges = edge_lanes(totals[0], totals[2])
        for row in range(first_row, last_row + 1):
            columns = spread_terms(spread_ref, row)
            part, place = strip_place(row)
            from_left, from_right = beside(columns[0], columns[2], edges[:, tile(part)], place)
            grad_ref[:, at(row)] = est_ref[:, at(row)] - (columns[1] + from_left + from_right)
        return strip

    strip = gradient(0, -1, 0, -1)
    for row in range(-4, 20):
        part, place = strip_place(row)
        edges = strip[:, tile(part)]
        total = jnp.where(
            lane < 2,
            lane_roll(edges, -(place + 8)),
            jnp.where(lane >= 126, lane_roll(edges, 126 - (place + 22)), first_ref[row + 4]),
        )
        total = total + adjoint_ref[row + 4]
        grad_ref[:, at(row)] = total if 0 <= row < ROWS else total * mask_ref[:, at(row)]
    grad_ref[:, strips] = (strip + adjoint_strip) * mask_ref[:, strips]
    windows(grad_ref, -3, 18, True)
    for where in pieces_of(-3, 18):
        sums = jnp.dot(w_gate_ref[HID:, 0:80], window_ref[:, where], preferred_element_type=F32)
        gate_in = 0.5 * jnp.tanh(sums[0:HID]) + 0.5
        gate_out = 0.5 * jnp.tanh(sums[HID : 2 * HID]) + 0.5
        cell = gate_in * jnp.tanh(sums[2 * HID : 3 * HID])
        hidden = (gate_out * jnp.tanh(cell) * mask_ref[0:1, where]).astype(BF16)
        cell_ref[:, where] = cell
        hidden_ref[:, where] = hidden
        update = jnp.dot(w_inc_ref[...], hidden, preferred_element_type=F32)
        est_ref[:, where] -= update[0:8]

    hidden_edges = {}
    for row in range(-1, ROWS + 1):
        part, place = strip_place(row)
        if part not in hidden_edges:
            strip = hidden_ref[:, tile(STRIP + part)]
            hidden_edges[part] = edge_lanes(strip, strip)
        main = hidden_ref[:, at(row)]
        hid_minus_ref[:, at(row)], hid_plus_ref[:, at(row)] = beside(main, main, hidden_edges[part], place)
    gradient(-1, 16, -2, 17)
    carried = zero
    for row in range(-2, ROWS + 1):
        now, later = adjoint_terms(base_sums(sums_ref, row), est_ref[:, at(row)], est_ref[:, at(row + 1)])
        if row > -2:
            total = grad_ref[:, at(row)] + carried + now
            grad_ref[:, at(row)] = total if 0 <= row < ROWS else total * mask_ref[:, at(row)]
        carried = later
    here = est_ref[:, strips]
    above = lane_roll(here, -32)

    def edge_term(source, lane_at, inner):
        constant, own, beside, up, up_beside, down_beside = [lane_roll(source, lane_at - k) for k in FACTOR_LANES]
        here_beside = lane_roll(here, inner)
        total = own * here + beside * here_beside + up * above + up_beside * lane_roll(above, inner) - constant
        return total + lane_roll(up * here + down_beside * here_beside, 32)

    extra_w = edge_term(from_west, 7, 1)
    extra_e = edge_term(from_east, 24 - 2, -1)
    grad_ref[:, strips] = (
        grad_ref[:, strips] + jnp.where(strip_lane % 32 < 16, extra_w, extra_e)
    ) * mask_ref[:, strips]
    windows(grad_ref, 0, ROWS - 1, False)
    for row in range(0, ROWS, 2):
        pieces = [window_ref[:, tile(row + FIRST, 2)]]
        for a in (-1, 0, 1):
            for source in (hid_minus_ref, hidden_ref, hid_plus_ref):
                pieces.append(source[:, tile(row + a + FIRST, 2)])
        sums = jnp.dot(w_gate_ref[:, 0:656], jnp.concatenate(pieces, axis=0), preferred_element_type=F32)
        old = cell_ref[:, tile(row + FIRST, 2)]
        forget = 0.5 * jnp.tanh(sums[0:HID]) + 0.5
        gate_in = 0.5 * jnp.tanh(sums[HID : 2 * HID]) + 0.5
        gate_out = 0.5 * jnp.tanh(sums[2 * HID : 3 * HID]) + 0.5
        cell = forget * old + gate_in * jnp.tanh(sums[3 * HID :])
        hidden = gate_out * jnp.tanh(cell)
        update = jnp.dot(w_inc_ref[...], hidden.astype(BF16), preferred_element_type=F32)
        for k in range(2):
            cell_out_ref[pl.ds(row + k, HID, stride=ROWS), :] = cell[:, tile(k)]
            final = est_ref[:, at(row + k)] - update[0:8, tile(k)]
            est_out_ref[pl.ds(row + k, DAYS, stride=ROWS), :] = final[0:DAYS]


def swap(value, axis, first, count, periodic):
    last = count if periodic else count - 1
    pairs = [(i, (i + 1) % count) for i in range(first, last, 2)]
    return lax.ppermute(value, axis, pairs + [(target, source) for source, target in pairs])


def on_device(
    state,
    prior_in,
    prior_bias,
    prior_out,
    lstm_weight,
    lstm_bias,
    lstm_out,
    obs_value,
    obs_weight,
    obs_tile,
    obs_time,
    obs_row,
    obs_col,
):
    lat_count = lax.axis_size("lat")
    lon_count = lax.axis_size("lon")
    mid = state.reshape(DAYS * ROWS, LANES)

    vmem = pl.BlockSpec(memory_space=pltpu.VMEM)
    track, lat_near, lat_far = pl.pallas_call(
        track_kernel,
        out_shape=(
            jax.ShapeDtypeStruct((lat_count * 8, SENT), BF16),
            jax.ShapeDtypeStruct((DAYS * HALO, LANES), F32),
            jax.ShapeDtypeStruct((DAYS * HALO, LANES), F32),
        ),
        in_specs=[vmem] * 7,
        out_specs=(vmem, vmem, vmem),
        cost_estimate=pl.CostEstimate(flops=100_000, bytes_accessed=150_000, transcendentals=0),
        name="track",
    )(
        obs_value.reshape(1, TRACK),
        obs_weight,
        obs_tile.reshape(1, TRACK),
        obs_time.reshape(1, TRACK),
        obs_row.reshape(1, TRACK),
        obs_col.reshape(1, TRACK),
        mid,
    )
    gathered = lax.all_to_all(
        track.reshape(lat_count, 8, SENT), "lat", split_axis=0, concat_axis=0, tiled=True
    ).reshape(lat_count * 8, SENT)
    far = swap(lat_far, "lat", 1, lat_count, False)
    near = swap(lat_near, "lat", 0, lat_count, False)
    w_gate, w_in, w_out, w_inc = pl.pallas_call(
        prepare_kernel,
        out_shape=(
            jax.ShapeDtypeStruct((4 * HID, 768), BF16),
            jax.ShapeDtypeStruct((HID, LANES), BF16),
            jax.ShapeDtypeStruct((80, HID), BF16),
            jax.ShapeDtypeStruct((16, HID), BF16),
        ),
        in_specs=[vmem] * 6,
        out_specs=(vmem,) * 4,
        compiler_params=pltpu.CompilerParams(vmem_limit_bytes=16 * 1024 * 1024),
        cost_estimate=pl.CostEstimate(flops=2_000_000, bytes_accessed=1_500_000, transcendentals=0),
        name="prepare",
    )(
        jnp.transpose(lstm_weight, (0, 2, 1)),
        lstm_bias.reshape(1, 4 * HID),
        jnp.transpose(prior_in, (0, 2, 1)),
        prior_bias.reshape(1, HID),
        prior_out,
        lstm_out,
    )
    sums = pl.pallas_call(
        sums_kernel,
        out_shape=jax.ShapeDtypeStruct((8, 256, LANES), F32),
        in_specs=[vmem],
        out_specs=vmem,
        scratch_shapes=[
            pltpu.VMEM((2, 512, CHUNK), BF16),
            pltpu.VMEM((2, 640, CHUNK), BF16),
        ],
        compiler_params=pltpu.CompilerParams(vmem_limit_bytes=32 * 1024 * 1024),
        cost_estimate=pl.CostEstimate(flops=4_000_000_000, bytes_accessed=1_500_000, transcendentals=0),
        name="sums",
    )(gathered)
    adjoint, to_far, to_near, field = pl.pallas_call(
        edges_kernel,
        out_shape=(
            jax.ShapeDtypeStruct((24, 8, LANES), F32),
            jax.ShapeDtypeStruct((56, LANES), F32),
            jax.ShapeDtypeStruct((56, LANES), F32),
            jax.ShapeDtypeStruct((28, 8, LANES), F32),
        ),
        in_specs=[vmem] * 4,
        out_specs=(vmem, vmem, vmem, vmem),
        compiler_params=pltpu.CompilerParams(vmem_limit_bytes=16 * 1024 * 1024),
        cost_estimate=pl.CostEstimate(flops=1_000_000, bytes_accessed=1_500_000, transcendentals=0),
        name="edges",
    )(mid, near, far, sums)

    width = TILES * LANES
    main_width = STRIP * LANES

    def first(*refs):
        first_kernel(*refs, lat_count=lat_count)

    started = pl.pallas_call(
        first,
        out_shape=jax.ShapeDtypeStruct((24, 8, LANES), F32),
        in_specs=[vmem] * 3,
        out_specs=vmem,
        scratch_shapes=[
            pltpu.VMEM((8, main_width), F32),
            pltpu.VMEM((8, main_width), F32),
            pltpu.VMEM((8, main_width), F32),
            pltpu.VMEM((80, main_width), BF16),
            pltpu.VMEM((80, main_width), F32),
        ],
        compiler_params=pltpu.CompilerParams(vmem_limit_bytes=16 * 1024 * 1024),
        cost_estimate=pl.CostEstimate(flops=2_000_000_000, bytes_accessed=500_000, transcendentals=0),
        name="first",
    )(field, w_in, w_out)
    from_far = swap(to_far, "lon", 1, lon_count, True)
    from_near = swap(to_near, "lon", 0, lon_count, True)

    def solve(*refs):
        solve_kernel(*refs, lat_count=lat_count)

    estimate, cell_state = pl.pallas_call(
        solve,
        out_shape=(
            jax.ShapeDtypeStruct((DAYS * ROWS, LANES), F32),
            jax.ShapeDtypeStruct((HID * ROWS, LANES), F32),
        ),
        in_specs=[vmem] * 12,
        out_specs=(vmem, vmem),
        scratch_shapes=[
            pltpu.VMEM((8, width), F32),
            pltpu.VMEM((8, width), F32),
            pltpu.VMEM((8, width), F32),
            pltpu.VMEM((8, width), F32),
            pltpu.VMEM((8, width), F32),
            pltpu.VMEM((80, width), BF16),
            pltpu.VMEM((80, width), F32),
            pltpu.VMEM((HID, width), F32),
            pltpu.VMEM((HID, width), BF16),
            pltpu.VMEM((HID, width), BF16),
            pltpu.VMEM((HID, width), BF16),
        ],
        compiler_params=pltpu.CompilerParams(vmem_limit_bytes=32 * 1024 * 1024),
        name="solve",
    )(field, sums, adjoint, started, to_far, to_near, from_far, from_near, w_in, w_out, w_gate, w_inc)
    return (
        estimate.reshape(DAYS, ROWS, LANES),
        cell_state.reshape(HID, ROWS, LANES),
    )


def solution(mesh):
    return jax.shard_map(
        on_device,
        mesh=mesh,
        in_specs=(
            P(None, "lat", "lon"),
            P(),
            P(),
            P(),
            P(),
            P(),
            P(),
            P(("lon", "lat")),
            P(None, ("lon", "lat")),
            P(("lon", "lat"), None),
            P(("lon", "lat")),
            P(("lon", "lat")),
            P(("lon", "lat")),
        ),
        out_specs=(P(None, "lat", "lon"), P(None, "lat", "lon")),
        check_vma=False,
    )
```
